32 devices in a mesh: cuts: 8 (over y, x, core), fsdp: 4 (over z).
Axes of the slice: x: 2, y: 2, z: 4, core: 2. Of those that a mesh axis runs over, the one named last changes fastest.
Arguments:
- source_ids: int32 [64, 512], P(('cuts', 'fsdp')), may hold values from 0 to 32127
- targets: int32 [64, 128], P(('cuts', 'fsdp')), may hold values from 0 to 32127
- source_lengths: int32 [64], P(('cuts', 'fsdp')), may hold values from 1 to 512, as said below
- target_lengths: int32 [64], P(('cuts', 'fsdp')), may hold values from 1 to 128, as said below
- task_ids: int32 [8], replicated, may hold values from 0 to 7
- task_counts: int32 [8], replicated, may hold values from 1 to 999
- blocks: float32 [768, 28, 768], P('cuts', None, 'fsdp'), may hold values from -0.57735027 to 0.57735027
- blocks_momentum: float32 [768, 28, 768], P('cuts', None, 'fsdp'), may hold values from -1.335144e-05 to 1.335144e-05
- embedding: float32 [32128, 768], P('fsdp', 'cuts'), may hold values from -12 to 12
- embed_momentum: float32 [32128, 768], P('fsdp', 'cuts'), may hold values from -2.9802322e-07 to 2.9802322e-07
- gain_rows: float32 [7, 768], replicated, may hold values from 0.4 to 2.4
- gain_momentum: float32 [7, 768], replicated, may hold values from -5.340576e-05 to 5.340576e-05
- position_bias: float32 [2, 32, 12], replicated, may hold values from -4 to 4
- bias_momentum: float32 [2, 32, 12], replicated, may hold values from -5.340576e-05 to 5.340576e-05
- right_blocks: float32 [28, 768, 8], P(None, 'fsdp'), may hold values from -6 to 6
- right_embed: float32 [32128, 8], P('fsdp'), may hold values from -6 to 6
- error_blocks: float32 [8, 768, 28, 768], P('cuts', None, None, 'fsdp'), may hold values from -0.0012207031 to 0.0012207031
- error_embed: float32 [8, 32128, 768], P('cuts', 'fsdp'), may hold values from -0.0012207031 to 0.0012207031
Outputs:
- loss_total: float32 [], replicated
- loss_count: float32 [], replicated
- grad_norm: float32 [], replicated
- blocks_new: float32 [768, 28, 768], P('cuts', None, 'fsdp')
- momentum_blocks: float32 [768, 28, 768], P('cuts', None, 'fsdp')
- embedding_new: float32 [32128, 768], P('fsdp', 'cuts')
- momentum_embed: float32 [32128, 768], P('fsdp', 'cuts')
- gains_new: float32 [7, 768], replicated
- momentum_gains: float32 [7, 768], replicated
- bias_new: float32 [2, 32, 12], replicated
- momentum_bias: float32 [2, 32, 12], replicated
- factors_blocks: float32 [28, 768, 8], P(None, 'fsdp')
- factors_embed: float32 [32128, 8], P('fsdp')
- errors_blocks: float32 [8, 768, 28, 768], P('cuts', None, None, 'fsdp')
- errors_embed: float32 [8, 32128, 768], P('cuts', 'fsdp')
The draws below stay inside these ranges and needn't reach their ends.
Inputs may be any that keep to these rules, and one draw needn't show every extreme that they name: `source_lengths`: one sequence has all 512 positions real in every draw. `target_lengths`: one sequence has all 128 positions real in every draw.
All inputs are finite; a program needn't handle non-finite values.
Results may differ from the reference program's by a relative error of at most 0.024.
The reference program's roundings to bfloat16 on the way count: a program that leaves them out, or rounds other values in their place, can miss the bound.
Values may be sent and summed in bfloat16 or wider, within the bound.
No kernel may reach another device: no remote copies, remote signals or barrier semaphores. Data moves between devices by JAX's collectives and lax.ppermute only.
A program may use at most 384 MiB of HBM per device.

```python
import math
import jax
import jax.numpy as jnp
import numpy as np
from jax import lax

MODEL_WIDTH = 768
H = 12
DH = 64
FEED_UNITS = 3072
VOCAB = 32128
NBK = 32
NB = 28
R = 8
GAINS = 7
TASKS = 8
SEQ_DEV = 2
SL = 512
TL = 128
SEQS = 64
PARAMS = 41189376
N_CUTS = 8
N_FSDP = 4


def ragged(key, longest):
    number = SEQ_DEV * N_CUTS * N_FSDP
    subkeys = jax.random.split(key, 4)
    shorter = jax.random.randint(subkeys[0], (number,), 1, longest * 3 // 16 + 1)
    taller = jax.random.randint(subkeys[1], (number,), longest * 3 // 16, longest + 1)
    choose = jax.random.randint(subkeys[2], (number,), 0, 8)
    rawest = jnp.where(choose == 0, taller, shorter)
    device = jnp.arange(number, dtype=jnp.int32) // SEQ_DEV
    slice_index = device // N_FSDP
    member = device % N_FSDP
    ramp_up = (N_FSDP - 1 + 2 * member) * (N_CUTS - 1 + 2 * slice_index)
    scaled = jnp.maximum(1, rawest * ramp_up // (9 * (N_FSDP - 1) * (N_CUTS - 1)))
    forced = jax.random.randint(subkeys[3], (), 0, number)
    return jnp.where(jnp.arange(number, dtype=jnp.int32) == forced, longest, scaled).astype(jnp.int32)


def draw_source_lengths(key, part):
    key = jax.random.fold_in(key, 11)
    return ragged(key, SL)


def draw_target_lengths(key, part):
    key = jax.random.fold_in(key, 12)
    return ragged(key, TL)


def draw_blocks(key, part):
    key = jax.random.fold_in(key, 13)
    noise = jnp.clip(jax.random.normal(key, (MODEL_WIDTH, NB, MODEL_WIDTH), jnp.float32), -4.0, 4.0)
    query_scale = DH ** (-0.5)
    first_block = [query_scale, 1.0, 1.0, 4.0] + [1.0] * 4 + [0.5] * 4
    second_block = [query_scale, 1.0, 1.0, 4.0] * 2 + [1.0] * 4 + [0.5] * 4
    scales = jnp.array(first_block + second_block, jnp.float32) * MODEL_WIDTH ** (-0.5)
    return noise * scales[None, :, None]


def draw_embedding(key, part):
    key = jax.random.fold_in(key, 14)
    rising = jnp.arange(VOCAB, dtype=jnp.float32) / (VOCAB - 1)
    noise = jnp.clip(jax.random.normal(key, (VOCAB, MODEL_WIDTH), jnp.float32), -4.0, 4.0)
    spread = 1.0 + 2.0 * rising
    return noise * spread[:, None]


def draw_gain_rows(key, part):
    key = jax.random.fold_in(key, 15)
    rising = 0.6 + 1.2 * jnp.arange(MODEL_WIDTH, dtype=jnp.float32) / (MODEL_WIDTH - 1)
    noise = jnp.clip(jax.random.normal(key, (GAINS, MODEL_WIDTH), jnp.float32), -3.0, 3.0)
    return rising[None, :] * (1.0 + 0.1 * noise)


def plant(values, own_key, low, largest):
    shape = values.shape
    index_at = [jax.random.randint(jax.random.fold_in(own_key, axis), (), 0, shape[axis]) for axis in range(len(shape))]
    values = values.at[tuple(index_at)].set(low)
    longest = shape.index(max(shape))
    index_at[longest] = (index_at[longest] + 1) % shape[longest]
    return values.at[tuple(index_at)].set(largest)


def block_levels(own_key, dims, pieces, low, top_value):
    gain = 1.0
    for dim, shards_of in pieces:
        heights = jax.random.uniform(jax.random.fold_in(jax.random.fold_in(own_key, 6), dim), (shards_of,), jnp.float32, low / len(pieces), top_value / len(pieces))
        gain = gain * jnp.repeat(jnp.exp(heights), dims[dim] // shards_of).reshape((-1,) + (1,) * (len(dims) - 1 - dim))
    return gain


def cumulative_ranks(number_of, skew):
    loads = [(1 << 20) // math.isqrt(standing ** skew) + 1 for standing in range(1, number_of + 1)]
    scale = 1 + sum(loads) // (1 << 30)
    return np.cumsum(np.array([max(1, weight // scale) for weight in loads]))


def ranked(rng, shape, number_of, lean):
    table = cumulative_ranks(number_of, lean)
    pick = jax.random.randint(jax.random.fold_in(rng, 1), shape, 0, int(table[number_of - 1]))
    grade = jnp.searchsorted(jnp.asarray(table, jnp.int32), pick, side="right")
    return jax.random.permutation(jax.random.fold_in(rng, 2), number_of)[grade].astype(jnp.int32)


def normal_values(stream_key, extent, scale, reach, cuts=(), kind=jnp.bfloat16):
    loudness = block_levels(stream_key, extent, cuts, -0.22, 0.18) if cuts else 1.0
    result = jax.random.normal(stream_key, extent, jnp.float32) * scale * loudness
    return jnp.minimum(jnp.maximum(result, -reach), reach).astype(kind)


def setup_inputs(seed: int = 0) -> dict:
    key_list = jax.random.split(jax.random.key(seed), 19)
    return {
        "source_ids": plant(ranked(key_list[0], (SEQS, SL), VOCAB, 2), jax.random.fold_in(key_list[0], 3), 0, VOCAB - 1).astype(jnp.int32),
        "targets": plant(ranked(key_list[1], (SEQS, TL), VOCAB, 2), jax.random.fold_in(key_list[1], 3), 0, VOCAB - 1).astype(jnp.int32),
        "source_lengths": draw_source_lengths(jax.random.fold_in(key_list[18], 71), 0),
        "target_lengths": draw_target_lengths(jax.random.fold_in(key_list[18], 71), 0),
        "task_ids": plant(jax.random.randint(key_list[4], (N_CUTS,), 0, TASKS), jax.random.fold_in(key_list[4], 1), 0, TASKS - 1).astype(jnp.int32),
        "task_counts": plant(jax.random.randint(key_list[5], (TASKS,), 1, 1000), jax.random.fold_in(key_list[5], 1), 1, 999).astype(jnp.int32),
        "blocks": draw_blocks(jax.random.fold_in(key_list[18], 71), 0),
        "blocks_momentum": normal_values(key_list[7], (MODEL_WIDTH, NB, MODEL_WIDTH), (0.0056 / PARAMS ** 0.5), 1.33514404296875e-05, ((0, 8), (2, 4)), jnp.float32),
        "embedding": draw_embedding(jax.random.fold_in(key_list[18], 71), 0),
        "embed_momentum": normal_values(key_list[9], (VOCAB, MODEL_WIDTH), (0.00014 / PARAMS ** 0.5), 2.980232238769531e-07, ((0, 4), (1, 8)), jnp.float32),
        "gain_rows": draw_gain_rows(jax.random.fold_in(key_list[18], 71), 0),
        "gain_momentum": normal_values(key_list[11], (GAINS, MODEL_WIDTH), (0.022 / PARAMS ** 0.5), 5.340576171875e-05, (), jnp.float32),
        "position_bias": normal_values(key_list[12], (2, NBK, H), 0.5, 4.0, (), jnp.float32),
        "bias_momentum": normal_values(key_list[13], (2, NBK, H), (0.022 / PARAMS ** 0.5), 5.340576171875e-05, (), jnp.float32),
        "right_blocks": normal_values(key_list[14], (NB, MODEL_WIDTH, R), 1.0, 6.0, ((1, 4),), jnp.float32),
        "right_embed": normal_values(key_list[15], (VOCAB, R), 1.0, 6.0, ((0, 4),), jnp.float32),
        "error_blocks": normal_values(key_list[16], (N_CUTS, MODEL_WIDTH, NB, MODEL_WIDTH), (0.5 / PARAMS ** 0.5), 0.0012207031, ((0, 8), (3, 4)), jnp.float32),
        "error_embed": normal_values(key_list[17], (N_CUTS, VOCAB, MODEL_WIDTH), (0.5 / PARAMS ** 0.5), 0.0012207031, ((0, 8), (1, 4)), jnp.float32),
    }


EPSILON = 1e-06
MASKED = -1000000000.0
CLIP_NORM = 0.05
MOMENTUM_DECAY = 0.9
STEP_RATE = 5.0
EMBED_SHARE = 50.0
SMALL_SHARE = 1.0 / 7.0
TOP_PRECISION = lax.Precision.HIGHEST
ENCODER_EDGES = (12, 16, 23, 32, 46, 64, 91)
DECODER_EDGES = (19, 21, 24, 27, 31, 35, 40, 46, 52, 59, 67, 77, 87, 99, 113)

@jax.custom_vjp
def low(v):
    return lax.optimization_barrier(v.astype(jnp.bfloat16)).astype(jnp.float32)

@jax.custom_vjp
def low_back(v):
    return v

def low_keep(v):
    return (low(v), None)

def low_pass(kept, grad):
    return (grad,)

def back_keep(v):
    return (v, None)

def back_low(kept, grad):
    return (low(grad),)
low.defvjp(low_keep, low_pass)
low_back.defvjp(back_keep, back_low)

def rounded_both(value):
    return low_back(low(value))

def root_norm(stream, gain_row):
    return stream * lax.rsqrt(lax.optimization_barrier(jnp.mean(stream * stream, axis=-1, keepdims=True)) + EPSILON) * gain_row

def bucket_table(length, causal):
    places = jnp.arange(length, dtype=jnp.int32)
    offset = places[None, :] - places[:, None]
    if causal:
        distance = jnp.maximum(-offset, 0)
        farther = 16 + sum(((distance >= boundary).astype(jnp.int32) for boundary in DECODER_EDGES))
        bucket = jnp.where(distance < 16, distance, farther)
    else:
        distance = jnp.abs(offset)
        farther = 8 + sum(((distance >= boundary).astype(jnp.int32) for boundary in ENCODER_EDGES))
        bucket = jnp.where(distance < 8, distance, farther) + jnp.where(offset > 0, 16, 0)
    return (bucket[:, :, None] == jnp.arange(NBK, dtype=jnp.int32)[None, None, :]).astype(jnp.float32)

def orthonormal(factor):
    gram_matrix = jnp.einsum('...nr,...ns->...rs', factor, factor, precision=TOP_PRECISION)
    cholesky_factor = jnp.linalg.cholesky(gram_matrix)
    return lax.linalg.triangular_solve(cholesky_factor, factor, left_side=False, lower=True, transpose_a=True)

def project(activation_output, weight_matrix):
    return jnp.einsum('wio,ob->wib', activation_output, weight_matrix, precision=TOP_PRECISION)

def attend(queries, key_rows, value_rows, keep_mask, bias_table):
    scores = jnp.einsum('qhd,khd->hqk', queries, key_rows, precision=TOP_PRECISION) + bias_table
    scores = low_back(jnp.where(keep_mask[None], scores, MASKED))
    weights = jax.nn.softmax(scores, axis=-1)
    return jnp.einsum('hqk,khd->qhd', low(weights), value_rows, precision=TOP_PRECISION)

def attention(stream, gain_row, source, matrices, keep_mask, bias_table):
    norm_output = low(root_norm(stream, gain_row))
    context = norm_output if source is None else source
    batch_size, row_count = (stream.shape[0], stream.shape[1])
    queries = rounded_both(project(norm_output, matrices[:, 0])).reshape(batch_size, row_count, H, DH)
    key_rows = rounded_both(project(context, matrices[:, 1])).reshape(batch_size, -1, H, DH)
    value_rows = rounded_both(project(context, matrices[:, 2])).reshape(batch_size, -1, H, DH)
    one_sequence = jax.checkpoint(lambda members: attend(members[0], members[1], members[2], members[3], bias_table))
    attended = lax.map(one_sequence, (queries, key_rows, value_rows, keep_mask))
    attended = rounded_both(attended.reshape(batch_size, row_count, MODEL_WIDTH))
    return stream + low_back(project(attended, matrices[:, 3]))

def feed_forward(stream, gain_row, nested_layer_blocks, outer_blocks):
    norm_output = low(root_norm(stream, gain_row))
    prior_input = low_back(jnp.einsum('cxp,pi->cxi', norm_output, nested_layer_blocks.reshape(MODEL_WIDTH, FEED_UNITS), precision=TOP_PRECISION))
    hidden = low(jax.nn.gelu(prior_input)).reshape(stream.shape[0], stream.shape[1], 4, MODEL_WIDTH)
    return stream + low_back(jnp.einsum('sljd,dje->sle', hidden, outer_blocks, precision=TOP_PRECISION))

def slice_loss(parameters, token_ids, target_ids, source_len, target_len, slice_weight, total_count):
    blocks, embedding, gain_rows, position_bias = parameters
    weights_low = low(blocks)
    embed_low = low(embedding)
    batch_size = token_ids.shape[0]
    source_places = jnp.arange(SL, dtype=jnp.int32)
    target_places = jnp.arange(TL, dtype=jnp.int32)
    source_ok = source_places[None, :] < source_len[:, None]
    target_ok = target_places[None, :] < target_len[:, None]
    keep_source = jnp.broadcast_to(source_ok[:, None, :], (batch_size, SL, SL))
    keep_target = target_ok[:, None, :] & (target_places[None, None, :] <= target_places[None, :, None])
    keep_cross = jnp.broadcast_to(source_ok[:, None, :], (batch_size, TL, SL))
    bias_source = jnp.einsum('ijb,bh->hij', bucket_table(SL, False), position_bias[0], precision=TOP_PRECISION)
    bias_target = jnp.einsum('ijb,bh->hij', bucket_table(TL, True), position_bias[1], precision=TOP_PRECISION)
    inputs = jnp.concatenate([jnp.zeros((batch_size, 1), jnp.int32), target_ids[:, :-1]], axis=1)
    stream = embed_low[token_ids]
    stream = attention(stream, gain_rows[0], None, weights_low[:, 0:4], keep_source, bias_source)
    stream = feed_forward(stream, gain_rows[1], weights_low[:, 4:8], weights_low[:, 8:12])
    encoded = low(root_norm(stream, gain_rows[2]))
    stream = embed_low[inputs]
    stream = attention(stream, gain_rows[3], None, weights_low[:, 12:16], keep_target, bias_target)
    stream = attention(stream, gain_rows[4], encoded, weights_low[:, 16:20], keep_cross, 0.0)
    stream = feed_forward(stream, gain_rows[5], weights_low[:, 20:24], weights_low[:, 24:28])
    final_rows = low(root_norm(stream, gain_rows[6]) * MODEL_WIDTH ** (-0.5)).reshape(-1, MODEL_WIDTH)
    block_rows = math.gcd(512, final_rows.shape[0])

    def block_loss(members):
        logits = low_back(jnp.einsum('rd,vd->rv', members[0], embed_low, precision=TOP_PRECISION))
        picked = lax.optimization_barrier(jnp.sum(jnp.where(jnp.arange(VOCAB, dtype=jnp.int32)[None, :] == members[1][:, None], logits, 0.0), axis=1))
        return jax.nn.logsumexp(logits, axis=1) - picked
    losses = lax.map(jax.checkpoint(block_loss), (final_rows.reshape(-1, block_rows, MODEL_WIDTH), target_ids.reshape(-1, block_rows)))
    ce_total = jnp.sum(losses.reshape(-1) * target_ok.reshape(-1).astype(jnp.float32))
    return (ce_total * slice_weight / total_count, ce_total * slice_weight)

def reference(source_ids, targets, source_lengths, target_lengths, task_ids, task_counts, blocks, blocks_momentum, embedding, embed_momentum, gain_rows, gain_momentum, position_bias, bias_momentum, right_blocks, right_embed, error_blocks, error_embed):
    per_slice = N_FSDP * SEQ_DEV
    total_count = jnp.sum(target_lengths).astype(jnp.float32)
    chosen = lax.optimization_barrier(jnp.sum(jnp.where(task_ids[:, None] == jnp.arange(TASKS, dtype=jnp.int32)[None, :], task_counts[None, :], 0), axis=1)).astype(jnp.float32)
    slice_weights = N_CUTS * chosen / jnp.sum(chosen)

    def grouped(array):
        return array.reshape((N_CUTS, per_slice) + array.shape[1:])
    parameters = (blocks, embedding, gain_rows, position_bias)

    def one_slice(carry, members):

        def loss_of(*values):
            return slice_loss(values, members[0], members[1], members[2], members[3], members[4], total_count)
        _, pull_back, loss_part = jax.vjp(loss_of, *parameters, has_aux=True)
        return (carry, (loss_part, pull_back(jnp.ones((), jnp.float32))))
    _, (loss_parts, gradients) = lax.scan(one_slice, jnp.zeros((), jnp.float32), (grouped(source_ids), grouped(targets), grouped(source_lengths), grouped(target_lengths), slice_weights))
    left_blocks = error_blocks + gradients[0]
    left_embed = error_embed + gradients[1]
    left_factor = orthonormal(jnp.einsum('cikj,kjr->kir', left_blocks, right_blocks, precision=TOP_PRECISION))
    embed_factor = orthonormal(jnp.einsum('cvd,vr->dr', left_embed, right_embed, precision=TOP_PRECISION))
    factors_blocks = jnp.einsum('cikj,kir->kjr', left_blocks, left_factor, precision=TOP_PRECISION)
    factors_embed = jnp.einsum('cvd,dr->vr', left_embed, embed_factor, precision=TOP_PRECISION)
    full_blocks = jnp.einsum('kir,kjr->ikj', left_factor, factors_blocks, precision=TOP_PRECISION)
    full_embed = jnp.einsum('vr,dr->vd', factors_embed, embed_factor, precision=TOP_PRECISION)
    gain_grad = lax.optimization_barrier(jnp.sum(gradients[2], axis=0))
    bias_grad = lax.optimization_barrier(jnp.sum(gradients[3], axis=0))
    grad_norm = jnp.sqrt(jnp.sum(full_blocks * full_blocks) + jnp.sum(full_embed * full_embed) + jnp.sum(gain_grad * gain_grad) + jnp.sum(bias_grad * bias_grad))
    clip_factor = jnp.minimum(1.0, CLIP_NORM / grad_norm)
    step_size = STEP_RATE * math.sqrt(PARAMS / MODEL_WIDTH) / CLIP_NORM
    embed_step = step_size * EMBED_SHARE * math.sqrt(MODEL_WIDTH)
    small_step = step_size * SMALL_SHARE * math.sqrt(MODEL_WIDTH)
    momentum_blocks = MOMENTUM_DECAY * blocks_momentum + (1.0 - MOMENTUM_DECAY) * (clip_factor * full_blocks)
    momentum_embed = MOMENTUM_DECAY * embed_momentum + (1.0 - MOMENTUM_DECAY) * (clip_factor * full_embed)
    momentum_gains = MOMENTUM_DECAY * gain_momentum + (1.0 - MOMENTUM_DECAY) * (clip_factor * gain_grad)
    momentum_bias = MOMENTUM_DECAY * bias_momentum + (1.0 - MOMENTUM_DECAY) * (clip_factor * bias_grad)
    return (jnp.sum(loss_parts), total_count, grad_norm, blocks - step_size * momentum_blocks, momentum_blocks, embedding - embed_step * momentum_embed, momentum_embed, gain_rows - small_step * momentum_gains, momentum_gains, position_bias - small_step * momentum_bias, momentum_bias, factors_blocks, factors_embed, left_blocks - full_blocks[None], left_embed - full_embed[None])
```

```python
import math

import jax
import jax.numpy as jnp
from jax import lax
from jax.experimental import pallas as pl
from jax.experimental.pallas import tpu as pltpu
from jax.sharding import PartitionSpec as P

MODEL_WIDTH = 768
H = 12
DH = 64
FEED_UNITS = 3072
NBK = 32
TASKS = 8
PARAMS = 41189376


EPSILON = 1e-06
MASKED = -1000000000.0
CLIP_NORM = 0.05
MOMENTUM_DECAY = 0.9
STEP_RATE = 5.0
EMBED_SHARE = 50.0
SMALL_SHARE = 1.0 / 7.0
TOP_PRECISION = lax.Precision.HIGHEST
TILE = 128
ROOM_SOURCE = 1280
ROOM_TARGET = 384
ENCODER_EDGES = (12, 16, 23, 32, 46, 64, 91)
DECODER_EDGES = (19, 21, 24, 27, 31, 35, 40, 46, 52, 59, 67, 77, 87, 99, 113)


def root_norm(stream, gain_row):
    return (
        stream * lax.rsqrt(jnp.mean(stream * stream, axis=-1, keepdims=True) + EPSILON) * gain_row
    )


def norm_backward(stream, gain_row, grad_normed):
    _, pull_back = jax.vjp(root_norm, stream, gain_row)
    return pull_back(grad_normed)


def dot(left, right):
    return jnp.dot(left, right, preferred_element_type=jnp.float32)


def dot_nt(left, right):
    return lax.dot_general(left, right, (((1,), (1,)), ((), ())), preferred_element_type=jnp.float32)


def dot_tn(left, right):
    return lax.dot_general(left, right, (((0,), (0,)), ((), ())), preferred_element_type=jnp.float32)


def gather_cuts(part, cuts_rank, cuts_count):
    number, rows, columns = part.shape
    ways = [1 << bit for bit in range(1, cuts_count.bit_length() - 1)]
    if cuts_count & (cuts_count - 1) or number % max(len(ways), 1):
        return lax.all_gather(part, "cuts", axis=1, tiled=True)

    def swap(array, mask):
        return lax.ppermute(array, "cuts", [(i, i ^ mask) for i in range(cuts_count)])

    share = number // max(len(ways), 1)
    joined = []
    for turn in range(max(len(ways), 1)):
        held = [(0, part[turn * share : (turn + 1) * share])]
        for mask in ways[turn:] + ways[:turn] + [1]:
            held = held + [(place ^ mask, swap(array, mask)) for place, array in held]
        whole = jnp.zeros((share, cuts_count, rows, columns), part.dtype)
        for place, array in held:
            whole = lax.dynamic_update_slice(
                whole, array[:, None], (0, jnp.bitwise_xor(cuts_rank, place), 0, 0)
            )
        joined.append(whole.reshape(share, cuts_count * rows, columns))
    return jnp.concatenate(joined, axis=0) if len(joined) > 1 else joined[0]


def offset_buckets(causal):
    places = jnp.arange(TILE, dtype=jnp.int32)
    offset = (
        (jnp.arange(5, dtype=jnp.int32)[:, None, None] - 2) * TILE
        + places[None, :, None]
        - places[None, None, :]
    )
    if causal:
        distance = jnp.maximum(-offset, 0)
        farther = 16 + sum(((distance >= boundary).astype(jnp.int32) for boundary in DECODER_EDGES))
        bucket = jnp.where(distance < 16, distance, farther)
    else:
        distance = jnp.abs(offset)
        farther = 8 + sum(((distance >= boundary).astype(jnp.int32) for boundary in ENCODER_EDGES))
        bucket = jnp.where(distance < 8, distance, farther) + jnp.where(offset > 0, 16, 0)
    return (bucket[..., None] == jnp.arange(NBK, dtype=jnp.int32)).astype(jnp.float32)


def kept(segment_column, segment_row, key_tile, query_tile, causal):
    keep = segment_column == segment_row
    if causal:
        key_place = key_tile * TILE + lax.broadcasted_iota(jnp.int32, (TILE, TILE), 0)
        query_place = query_tile * TILE + lax.broadcasted_iota(jnp.int32, (TILE, TILE), 1)
        keep = keep & (key_place <= query_place)
    return keep


def lane_half(rows, half):
    return (lax.broadcasted_iota(jnp.int32, (rows, TILE), 1) // DH) == half


def tile_scores(keys, queries, keep, bias):
    scores = dot_nt(keys, queries)
    if bias is not None:
        scores = scores + bias
    return jnp.where(keep, scores, MASKED)


def forward_kernel(
    causal, biased, first_ref, last_ref, q_ref, k_ref, v_ref, row_ref, column_ref, *rest
):
    bias_ref = rest[0] if biased else None
    out_ref, level_ref, top_ref, sum_ref, total_ref = rest[1:] if biased else rest
    here = pl.program_id(0)
    top_ref[...] = jnp.full_like(top_ref, -1e30)
    sum_ref[...] = jnp.zeros_like(sum_ref)
    total_ref[...] = jnp.zeros_like(total_ref)
    segment_row = row_ref[...]

    def step(there, carry):
        rows = pl.ds(pl.multiple_of(there * TILE, TILE), TILE)
        keep = kept(column_ref[rows, :], segment_row, there, here, causal)
        offset = jnp.clip(there - here, -2, 2) + 2
        for pair in range(H // 2):
            lanes = slice(pair * TILE, (pair + 1) * TILE)
            keys = k_ref[rows, lanes]
            values = v_ref[rows, lanes].T
            both = q_ref[:, lanes]
            for half in range(2):
                head = 2 * pair + half
                queries = jnp.where(lane_half(TILE, half), both, jnp.zeros_like(both))
                scores = tile_scores(
                    keys, queries, keep, bias_ref[offset, head] if biased else None
                )
                before = top_ref[head : head + 1, :]
                after = jnp.maximum(before, jnp.max(scores, axis=0, keepdims=True))
                weights = jnp.exp(scores - after)
                scale = jnp.exp(before - after)
                top_ref[head : head + 1, :] = after
                sum_ref[head : head + 1, :] = sum_ref[head : head + 1, :] * scale + jnp.sum(
                    weights, axis=0, keepdims=True
                )
                own = slice(head * DH, (head + 1) * DH)
                total_ref[own, :] = total_ref[own, :] * scale + dot(
                    values[half * DH : (half + 1) * DH], weights.astype(jnp.bfloat16)
                )
        return carry

    lax.fori_loop(first_ref[here], last_ref[here], step, 0)
    seen = sum_ref[...] > 0.0
    divisor = jnp.where(seen, sum_ref[...], 1.0)
    level_ref[...] = jnp.where(seen, top_ref[...] + jnp.log(divisor), 0.0)
    for head in range(H):
        own = slice(head * DH, (head + 1) * DH)
        total_ref[own, :] = total_ref[own, :] / divisor[head : head + 1, :]
    for pair in range(H // 2):
        lanes = slice(pair * TILE, (pair + 1) * TILE)
        out_ref[:, lanes] = total_ref[lanes, :].T.astype(jnp.bfloat16)


def backward_kernel(
    causal, biased, first_ref, last_ref, q_ref, o_ref, k_ref, v_ref, level_ref, row_ref, column_ref, *rest
):
    bias_ref = rest[0] if biased else None
    rest = rest[1:] if biased else rest
    gq_ref, gk_ref, gv_ref = rest[:3]
    gb_ref = rest[3] if biased else None
    weight_ref, slope_ref, mean_ref, tq_ref, tk_ref, tv_ref = rest[-6:]
    here = pl.program_id(0)

    @pl.when(here == 0)
    def _():
        tk_ref[...] = jnp.zeros_like(tk_ref)
        tv_ref[...] = jnp.zeros_like(tv_ref)
        if biased:
            gb_ref[...] = jnp.zeros_like(gb_ref)

    mean_ref[...] = jnp.zeros_like(mean_ref)
    tq_ref[...] = jnp.zeros_like(tq_ref)
    segment_row = row_ref[...]
    first = first_ref[here]
    last = last_ref[here]

    def halves(array):
        return [jnp.where(lane_half(TILE, half), array, jnp.zeros_like(array)) for half in range(2)]

    def look(there, carry):
        rows = pl.ds(pl.multiple_of(there * TILE, TILE), TILE)
        keep = kept(column_ref[rows, :], segment_row, there, here, causal)
        offset = jnp.clip(there - here, -2, 2) + 2
        for pair in range(H // 2):
            lanes = slice(pair * TILE, (pair + 1) * TILE)
            keys = k_ref[rows, lanes]
            values = v_ref[rows, lanes]
            queries = halves(q_ref[:, lanes])
            arriving = halves(o_ref[:, lanes])
            rounded = []
            for half in range(2):
                head = 2 * pair + half
                scores = tile_scores(
                    keys, queries[half], keep, bias_ref[offset, head] if biased else None
                )
                weights = jnp.exp(scores - level_ref[head : head + 1, :])
                slopes = dot_nt(values, arriving[half])
                mean_ref[head : head + 1, :] = mean_ref[head : head + 1, :] + jnp.sum(
                    weights * slopes, axis=0, keepdims=True
                )
                weight_ref[there - first, head] = weights
                slope_ref[there - first, head] = slopes
                rounded.append(weights.astype(jnp.bfloat16))
            tv_ref[rows, lanes] = tv_ref[rows, lanes] + dot(
                jnp.concatenate(rounded, axis=1), jnp.concatenate(arriving, axis=0)
            )
        return carry

    def push(there, carry):
        rows = pl.ds(pl.multiple_of(there * TILE, TILE), TILE)
        offset = jnp.clip(there - here, -2, 2) + 2
        for pair in range(H // 2):
            lanes = slice(pair * TILE, (pair + 1) * TILE)
            keys = k_ref[rows, lanes].T
            queries = halves(q_ref[:, lanes])
            rounded = []
            for half in range(2):
                head = 2 * pair + half
                slopes = (
                    weight_ref[there - first, head]
                    * (slope_ref[there - first, head] - mean_ref[head : head + 1, :])
                ).astype(jnp.bfloat16)
                if biased:
                    gb_ref[offset, head] = gb_ref[offset, head] + slopes.astype(jnp.float32)
                own = slice(head * DH, (head + 1) * DH)
                tq_ref[own, :] = tq_ref[own, :] + dot(keys[half * DH : (half + 1) * DH], slopes)
                rounded.append(slopes)
            tk_ref[rows, lanes] = tk_ref[rows, lanes] + dot(
                jnp.concatenate(rounded, axis=1), jnp.concatenate(queries, axis=0)
            )
        return carry

    lax.fori_loop(first, last, look, 0)
    lax.fori_loop(first, last, push, 0)
    for pair in range(H // 2):
        lanes = slice(pair * TILE, (pair + 1) * TILE)
        gq_ref[:, lanes] = tq_ref[lanes, :].T.astype(jnp.bfloat16)

    @pl.when(here == pl.num_programs(0) - 1)
    def _():
        gk_ref[...] = tk_ref[...].astype(jnp.bfloat16)
        gv_ref[...] = tv_ref[...].astype(jnp.bfloat16)


def whole_block(shape):
    return pl.BlockSpec(shape, lambda i, *_: (0,) * len(shape))


def packed_forward(queries, key_rows, value_rows, span, segment_row, segment_column, causal, bias):
    count, other = queries.shape[0], key_rows.shape[0]
    biased = bias is not None
    tile = pl.BlockSpec((TILE, MODEL_WIDTH), lambda i, *_: (i, 0))
    return pl.pallas_call(
        lambda *refs: forward_kernel(causal, biased, *refs),
        grid_spec=pltpu.PrefetchScalarGridSpec(
            num_scalar_prefetch=2,
            grid=(count // TILE,),
            in_specs=[
                tile,
                whole_block((other, MODEL_WIDTH)),
                whole_block((other, MODEL_WIDTH)),
                pl.BlockSpec((1, TILE), lambda i, *_: (0, i)),
                whole_block((other, 1)),
            ]
            + ([whole_block((5, H, TILE, TILE))] if biased else []),
            out_specs=[tile, pl.BlockSpec((16, TILE), lambda i, *_: (0, i))],
            scratch_shapes=[
                pltpu.VMEM((16, TILE), jnp.float32),
                pltpu.VMEM((16, TILE), jnp.float32),
                pltpu.VMEM((MODEL_WIDTH, TILE), jnp.float32),
            ],
        ),
        out_shape=[
            jax.ShapeDtypeStruct((count, MODEL_WIDTH), jnp.bfloat16),
            jax.ShapeDtypeStruct((16, count), jnp.float32),
        ],
        compiler_params=pltpu.CompilerParams(vmem_limit_bytes=40 << 20),
        name="attend",
    )(*span, queries, key_rows, value_rows, segment_row, segment_column, *([bias] if biased else []))


def packed_backward(
    queries, grad_out, key_rows, value_rows, levels, span, segment_row, segment_column, causal, bias
):
    count, other = queries.shape[0], key_rows.shape[0]
    biased = bias is not None
    reach = min(other // TILE, 9) if biased else other // TILE
    tile = pl.BlockSpec((TILE, MODEL_WIDTH), lambda i, *_: (i, 0))
    table = (5, H, TILE, TILE)
    return pl.pallas_call(
        lambda *refs: backward_kernel(causal, biased, *refs),
        grid_spec=pltpu.PrefetchScalarGridSpec(
            num_scalar_prefetch=2,
            grid=(count // TILE,),
            in_specs=[
                tile,
                tile,
                whole_block((other, MODEL_WIDTH)),
                whole_block((other, MODEL_WIDTH)),
                pl.BlockSpec((16, TILE), lambda i, *_: (0, i)),
                pl.BlockSpec((1, TILE), lambda i, *_: (0, i)),
                whole_block((other, 1)),
            ]
            + ([whole_block(table)] if biased else []),
            out_specs=[tile, whole_block((other, MODEL_WIDTH)), whole_block((other, MODEL_WIDTH))]
            + ([whole_block(table)] if biased else []),
            scratch_shapes=[
                pltpu.VMEM((reach, H, TILE, TILE), jnp.float32),
                pltpu.VMEM((reach, H, TILE, TILE), jnp.float32),
                pltpu.VMEM((16, TILE), jnp.float32),
                pltpu.VMEM((MODEL_WIDTH, TILE), jnp.float32),
                pltpu.VMEM((other, MODEL_WIDTH), jnp.float32),
                pltpu.VMEM((other, MODEL_WIDTH), jnp.float32),
            ],
        ),
        out_shape=[
            jax.ShapeDtypeStruct((count, MODEL_WIDTH), jnp.bfloat16),
            jax.ShapeDtypeStruct((other, MODEL_WIDTH), jnp.bfloat16),
            jax.ShapeDtypeStruct((other, MODEL_WIDTH), jnp.bfloat16),
        ]
        + ([jax.ShapeDtypeStruct(table, jnp.float32)] if biased else []),
        compiler_params=pltpu.CompilerParams(vmem_limit_bytes=58 << 20),
        name="attend_back",
    )(
        *span,
        queries,
        grad_out,
        key_rows,
        value_rows,
        levels,
        segment_row,
        segment_column,
        *([bias] if biased else []),
    )


def lookup_kernel(rows_in, blocks_ref, id_ref, vocab_ref, out_ref, total_ref):
    step = pl.program_id(0)
    width = vocab_ref.shape[1]
    chunk = 2 * TILE

    @pl.when(step == 0)
    def _():
        total_ref[...] = jnp.zeros_like(total_ref)

    inside = step * width + lax.broadcasted_iota(jnp.int32, (1, width), 1) < rows_in
    table = jnp.where(inside, vocab_ref[...], jnp.zeros_like(vocab_ref[...]))
    places = step * width + lax.broadcasted_iota(jnp.int32, (chunk, width), 1)

    def one(index, carry):
        rows = pl.ds(pl.multiple_of(index * chunk, chunk), chunk)
        hot = (id_ref[rows, :] == places).astype(jnp.bfloat16)
        total_ref[rows, :] = total_ref[rows, :] + dot_nt(hot, table)
        return carry

    lax.fori_loop(0, blocks_ref[0], one, 0)
    lax.fori_loop(blocks_ref[1], blocks_ref[2], one, 0)

    @pl.when(step == pl.num_programs(0) - 1)
    def _():
        out_ref[...] = total_ref[...].astype(jnp.bfloat16)


def lookup_rows(local_ids, spans, vocab):
    count, width = local_ids.shape[0], 4 * TILE
    rows_in = vocab.shape[1]
    return pl.pallas_call(
        lambda *refs: lookup_kernel(rows_in, *refs),
        grid_spec=pltpu.PrefetchScalarGridSpec(
            num_scalar_prefetch=1,
            grid=(pl.cdiv(rows_in, width),),
            in_specs=[
                whole_block((count, 1)),
                pl.BlockSpec((MODEL_WIDTH, width), lambda i, *_: (0, i)),
            ],
            out_specs=whole_block((count, MODEL_WIDTH)),
            scratch_shapes=[pltpu.VMEM((count, MODEL_WIDTH), jnp.float32)],
        ),
        out_shape=jax.ShapeDtypeStruct((count, MODEL_WIDTH), jnp.bfloat16),
        compiler_params=pltpu.CompilerParams(vmem_limit_bytes=40 << 20),
        name="lookup",
    )(spans, local_ids[:, None], vocab)


def vocab_grad_kernel(blocks_ref, id_ref, grad_ref, logit_ref, final_ref, left_ref, out_ref):
    step = pl.program_id(0)
    width = left_ref.shape[0]
    chunk = 2 * TILE
    out_ref[...] = left_ref[...] + dot_tn(logit_ref[...], final_ref[...])
    places = step * width + lax.broadcasted_iota(jnp.int32, (width, chunk), 0)

    def one(index, carry):
        rows = pl.ds(pl.multiple_of(index * chunk, chunk), chunk)
        hot = (places == id_ref[:, rows]).astype(jnp.bfloat16)
        out_ref[...] = out_ref[...] + dot(hot, grad_ref[rows, :])
        return carry

    lax.fori_loop(0, blocks_ref[0], one, 0)
    lax.fori_loop(blocks_ref[1], blocks_ref[2], one, 0)


def vocab_grad(left, local_ids, spans, lookups, grad_logits, final_rows):
    count, width = local_ids.shape[0], 4 * TILE
    rows_in = left.shape[0]
    block = pl.BlockSpec((width, MODEL_WIDTH), lambda i, *_: (i, 0))
    return pl.pallas_call(
        vocab_grad_kernel,
        grid_spec=pltpu.PrefetchScalarGridSpec(
            num_scalar_prefetch=1,
            grid=(pl.cdiv(rows_in, width),),
            in_specs=[
                whole_block((1, count)),
                whole_block((count, MODEL_WIDTH)),
                pl.BlockSpec((grad_logits.shape[0], width), lambda i, *_: (0, i)),
                whole_block(final_rows.shape),
                block,
            ],
            out_specs=block,
        ),
        out_shape=jax.ShapeDtypeStruct(left.shape, jnp.float32),
        input_output_aliases={5: 0},
        compiler_params=pltpu.CompilerParams(vmem_limit_bytes=40 << 20),
        name="vocab_grad",
    )(spans, local_ids[None, :], lookups, grad_logits, final_rows, left)


def packing(lengths, room):
    ends = jnp.cumsum(lengths)
    starts = ends - lengths
    places = jnp.arange(room, dtype=jnp.int32)
    segment = jnp.sum((places[:, None] >= ends[None, :]).astype(jnp.int32), axis=1)
    inside = segment[:, None] == jnp.arange(lengths.shape[0], dtype=jnp.int32)[None, :]
    position = places - jnp.sum(jnp.where(inside, starts[None, :], 0), axis=1)
    return segment, position, jnp.minimum(starts, room), jnp.minimum(ends, room)


def key_span(query_segment, query_total, key_starts, key_ends):
    number = key_starts.shape[0]
    count = query_segment.shape[0] // TILE
    begins = jnp.arange(count, dtype=jnp.int32) * TILE
    last_real = jnp.clip(query_total - 1, 0, query_segment.shape[0] - 1)
    finals = jnp.minimum(begins + TILE - 1, last_real)

    def pick(table, places):
        chosen = jnp.sum(
            jnp.where(
                jnp.arange(query_segment.shape[0], dtype=jnp.int32)[None, :] == places[:, None],
                query_segment[None, :],
                0,
            ),
            axis=1,
        )
        return jnp.sum(
            jnp.where(
                chosen[:, None] == jnp.arange(number, dtype=jnp.int32)[None, :], table[None, :], 0
            ),
            axis=1,
        )

    some = begins < query_total
    first = jnp.where(some, pick(key_starts, begins) // TILE, 0)
    last = jnp.where(some, (pick(key_ends, finals) + TILE - 1) // TILE, 0)
    return first, jnp.maximum(first, last)


def column_shards(grads, start, width):
    return [lax.dynamic_slice_in_dim(grad, start, width, 1) for grad in grads]


def packed_gradients(
    source_stream, target_stream, gain_rows, position_bias, weights, layout, head, column_start, column_width
):
    enc_attention, enc_feed, dec = weights
    (
        source_span,
        target_span,
        cross_span,
        source_row,
        source_column,
        target_row,
        target_column,
    ) = layout
    hot_source, hot_target = offset_buckets(False), offset_buckets(True)
    bias_source = jnp.einsum("tkqb,bh->thkq", hot_source, position_bias[0], precision=TOP_PRECISION)
    bias_target = jnp.einsum("tkqb,bh->thkq", hot_target, position_bias[1], precision=TOP_PRECISION)

    def shard(grad):
        return lax.dynamic_slice_in_dim(grad, column_start, column_width, 1)

    def attention(stream, gain_row, context, matrices, span, row, column, causal, bias):
        normed = root_norm(stream, gain_row).astype(jnp.bfloat16)
        context = normed if context is None else context
        queries = dot(normed, matrices[0]).astype(jnp.bfloat16)
        key_rows = dot(context, matrices[1]).astype(jnp.bfloat16)
        value_rows = dot(context, matrices[2]).astype(jnp.bfloat16)
        attended, levels = packed_forward(
            queries, key_rows, value_rows, span, row, column, causal, bias
        )
        return stream + dot(attended, matrices[3]), (
            normed,
            context,
            queries,
            key_rows,
            value_rows,
            attended,
            levels,
        )

    def attention_back(grad, stream, gain_row, crossed, matrices, saved, span, row, column, causal, bias):
        normed, context, queries, key_rows, value_rows, attended, levels = saved
        branch = grad.astype(jnp.bfloat16)
        arriving = dot_nt(branch, matrices[3]).astype(jnp.bfloat16)
        grads = packed_backward(
            queries, arriving, key_rows, value_rows, levels, span, row, column, causal, bias
        )
        grad_queries, grad_keys, grad_values = grads[:3]
        shares = [
            dot_tn(normed, shard(grad_queries)),
            dot_tn(context, shard(grad_keys)),
            dot_tn(context, shard(grad_values)),
            dot_tn(attended, shard(branch)),
        ]
        grad_normed = dot_nt(grad_queries, matrices[0])
        grad_context = dot_nt(grad_keys, matrices[1]) + dot_nt(grad_values, matrices[2])
        if not crossed:
            grad_normed = grad_normed + grad_context
        grad_input, grad_gain = norm_backward(stream, gain_row, grad_normed)
        return grad + grad_input, grad_gain, shares, grads[3:], grad_context

    def feed(stream, gain_row, matrices):
        normed = root_norm(stream, gain_row).astype(jnp.bfloat16)
        inner = [dot(normed, matrices[j]) for j in range(4)]
        hidden = [jax.nn.gelu(a).astype(jnp.bfloat16) for a in inner]
        branch = sum(dot(hidden[j], matrices[4 + j]) for j in range(4))
        return stream + branch, (normed, inner, hidden)

    def feed_back(grad, stream, gain_row, matrices, saved):
        normed, inner, hidden = saved
        branch = grad.astype(jnp.bfloat16)
        grad_inner = [
            jax.vjp(jax.nn.gelu, inner[j])[1](dot_nt(branch, matrices[4 + j]))[0].astype(jnp.bfloat16)
            for j in range(4)
        ]
        grad_normed = sum(dot_nt(grad_inner[j], matrices[j]) for j in range(4))
        branch_shard = shard(branch)
        shares = [dot_tn(normed, shard(grad_inner[j])) for j in range(4)] + [
            dot_tn(hidden[j], branch_shard) for j in range(4)
        ]
        grad_input, grad_gain = norm_backward(stream, gain_row, grad_normed)
        return grad + grad_input, grad_gain, shares

    x1, enc_saved = attention(
        source_stream, gain_rows[0], None, enc_attention, source_span, source_row, source_column, False, bias_source
    )
    x2, enc_feed_saved = feed(x1, gain_rows[1], enc_feed)
    encoded = root_norm(x2, gain_rows[2]).astype(jnp.bfloat16)
    y1, self_saved = attention(
        target_stream, gain_rows[3], None, dec[0:4], target_span, target_row, target_column, True, bias_target
    )
    y2, cross_saved = attention(
        y1, gain_rows[4], encoded, dec[4:8], cross_span, target_row, source_column, False, None
    )
    y3, dec_feed_saved = feed(y2, gain_rows[5], dec[8:16])
    final_rows = (root_norm(y3, gain_rows[6]) * MODEL_WIDTH ** (-0.5)).astype(jnp.bfloat16)

    grad_final, grad_logits, token_loss = head(final_rows)

    grad, gain_final = norm_backward(y3, gain_rows[6], grad_final * MODEL_WIDTH ** (-0.5))
    grad, gain_feed, feed_shares = feed_back(grad, y2, gain_rows[5], dec[8:16], dec_feed_saved)
    grad, gain_cross, cross_shares, _, grad_encoded = attention_back(
        grad, y1, gain_rows[4], True, dec[4:8], cross_saved, cross_span, target_row, source_column, False, None
    )
    target_grad, gain_self, self_shares, table_target, _ = attention_back(
        grad, target_stream, gain_rows[3], False, dec[0:4], self_saved, target_span, target_row, target_column, True, bias_target
    )
    grad, gain_encoded = norm_backward(x2, gain_rows[2], grad_encoded)
    grad, gain_enc_feed, enc_feed_shares = feed_back(grad, x1, gain_rows[1], enc_feed, enc_feed_saved)
    source_grad, gain_enc, enc_shares, table_source, _ = attention_back(
        grad, source_stream, gain_rows[0], False, enc_attention, enc_saved, source_span, source_row, source_column, False, bias_source
    )
    gains = jnp.stack(
        [gain_enc, gain_enc_feed, gain_encoded, gain_self, gain_cross, gain_feed, gain_final]
    )
    tables = jnp.stack(
        [
            jnp.einsum("thkq,tkqb->bh", table_source[0], hot_source, precision=TOP_PRECISION),
            jnp.einsum("thkq,tkqb->bh", table_target[0], hot_target, precision=TOP_PRECISION),
        ]
    )
    shares = jnp.stack(enc_shares + enc_feed_shares + self_shares + cross_shares + feed_shares)
    return shares, gains, tables, source_grad, target_grad, final_rows, grad_logits, token_loss


def orthonormal_kernel(factor_ref, out_ref):
    rank = factor_ref.shape[0]
    for r in range(rank):
        out_ref[r] = factor_ref[r]
    for r in range(rank):
        row = out_ref[r]
        row = row * lax.rsqrt(jnp.sum(row * row, axis=-1, keepdims=True))
        out_ref[r] = row
        for s in range(r + 1, rank):
            other = out_ref[s]
            out_ref[s] = other - row * jnp.sum(row * other, axis=-1, keepdims=True)


def orthonormal_rows(factor):
    return pl.pallas_call(
        orthonormal_kernel,
        out_shape=jax.ShapeDtypeStruct(factor.shape, jnp.float32),
        name="orthonormal",
    )(factor)


def local(
    source_ids,
    targets,
    source_lengths,
    target_lengths,
    task_ids,
    task_counts,
    blocks,
    blocks_momentum,
    embedding,
    embed_momentum,
    gain_rows,
    gain_momentum,
    position_bias,
    bias_momentum,
    right_blocks,
    right_embed,
    error_blocks,
    error_embed,
):
    fsdp_rank = lax.axis_index("fsdp")
    cuts_rank = lax.axis_index("cuts")
    cuts_count = lax.axis_size("cuts")
    seq_count, source_len = source_ids.shape
    target_len = targets.shape[1]
    number = seq_count * lax.axis_size("fsdp")
    room_source = min(ROOM_SOURCE, source_len * number)
    room_target = min(ROOM_TARGET, target_len * number)
    fewest = min(room_source // source_len, room_target // target_len)
    shares_of = sorted({number, -(-number // 2), fewest}, reverse=True)
    vocab_rows = embedding.shape[0]
    vocab_start = fsdp_rank * vocab_rows
    once = (fsdp_rank == 0).astype(jnp.float32)

    def one_round(state):
        _, turn, _, _, left_blocks, left_embed, gains_sum, table_sum, loss_sum = state
        group = lax.all_gather(
            jnp.concatenate(
                [source_ids, targets, source_lengths[:, None], target_lengths[:, None]], axis=1
            ),
            "fsdp",
            axis=0,
            tiled=True,
        )
        group_source = group[:, :source_len]
        group_target = group[:, source_len : source_len + target_len]
        lengths = group[:, -2:]

        def fullest(share):
            padded = jnp.pad(lengths, ((0, -number % share), (0, 0)))
            return jnp.max(jnp.sum(padded.reshape(-1, share, 2), axis=1), axis=0)

        needs = lax.all_gather(
            jnp.concatenate([jnp.sum(lengths, axis=0)] + [fullest(share) for share in shares_of]),
            "cuts",
            axis=0,
        )
        total_count = jnp.sum(needs[:, 1]).astype(jnp.float32)
        most = jnp.max(needs[:, 2:], axis=0)
        share = jnp.int32(shares_of[-1])
        for index in range(len(shares_of) - 2, -1, -1):
            fits = (most[2 * index] <= room_source) & (most[2 * index + 1] <= room_target)
            share = jnp.where(fits, shares_of[index], share)
        members = jnp.arange(number, dtype=jnp.int32)
        taken = (members >= turn * share) & (members < (turn + 1) * share)
        source_taken = jnp.where(taken, lengths[:, 0], 0)
        target_taken = jnp.where(taken, lengths[:, 1], 0)
        more = (turn + 1) * share < number

        chosen = jnp.sum(
            jnp.where(
                task_ids[:, None] == jnp.arange(TASKS, dtype=jnp.int32)[None, :],
                task_counts[None, :],
                0,
            ),
            axis=1,
        ).astype(jnp.float32)
        slice_weight = jnp.sum(
            jnp.where(
                jnp.arange(cuts_count, dtype=jnp.int32) == cuts_rank,
                cuts_count * chosen / jnp.sum(chosen),
                0.0,
            )
        )

        stored_vocab = embedding.T.astype(jnp.bfloat16)
        vocab = gather_cuts(stored_vocab.reshape(2, -1, vocab_rows), cuts_rank, cuts_count)
        vocab = vocab.reshape(2, cuts_count, -1, vocab_rows).transpose(1, 0, 2, 3)
        vocab = vocab.reshape(MODEL_WIDTH, vocab_rows)
        stored = jnp.transpose(blocks, (1, 0, 2)).astype(jnp.bfloat16)
        weights = []
        for begin, end in ((0, 4), (4, 12), (12, 28)):
            columns = lax.all_gather(stored[begin:end], "fsdp", axis=2, tiled=True)
            weights.append(gather_cuts(columns, cuts_rank, cuts_count))

        source_segment, source_place, source_starts, source_ends = packing(source_taken, room_source)
        target_segment, target_place, target_starts, target_ends = packing(target_taken, room_target)
        source_real = source_segment < number
        target_real = target_segment < number
        packed_source = jnp.take(
            group_source.reshape(-1),
            jnp.where(source_real, source_segment * source_len + source_place, 0),
        )
        group_input = jnp.concatenate(
            [jnp.zeros_like(group_target[:, :1]), group_target[:, :-1]], axis=1
        )
        target_from = jnp.where(target_real, target_segment * target_len + target_place, 0)
        packed_target = jnp.take(group_target.reshape(-1), target_from)
        packed_input = jnp.take(group_input.reshape(-1), target_from)
        packed_ids = jnp.concatenate([packed_source, packed_input])
        packed_real = jnp.concatenate([source_real, target_real])
        vocab_places = jnp.arange(vocab_rows, dtype=jnp.int32)
        local_ids = jnp.where(packed_real, packed_ids - vocab_start, -1)
        source_total, target_total = jnp.sum(source_taken), jnp.sum(target_taken)
        chunk = 2 * TILE
        local_ids = jnp.pad(local_ids, (0, -local_ids.shape[0] % chunk), constant_values=-1)
        spans = jnp.stack(
            [
                jnp.minimum((source_total + chunk - 1) // chunk, room_source // chunk),
                jnp.int32(room_source // chunk),
                jnp.minimum(
                    (room_source + target_total + chunk - 1) // chunk,
                    local_ids.shape[0] // chunk,
                ),
            ]
        )
        rows = lax.psum(lookup_rows(local_ids, spans, vocab), "fsdp").astype(jnp.float32)
        source_stream, target_stream = (
            rows[:room_source],
            rows[room_source : room_source + room_target],
        )
        layout = (
            key_span(source_segment, source_total, source_starts, source_ends),
            key_span(target_segment, target_total, target_starts, target_ends),
            key_span(target_segment, target_total, source_starts, source_ends),
            source_segment[None, :],
            source_segment[:, None],
            target_segment[None, :],
            target_segment[:, None],
        )

        token_mask = target_real.astype(jnp.float32)
        token_weight = token_mask * (slice_weight / total_count)
        target_hit = vocab_places[None, :] == (packed_target - vocab_start)[:, None]

        def head(final_rows):
            logits = dot(final_rows, vocab)
            highest = jnp.max(logits, axis=1)
            total_exp = jnp.sum(jnp.exp(logits - highest[:, None]), axis=1)
            picked = jnp.sum(jnp.where(target_hit, logits, 0.0), axis=1)
            stats = lax.all_gather(jnp.stack([highest, total_exp, picked]), "fsdp", axis=0)
            top = jnp.max(stats[:, 0], axis=0)
            log_total = top + jnp.log(
                jnp.sum(stats[:, 1] * jnp.exp(stats[:, 0] - top[None, :]), axis=0)
            )
            token_loss = (log_total - jnp.sum(stats[:, 2], axis=0)) * token_mask
            grad_logits = (
                (jnp.exp(logits - log_total[:, None]) - target_hit.astype(jnp.float32))
                * token_weight[:, None]
            ).astype(jnp.bfloat16)
            grad_rows = lax.psum(dot_nt(grad_logits, vocab), "fsdp")
            return grad_rows, grad_logits, token_loss

        shares, gains, table, source_grad, target_grad, final_rows, grad_logits, token_loss = (
            packed_gradients(
                source_stream,
                target_stream,
                gain_rows,
                position_bias,
                (weights[0], weights[1], weights[2]),
                layout,
                head,
                fsdp_rank * blocks.shape[2],
                blocks.shape[2],
            )
        )
        lookups = jnp.concatenate([source_grad, target_grad]).astype(jnp.bfloat16)
        lookups = jnp.pad(lookups, ((0, local_ids.shape[0] - lookups.shape[0]), (0, 0)))
        left_embed = vocab_grad(left_embed, local_ids, spans, lookups, grad_logits, final_rows)
        return (
            more,
            turn + 1,
            total_count,
            slice_weight,
            left_blocks + shares,
            left_embed,
            gains_sum + gains,
            table_sum + table,
            loss_sum + jnp.sum(token_loss),
        )

    zero = jnp.zeros((), jnp.float32)
    _, _, total_count, slice_weight, left_blocks, left_embed, gains_grad, table_grad, loss_local = (
        lax.while_loop(
            lambda state: state[0],
            one_round,
            (
                jnp.ones((), jnp.bool_),
                jnp.zeros((), jnp.int32),
                zero,
                zero,
                jnp.transpose(error_blocks[0], (1, 0, 2)),
                error_embed[0],
                jnp.zeros_like(gain_rows),
                jnp.zeros_like(position_bias),
                zero,
            ),
        )
    )

    left_factor = jnp.einsum("kij,kjr->rki", left_blocks, right_blocks, precision=TOP_PRECISION)
    embed_factor = jnp.einsum("vd,vr->rd", left_embed, right_embed, precision=TOP_PRECISION)
    factor = jnp.concatenate([left_factor, embed_factor[:, None]], axis=1)
    factor, gains_grad, table_grad, loss_total = lax.psum(
        (factor, gains_grad * once, table_grad * once, loss_local * slice_weight * once),
        ("cuts", "fsdp"),
    )
    factor = orthonormal_rows(factor)
    left_factor, embed_factor = factor[:, :-1], factor[:, -1]
    factors_blocks = jnp.einsum("kij,rki->rkj", left_blocks, left_factor, precision=TOP_PRECISION)
    factors_embed = jnp.einsum("vd,rd->rv", left_embed, embed_factor, precision=TOP_PRECISION)
    rank = factors_blocks.shape[0]
    both = jnp.concatenate([factors_blocks.reshape(rank, -1), factors_embed], axis=1)
    both = lax.psum(both.astype(jnp.bfloat16), "cuts").astype(jnp.float32)
    factors_embed = both[:, -vocab_rows:]
    factors_blocks = both[:, :-vocab_rows].reshape(factors_blocks.shape)
    gram_blocks = jnp.einsum("rki,ski->krs", left_factor, left_factor, precision=TOP_PRECISION)
    gram_embed = jnp.einsum("rd,sd->rs", embed_factor, embed_factor, precision=TOP_PRECISION)
    squares = jnp.sum(
        factors_blocks
        * jnp.einsum("krs,skj->rkj", gram_blocks, factors_blocks, precision=TOP_PRECISION)
    ) + jnp.sum(factors_embed * jnp.dot(gram_embed, factors_embed, precision=TOP_PRECISION))
    squares = lax.psum(squares, "fsdp")
    full_blocks = jnp.einsum("rki,rkj->kij", left_factor, factors_blocks, precision=TOP_PRECISION)
    full_embed = jnp.einsum("rv,rd->vd", factors_embed, embed_factor, precision=TOP_PRECISION)
    owned_rows = blocks.shape[0]
    owned_columns = embedding.shape[1]
    own_left = lax.dynamic_slice_in_dim(left_factor, cuts_rank * owned_rows, owned_rows, 2)
    own_right = lax.dynamic_slice_in_dim(embed_factor, cuts_rank * owned_columns, owned_columns, 1)
    own_blocks = jnp.einsum("rki,rkj->ikj", own_left, factors_blocks, precision=TOP_PRECISION)
    own_embed = jnp.einsum("rv,rd->vd", factors_embed, own_right, precision=TOP_PRECISION)
    small_squares = jnp.sum(gains_grad * gains_grad) + jnp.sum(table_grad * table_grad)
    grad_norm = jnp.sqrt(squares + small_squares)
    clip_factor = jnp.minimum(1.0, CLIP_NORM / grad_norm)
    step_size = STEP_RATE * math.sqrt(PARAMS / MODEL_WIDTH) / CLIP_NORM
    embed_step = step_size * EMBED_SHARE * math.sqrt(MODEL_WIDTH)
    small_step = step_size * SMALL_SHARE * math.sqrt(MODEL_WIDTH)
    momentum_blocks = MOMENTUM_DECAY * blocks_momentum + (1.0 - MOMENTUM_DECAY) * (
        clip_factor * own_blocks
    )
    momentum_embed = MOMENTUM_DECAY * embed_momentum + (1.0 - MOMENTUM_DECAY) * (
        clip_factor * own_embed
    )
    momentum_gains = MOMENTUM_DECAY * gain_momentum + (1.0 - MOMENTUM_DECAY) * (
        clip_factor * gains_grad
    )
    momentum_bias = MOMENTUM_DECAY * bias_momentum + (1.0 - MOMENTUM_DECAY) * (
        clip_factor * table_grad
    )
    return (
        loss_total,
        total_count,
        grad_norm,
        blocks - step_size * momentum_blocks,
        momentum_blocks,
        embedding - embed_step * momentum_embed,
        momentum_embed,
        gain_rows - small_step * momentum_gains,
        momentum_gains,
        position_bias - small_step * momentum_bias,
        momentum_bias,
        jnp.transpose(factors_blocks, (1, 2, 0)),
        factors_embed.T,
        jnp.transpose(left_blocks - full_blocks, (1, 0, 2))[None],
        (left_embed - full_embed)[None],
    )


def solution(mesh):
    return jax.shard_map(
        local,
        mesh=mesh,
        in_specs=(
            P(("cuts", "fsdp"), None),
            P(("cuts", "fsdp"), None),
            P(("cuts", "fsdp")),
            P(("cuts", "fsdp")),
            P(),
            P(),
            P("cuts", None, "fsdp"),
            P("cuts", None, "fsdp"),
            P("fsdp", "cuts"),
            P("fsdp", "cuts"),
            P(),
            P(),
            P(),
            P(),
            P(None, "fsdp", None),
            P("fsdp", None),
            P("cuts", None, None, "fsdp"),
            P("cuts", "fsdp", None),
        ),
        out_specs=(
            P(),
            P(),
            P(),
            P("cuts", None, "fsdp"),
            P("cuts", None, "fsdp"),
            P("fsdp", "cuts"),
            P("fsdp", "cuts"),
            P(),
            P(),
            P(),
            P(),
            P(None, "fsdp", None),
            P("fsdp", None),
            P("cuts", None, None, "fsdp"),
            P("cuts", "fsdp", None),
        ),
        check_vma=False,
    )
```

```python
import itertools
import math

import jax
import jax.numpy as jnp
from jax import lax
from jax.experimental import pallas as pl
from jax.experimental.layout import Layout, with_layout_constraint
from jax.experimental.pallas import tpu as pltpu
from jax.sharding import PartitionSpec as P

MODEL_WIDTH = 768
H = 12
DH = 64
FEED_UNITS = 3072
NBK = 32
TASKS = 8
PARAMS = 41189376


EPSILON = 1e-06
MASKED = -1000000000.0
CLIP_NORM = 0.05
MOMENTUM_DECAY = 0.9
STEP_RATE = 5.0
EMBED_SHARE = 50.0
SMALL_SHARE = 1.0 / 7.0
TOP_PRECISION = lax.Precision.HIGHEST
TILE = 128
ROOM_SOURCE = 1280
ROOM_TARGET = 384
ENCODER_EDGES = (12, 16, 23, 32, 46, 64, 91)
DECODER_EDGES = (19, 21, 24, 27, 31, 35, 40, 46, 52, 59, 67, 77, 87, 99, 113)


def root_norm(stream, gain_row):
    return (
        stream * lax.rsqrt(jnp.mean(stream * stream, axis=-1, keepdims=True) + EPSILON) * gain_row
    )


def norm_backward(stream, gain_row, grad_normed):
    _, pull_back = jax.vjp(root_norm, stream, gain_row)
    return pull_back(grad_normed)


def dot(left, right):
    return jnp.dot(left, right, preferred_element_type=jnp.float32)


def dot_nt(left, right):
    return lax.dot_general(left, right, (((1,), (1,)), ((), ())), preferred_element_type=jnp.float32)


def dot_tn(left, right):
    return lax.dot_general(left, right, (((0,), (0,)), ((), ())), preferred_element_type=jnp.float32)


def exchange(array, mask):
    return lax.ppermute(array, "cuts", [(i, i ^ mask) for i in range(lax.axis_size("cuts"))])


def shifted(array, distance):
    count = lax.axis_size("fsdp")
    return lax.ppermute(array, "fsdp", [(i, (i + distance) % count) for i in range(count)])


def in_order(pieces, rank):
    count = len(pieces)
    ordered = []
    for place in range(count):
        chosen = pieces[-place % count]
        for own in range(1, count):
            chosen = jnp.where(rank == own, pieces[(own - place) % count], chosen)
        ordered.append(chosen)
    return ordered


def gather_fsdp(part, rank):
    count = lax.axis_size("fsdp")
    return in_order([part] + [shifted(part, distance) for distance in range(1, count)], rank)


def sum_fsdp(part, rank):
    count = lax.axis_size("fsdp")
    rows = part.shape[0] // count
    low = part.astype(jnp.bfloat16)
    total = lax.dynamic_slice_in_dim(part, rank * rows, rows, 0)
    for distance in range(1, count):
        piece = lax.dynamic_slice_in_dim(low, (rank + distance) % count * rows, rows, 0)
        total = total + shifted(piece, distance).astype(jnp.float32)
    return jnp.concatenate(gather_fsdp(total.astype(jnp.bfloat16), rank), axis=0).astype(jnp.float32)


def sum_everywhere(part, cuts_rank):
    count = lax.axis_size("cuts")
    masks = [1 << bit for bit in range(count.bit_length() - 1)]
    if count & (count - 1) or part.shape[0] % count:
        return lax.psum(part, ("cuts", "fsdp"))
    bits = [(cuts_rank // mask) % 2 for mask in masks]
    for mask, bit in zip(masks, bits):
        half = part.shape[0] // 2
        away = lax.dynamic_slice_in_dim(part, (1 - bit) * half, half, 0)
        part = lax.dynamic_slice_in_dim(part, bit * half, half, 0) + exchange(away, mask)
    part = jnp.sum(lax.all_gather(part, "fsdp", axis=0), axis=0)
    for mask, bit in zip(masks[::-1], bits[::-1]):
        other = exchange(part, mask)
        part = jnp.where(
            bit == 1, jnp.concatenate([other, part], axis=0), jnp.concatenate([part, other], axis=0)
        )
    return part


def sum_cuts(part):
    count = lax.axis_size("cuts")
    if count & (count - 1):
        return lax.psum(part.astype(jnp.bfloat16), "cuts").astype(jnp.float32)
    for bit in range(count.bit_length() - 1):
        low = part.astype(jnp.bfloat16)
        part = low.astype(jnp.float32) + exchange(low, 1 << bit).astype(jnp.float32)
    return part


def spread_ways():
    return [1 << bit for bit in range(1, lax.axis_size("cuts").bit_length() - 1)]


def spread_begin(part):
    number = max(min(len(spread_ways()), part.shape[0]), 1)
    ends = [part.shape[0] * turn // number for turn in range(number + 1)]
    return [([0], part[None, begin:end]) for begin, end in zip(ends, ends[1:])]


def spread_step(shares, step):
    ways = spread_ways()
    after = []
    for turn, (bits, held) in enumerate(shares):
        mask = ways[(turn + step) % len(ways)]
        after.append(
            (bits + [bit ^ mask for bit in bits], jnp.concatenate([held, exchange(held, mask)]))
        )
    return after


def spread_end(shares):
    found, first = [], 0
    for bits, held in shares:
        found.append((first, [(bits, held), ([bit ^ 1 for bit in bits], exchange(held, 1))]))
        first += held.shape[1]
    return found


def spread_tied(shares, *others):
    arrays, others = lax.optimization_barrier(([held for _, held in shares], others))
    return [(bits, held) for (bits, _), held in zip(shares, arrays)], *others


def cost(flops, moved, powers=0):
    return pl.CostEstimate(flops=int(flops), bytes_accessed=int(moved), transcendentals=int(powers))


def place_kernel(moves, number, rank_ref, *refs):
    sources, outs, sem = refs[:number], refs[number:-1], refs[-1]
    rank = rank_ref[0]
    copies = []
    for source, piece, index, bits, (out, pitch, row, column), shape in moves:
        rows = pl.ds(pl.multiple_of((rank ^ bits) * pitch + row, 16), shape[0])
        copies.append(
            pltpu.make_async_copy(
                sources[source].at[piece, index],
                outs[out].at[rows, pl.ds(column, shape[1])],
                sem.at[len(copies)],
            )
        )
    for copy in copies:
        copy.start()
    for copy in copies:
        copy.wait()


def place_pieces(found, groups, rank):
    count = lax.axis_size("cuts")
    height, width = found[0][1][0][1].shape[2:]
    where = {}
    shapes = []
    for out, (members, how) in enumerate(groups):
        for order, matrix in enumerate(members):
            row = {"columns": 0, "rows": order * count * height, "mixed": order * height}[how]
            pitch = height * (len(members) if how == "mixed" else 1)
            where[matrix] = (out, pitch, row, order * width if how == "columns" else 0)
        tall, wide = (1, len(members)) if how == "columns" else (len(members), 1)
        shapes.append((tall * count * height, wide * width))
    sources, moves = [], []
    for first, held in found:
        for bits, array in held:
            for piece, index in itertools.product(range(array.shape[0]), range(array.shape[1])):
                if first + index in where:
                    moves.append(
                        (len(sources), piece, index, bits[piece], where[first + index], (height, width))
                    )
            sources.append(array)
    space = pl.BlockSpec(memory_space=pl.ANY)
    return pl.pallas_call(
        lambda *refs: place_kernel(moves, len(sources), *refs),
        in_specs=[pl.BlockSpec(memory_space=pltpu.SMEM)] + [space] * len(sources),
        out_specs=[pl.BlockSpec(memory_space=pltpu.VMEM)] * len(shapes),
        out_shape=[jax.ShapeDtypeStruct(shape, sources[0].dtype) for shape in shapes],
        scratch_shapes=[pltpu.SemaphoreType.DMA((len(moves),))],
        compiler_params=pltpu.CompilerParams(vmem_limit_bytes=40 << 20),
        cost_estimate=cost(0, 5 * sum(math.prod(shape) for shape in shapes)),
        name="place",
    )(rank[None], *sources)


def unset_kernel(out_ref):
    pass


def unset(shape):
    return pl.pallas_call(
        unset_kernel,
        out_specs=pl.BlockSpec(memory_space=pl.ANY),
        out_shape=jax.ShapeDtypeStruct(shape, jnp.float32),
        name="unset",
    )()


PAIRS = H // 2
WIDE = 2 * TILE


def offset_buckets(causal, offset):
    if causal:
        distance = jnp.maximum(-offset, 0)
        farther = 16 + sum(((distance >= boundary).astype(jnp.int32) for boundary in DECODER_EDGES))
        bucket = jnp.where(distance < 16, distance, farther)
    else:
        distance = jnp.abs(offset)
        farther = 8 + sum(((distance >= boundary).astype(jnp.int32) for boundary in ENCODER_EDGES))
        bucket = jnp.where(distance < 8, distance, farther) + jnp.where(offset > 0, 16, 0)
    return (bucket[..., None] == jnp.arange(NBK, dtype=jnp.int32)).astype(jnp.float32)


def bias_kernel(row_ref, out_ref):
    for head in range(H):
        row = jnp.broadcast_to(row_ref[0, head : head + 1, :], (TILE, WIDE))
        tile = pltpu.roll(row, 0, 1, stride=1, stride_axis=0)[:, :TILE]
        out_ref[0, head // 2, :, (head % 2) * TILE : (head % 2 + 1) * TILE] = tile


def bias_tiles(causal, table):
    lane = jnp.arange(WIDE, dtype=jnp.int32)
    offset = (jnp.arange(5, dtype=jnp.int32)[:, None] - 2) * TILE + jnp.where(
        lane < TILE, -lane, WIDE - lane
    )
    rows = jnp.einsum(
        "tqb,bh->thq", offset_buckets(causal, offset), table, precision=TOP_PRECISION
    )
    return pl.pallas_call(
        bias_kernel,
        grid=(5,),
        in_specs=[pl.BlockSpec((1, 16, WIDE), lambda i: (i, 0, 0))],
        out_specs=pl.BlockSpec((1, PAIRS, TILE, WIDE), lambda i: (i, 0, 0, 0)),
        out_shape=jax.ShapeDtypeStruct((5, PAIRS, TILE, WIDE), jnp.float32),
        name="bias",
    )(jnp.pad(rows, ((0, 0), (0, 16 - H), (0, 0))))


def bias_grad(tiles, causal):
    places = jnp.arange(TILE, dtype=jnp.int32)
    offset = (
        (jnp.arange(5, dtype=jnp.int32)[:, None, None] - 2) * TILE
        + places[None, :, None]
        - places[None, None, :]
    )
    hot = offset_buckets(causal, offset)
    found = [
        jnp.einsum("tpkq,tkqb->bp", tiles[..., half], hot, precision=lax.Precision.HIGH)
        for half in (slice(0, TILE), slice(TILE, WIDE))
    ]
    return jnp.stack(found, axis=-1).reshape(NBK, H)


def stack_heads(pair):
    half = lax.broadcasted_iota(jnp.int32, (TILE, TILE), 1) // DH
    return jnp.concatenate(
        [jnp.where(half == which, pair, jnp.zeros_like(pair)) for which in range(2)], axis=0
    )


def own_features(wide):
    return jnp.concatenate([wide[:DH, :TILE], wide[DH:, TILE:]], axis=0)


def kept(segment_column, segment_row, key_tile, query_tile, causal):
    keep = segment_column == jnp.concatenate([segment_row, segment_row], axis=1)
    if causal:
        key_place = key_tile * TILE + lax.broadcasted_iota(jnp.int32, (TILE, WIDE), 0)
        query_place = query_tile * TILE + lax.broadcasted_iota(jnp.int32, (TILE, WIDE), 1) % TILE
        keep = keep & (key_place <= query_place)
    return keep


def tile_scores(keys, queries, keep, bias):
    scores = dot_nt(keys, queries)
    if bias is not None:
        scores = scores + bias
    return jnp.where(keep, scores, MASKED)


def forward_kernel(
    causal, biased, first_ref, last_ref, q_ref, k_ref, v_ref, row_ref, column_ref, *rest
):
    bias_ref = rest[0] if biased else None
    out_ref, level_ref, stack_ref, top_ref, sum_ref, total_ref = rest[1:] if biased else rest
    here = pl.program_id(0)
    top_ref[...] = jnp.full_like(top_ref, -1e30)
    sum_ref[...] = jnp.zeros_like(sum_ref)
    total_ref[...] = jnp.zeros_like(total_ref)
    segment_row = row_ref[...]
    for pair in range(PAIRS):
        stack_ref[pair] = stack_heads(q_ref[:, pair * TILE : (pair + 1) * TILE])

    def step(there, carry):
        rows = pl.ds(pl.multiple_of(there * TILE, TILE), TILE)
        keep = kept(column_ref[rows, :], segment_row, there, here, causal)
        offset = jnp.clip(there - here, -2, 2) + 2
        before, sums = top_ref[...], sum_ref[...]
        tops, sums_after = [], []
        for pair in range(PAIRS):
            lanes = slice(pair * TILE, (pair + 1) * TILE)
            scores = tile_scores(
                k_ref[rows, lanes], stack_ref[pair], keep, bias_ref[offset, pair] if biased else None
            )
            old = before[pair : pair + 1, :]
            top = jnp.maximum(old, jnp.max(scores, axis=0, keepdims=True))
            weights = jnp.exp(scores - top)
            scale = jnp.exp(old - top)
            tops.append(top)
            sums_after.append(
                sums[pair : pair + 1, :] * scale + jnp.sum(weights, axis=0, keepdims=True)
            )
            total_ref[pair] = total_ref[pair] * scale + dot(
                v_ref[rows, lanes].T, weights.astype(jnp.bfloat16)
            )
        for pair in range(PAIRS):
            top_ref[pair : pair + 1, :] = tops[pair]
            sum_ref[pair : pair + 1, :] = sums_after[pair]
        return carry

    lax.fori_loop(first_ref[here], last_ref[here], step, 0)
    seen = sum_ref[...] > 0.0
    divisor = jnp.where(seen, sum_ref[...], 1.0)
    level_ref[...] = jnp.where(seen, top_ref[...] + jnp.log(divisor), 0.0)
    for pair in range(PAIRS):
        lanes = slice(pair * TILE, (pair + 1) * TILE)
        wide = total_ref[pair] / divisor[pair : pair + 1, :]
        out_ref[:, lanes] = own_features(wide).T.astype(jnp.bfloat16)


def backward_kernel(
    causal, biased, first_ref, last_ref, q_ref, o_ref, k_ref, v_ref, level_ref, row_ref, column_ref, *rest
):
    bias_ref = rest[0] if biased else None
    rest = rest[1:] if biased else rest
    gq_ref, gkv_ref = rest[:2]
    gb_ref = rest[2] if biased else None
    weight_ref, slope_ref, mean_ref, stack_ref, arrive_ref, tq_ref, tk_ref, tv_ref = rest[-8:]
    here = pl.program_id(0)

    @pl.when(here == 0)
    def _():
        tk_ref[...] = jnp.zeros_like(tk_ref)
        tv_ref[...] = jnp.zeros_like(tv_ref)
        if biased:
            gb_ref[...] = jnp.zeros_like(gb_ref)

    mean_ref[...] = jnp.zeros_like(mean_ref)
    tq_ref[...] = jnp.zeros_like(tq_ref)
    segment_row = row_ref[...]
    first = first_ref[here]
    last = last_ref[here]
    for pair in range(PAIRS):
        lanes = slice(pair * TILE, (pair + 1) * TILE)
        stack_ref[pair] = stack_heads(q_ref[:, lanes])
        arrive_ref[pair] = stack_heads(o_ref[:, lanes])

    def look(there, carry):
        rows = pl.ds(pl.multiple_of(there * TILE, TILE), TILE)
        keep = kept(column_ref[rows, :], segment_row, there, here, causal)
        offset = jnp.clip(there - here, -2, 2) + 2
        means = mean_ref[...]
        sums = []
        for pair in range(PAIRS):
            lanes = slice(pair * TILE, (pair + 1) * TILE)
            scores = tile_scores(
                k_ref[rows, lanes], stack_ref[pair], keep, bias_ref[offset, pair] if biased else None
            )
            weights = jnp.exp(scores - level_ref[pair : pair + 1, :])
            slopes = dot_nt(v_ref[rows, lanes], arrive_ref[pair])
            sums.append(
                means[pair : pair + 1, :] + jnp.sum(weights * slopes, axis=0, keepdims=True)
            )
            weight_ref[there - first, pair] = weights
            slope_ref[there - first, pair] = slopes
            tv_ref[rows, lanes] = tv_ref[rows, lanes] + dot(
                weights.astype(jnp.bfloat16), arrive_ref[pair]
            )
        for pair in range(PAIRS):
            mean_ref[pair : pair + 1, :] = sums[pair]
        return carry

    def push(there, carry):
        rows = pl.ds(pl.multiple_of(there * TILE, TILE), TILE)
        offset = jnp.clip(there - here, -2, 2) + 2
        for pair in range(PAIRS):
            lanes = slice(pair * TILE, (pair + 1) * TILE)
            slopes = (
                weight_ref[there - first, pair]
                * (slope_ref[there - first, pair] - mean_ref[pair : pair + 1, :])
            ).astype(jnp.bfloat16)
            if biased:
                gb_ref[offset, pair] = gb_ref[offset, pair] + slopes.astype(jnp.float32)
            tq_ref[pair] = tq_ref[pair] + dot(k_ref[rows, lanes].T, slopes)
            tk_ref[rows, lanes] = tk_ref[rows, lanes] + dot(slopes, stack_ref[pair])
        return carry

    lax.fori_loop(first, last, look, 0)
    lax.fori_loop(first, last, push, 0)
    for pair in range(PAIRS):
        lanes = slice(pair * TILE, (pair + 1) * TILE)
        gq_ref[:, lanes] = own_features(tq_ref[pair]).T.astype(jnp.bfloat16)

    @pl.when(here == pl.num_programs(0) - 1)
    def _():
        gkv_ref[:, :MODEL_WIDTH] = tk_ref[...].astype(jnp.bfloat16)
        gkv_ref[:, MODEL_WIDTH:] = tv_ref[...].astype(jnp.bfloat16)


def whole_block(shape):
    return pl.BlockSpec(shape, lambda i, *_: (0,) * len(shape))


def column_block(rows, index):
    return pl.BlockSpec((rows, MODEL_WIDTH), lambda i, *_: (0, index))


def packed_forward(queries, pair_rows, span, segment_row, segment_column, causal, bias):
    count, other = queries.shape[0], pair_rows.shape[0]
    biased = bias is not None
    tile = pl.BlockSpec((TILE, MODEL_WIDTH), lambda i, *_: (i, 0))
    return pl.pallas_call(
        lambda *refs: forward_kernel(causal, biased, *refs),
        grid_spec=pltpu.PrefetchScalarGridSpec(
            num_scalar_prefetch=2,
            grid=(count // TILE,),
            in_specs=[
                tile,
                column_block(other, 0),
                column_block(other, 1),
                pl.BlockSpec((1, TILE), lambda i, *_: (0, i)),
                whole_block((other, 1)),
            ]
            + ([whole_block((5, PAIRS, TILE, WIDE))] if biased else []),
            out_specs=[tile, pl.BlockSpec((8, WIDE), lambda i, *_: (0, i))],
            scratch_shapes=[
                pltpu.VMEM((PAIRS, WIDE, TILE), jnp.bfloat16),
                pltpu.VMEM((8, WIDE), jnp.float32),
                pltpu.VMEM((8, WIDE), jnp.float32),
                pltpu.VMEM((PAIRS, TILE, WIDE), jnp.float32),
            ],
        ),
        out_shape=[
            jax.ShapeDtypeStruct((count, MODEL_WIDTH), jnp.bfloat16),
            jax.ShapeDtypeStruct((8, 2 * count), jnp.float32),
        ],
        compiler_params=pltpu.CompilerParams(vmem_limit_bytes=40 << 20),
        cost_estimate=cost(8 * count * other * MODEL_WIDTH, 20 << 20),
        name="attend",
    )(*span, queries, pair_rows, pair_rows, segment_row, segment_column, *([bias] if biased else []))


def packed_backward(
    queries, grad_out, pair_rows, levels, span, segment_row, segment_column, causal, bias
):
    count, other = queries.shape[0], pair_rows.shape[0]
    biased = bias is not None
    reach = min(other // TILE, 9) if biased else other // TILE
    tile = pl.BlockSpec((TILE, MODEL_WIDTH), lambda i, *_: (i, 0))
    table = (5, PAIRS, TILE, WIDE)
    return pl.pallas_call(
        lambda *refs: backward_kernel(causal, biased, *refs),
        grid_spec=pltpu.PrefetchScalarGridSpec(
            num_scalar_prefetch=2,
            grid=(count // TILE,),
            in_specs=[
                tile,
                tile,
                column_block(other, 0),
                column_block(other, 1),
                pl.BlockSpec((8, WIDE), lambda i, *_: (0, i)),
                pl.BlockSpec((1, TILE), lambda i, *_: (0, i)),
                whole_block((other, 1)),
            ]
            + ([whole_block(table)] if biased else []),
            out_specs=[tile, whole_block((other, 2 * MODEL_WIDTH))]
            + ([whole_block(table)] if biased else []),
            scratch_shapes=[
                pltpu.VMEM((reach, PAIRS, TILE, WIDE), jnp.float32),
                pltpu.VMEM((reach, PAIRS, TILE, WIDE), jnp.float32),
                pltpu.VMEM((8, WIDE), jnp.float32),
                pltpu.VMEM((PAIRS, WIDE, TILE), jnp.bfloat16),
                pltpu.VMEM((PAIRS, WIDE, TILE), jnp.bfloat16),
                pltpu.VMEM((PAIRS, TILE, WIDE), jnp.float32),
                pltpu.VMEM((other, MODEL_WIDTH), jnp.float32),
                pltpu.VMEM((other, MODEL_WIDTH), jnp.float32),
            ],
        ),
        out_shape=[
            jax.ShapeDtypeStruct((count, MODEL_WIDTH), jnp.bfloat16),
            jax.ShapeDtypeStruct((other, 2 * MODEL_WIDTH), jnp.bfloat16),
        ]
        + ([jax.ShapeDtypeStruct(table, jnp.float32)] if biased else []),
        compiler_params=pltpu.CompilerParams(vmem_limit_bytes=58 << 20),
        cost_estimate=cost(20 * count * other * MODEL_WIDTH, 40 << 20),
        name="attend_back",
    )(
        *span,
        queries,
        grad_out,
        pair_rows,
        pair_rows,
        levels,
        segment_row,
        segment_column,
        *([bias] if biased else []),
    )


def lookup_kernel(rows_in, blocks_ref, id_ref, vocab_ref, out_ref, total_ref):
    step = pl.program_id(0)
    width = vocab_ref.shape[1]
    chunk = 2 * TILE

    @pl.when(step == 0)
    def _():
        total_ref[...] = jnp.zeros_like(total_ref)

    inside = step * width + lax.broadcasted_iota(jnp.int32, (1, width), 1) < rows_in
    table = jnp.where(inside, vocab_ref[...], jnp.zeros_like(vocab_ref[...]))
    places = step * width + lax.broadcasted_iota(jnp.int32, (chunk, width), 1)

    def one(index, carry):
        rows = pl.ds(pl.multiple_of(index * chunk, chunk), chunk)
        hot = (id_ref[rows, :] == places).astype(jnp.bfloat16)
        total_ref[rows, :] = total_ref[rows, :] + dot_nt(hot, table)
        return carry

    lax.fori_loop(0, blocks_ref[0], one, 0)
    lax.fori_loop(blocks_ref[1], blocks_ref[2], one, 0)

    @pl.when(step == pl.num_programs(0) - 1)
    def _():
        out_ref[...] = total_ref[...].astype(jnp.bfloat16)


def lookup_rows(local_ids, spans, vocab):
    count, width = local_ids.shape[0], 4 * TILE
    rows_in = vocab.shape[1]
    return pl.pallas_call(
        lambda *refs: lookup_kernel(rows_in, *refs),
        grid_spec=pltpu.PrefetchScalarGridSpec(
            num_scalar_prefetch=1,
            grid=(pl.cdiv(rows_in, width),),
            in_specs=[
                whole_block((count, 1)),
                pl.BlockSpec((MODEL_WIDTH, width), lambda i, *_: (0, i)),
            ],
            out_specs=whole_block((count, MODEL_WIDTH)),
            scratch_shapes=[pltpu.VMEM((count, MODEL_WIDTH), jnp.float32)],
        ),
        out_shape=jax.ShapeDtypeStruct((count, MODEL_WIDTH), jnp.bfloat16),
        compiler_params=pltpu.CompilerParams(vmem_limit_bytes=40 << 20),
        cost_estimate=cost(2 * count * rows_in * MODEL_WIDTH, 90 << 20),
        name="lookup",
    )(spans, local_ids[:, None], vocab)


def vocab_grad_kernel(blocks_ref, id_ref, grad_ref, logit_ref, final_ref, start_ref, left_ref, out_ref):
    step = pl.program_id(0)
    width = left_ref.shape[0]
    chunk = 2 * TILE
    before = jnp.where(blocks_ref[3] == 0, start_ref[...], left_ref[...])
    out_ref[...] = before + dot_tn(logit_ref[...], final_ref[...])
    places = step * width + lax.broadcasted_iota(jnp.int32, (width, chunk), 0)

    def one(index, carry):
        rows = pl.ds(pl.multiple_of(index * chunk, chunk), chunk)
        hot = (places == id_ref[:, rows]).astype(jnp.bfloat16)
        out_ref[...] = out_ref[...] + dot(hot, grad_ref[rows, :])
        return carry

    lax.fori_loop(0, blocks_ref[0], one, 0)
    lax.fori_loop(blocks_ref[1], blocks_ref[2], one, 0)


def vocab_grad(start, left, turn, local_ids, spans, lookups, grad_logits, final_rows):
    count, width = local_ids.shape[0], 4 * TILE
    rows_in = left.shape[0]
    block = pl.BlockSpec((width, MODEL_WIDTH), lambda i, *_: (i, 0))
    return pl.pallas_call(
        vocab_grad_kernel,
        grid_spec=pltpu.PrefetchScalarGridSpec(
            num_scalar_prefetch=1,
            grid=(pl.cdiv(rows_in, width),),
            in_specs=[
                whole_block((1, count)),
                whole_block((count, MODEL_WIDTH)),
                pl.BlockSpec((grad_logits.shape[0], width), lambda i, *_: (0, i)),
                whole_block(final_rows.shape),
                pl.BlockSpec((width, MODEL_WIDTH), lambda i, s: (jnp.where(s[3] == 0, i, 0), 0)),
                pl.BlockSpec((width, MODEL_WIDTH), lambda i, s: (jnp.where(s[3] == 0, 0, i), 0)),
            ],
            out_specs=block,
        ),
        out_shape=jax.ShapeDtypeStruct(left.shape, jnp.float32),
        input_output_aliases={6: 0},
        compiler_params=pltpu.CompilerParams(vmem_limit_bytes=40 << 20),
        cost_estimate=cost(2 * (count + 384) * rows_in * MODEL_WIDTH, 100 << 20),
        name="vocab_grad",
    )(
        jnp.concatenate([spans, turn[None]]),
        local_ids[None, :],
        lookups,
        grad_logits,
        final_rows,
        start,
        left,
    )


def packing(lengths, room):
    ends = jnp.cumsum(lengths)
    starts = ends - lengths
    places = jnp.arange(room, dtype=jnp.int32)
    segment = jnp.sum((places[:, None] >= ends[None, :]).astype(jnp.int32), axis=1)
    inside = segment[:, None] == jnp.arange(lengths.shape[0], dtype=jnp.int32)[None, :]
    position = places - jnp.sum(jnp.where(inside, starts[None, :], 0), axis=1)
    return segment, position, jnp.minimum(starts, room), jnp.minimum(ends, room)


def key_span(query_segment, query_total, key_starts, key_ends):
    number = key_starts.shape[0]
    count = query_segment.shape[0] // TILE
    begins = jnp.arange(count, dtype=jnp.int32) * TILE
    last_real = jnp.clip(query_total - 1, 0, query_segment.shape[0] - 1)
    finals = jnp.minimum(begins + TILE - 1, last_real)

    def pick(table, places):
        chosen = jnp.sum(
            jnp.where(
                jnp.arange(query_segment.shape[0], dtype=jnp.int32)[None, :] == places[:, None],
                query_segment[None, :],
                0,
            ),
            axis=1,
        )
        return jnp.sum(
            jnp.where(
                chosen[:, None] == jnp.arange(number, dtype=jnp.int32)[None, :], table[None, :], 0
            ),
            axis=1,
        )

    some = begins < query_total
    first = jnp.where(some, pick(key_starts, begins) // TILE, 0)
    last = jnp.where(some, (pick(key_ends, finals) + TILE - 1) // TILE, 0)
    return first, jnp.maximum(first, last)


def packed_gradients(
    source_stream, target_stream, gain_rows, position_bias, weights, layout, head, column_start, column_width
):
    enc_attention, enc_feed, dec_self, dec_cross, dec_feed = weights
    (
        source_span,
        target_span,
        cross_span,
        source_row,
        source_column,
        target_row,
        target_column,
    ) = layout
    bias_source = bias_tiles(False, position_bias[0])
    bias_target = bias_tiles(True, position_bias[1])

    def shard(grad, which=0):
        return lax.dynamic_slice_in_dim(grad, which * MODEL_WIDTH + column_start, column_width, 1)

    def attention(stream, gain_row, context, matrices, span, row, column, causal, bias):
        to_query, to_pair, outward = matrices
        normed = root_norm(stream, gain_row).astype(jnp.bfloat16)
        context = normed if context is None else context
        queries = dot(normed, to_query).astype(jnp.bfloat16)
        pair_rows = dot(context, to_pair).astype(jnp.bfloat16)
        attended, levels = packed_forward(queries, pair_rows, span, row, column, causal, bias)
        return stream + dot(attended, outward), (
            normed,
            context,
            queries,
            pair_rows,
            attended,
            levels,
        )

    def attention_back(grad, stream, gain_row, crossed, matrices, saved, span, row, column, causal, bias):
        to_query, to_pair, outward = matrices
        normed, context, queries, pair_rows, attended, levels = saved
        branch = grad.astype(jnp.bfloat16)
        arriving = dot_nt(branch, outward).astype(jnp.bfloat16)
        grads = packed_backward(
            queries, arriving, pair_rows, levels, span, row, column, causal, bias
        )
        grad_queries, grad_pair = grads[:2]
        pair_shards = [shard(grad_pair), shard(grad_pair, 1)]
        if crossed:
            shares = [
                dot_tn(shard(grad_queries), normed),
                dot_tn(jnp.concatenate(pair_shards, axis=1), context),
                dot_tn(shard(branch), attended),
            ]
        else:
            shares = [
                dot_tn(jnp.concatenate([shard(grad_queries)] + pair_shards, axis=1), normed),
                dot_tn(shard(branch), attended),
            ]
        grad_normed = dot_nt(grad_queries, to_query)
        grad_context = dot_nt(grad_pair, to_pair)
        if not crossed:
            grad_normed = grad_normed + grad_context
        grad_input, grad_gain = norm_backward(stream, gain_row, grad_normed)
        return grad + grad_input, grad_gain, shares, grads[2:], grad_context

    def feed(stream, gain_row, matrices):
        inward, outward = matrices
        normed = root_norm(stream, gain_row).astype(jnp.bfloat16)
        inner = dot(normed, inward)
        hidden = jax.nn.gelu(inner).astype(jnp.bfloat16)
        return stream + dot(hidden, outward), (normed, inner, hidden)

    def feed_back(grad, stream, gain_row, matrices, saved):
        inward, outward = matrices
        normed, inner, hidden = saved
        branch = grad.astype(jnp.bfloat16)
        grad_inner = jax.vjp(jax.nn.gelu, inner)[1](dot_nt(branch, outward))[0].astype(jnp.bfloat16)
        grad_normed = dot_nt(grad_inner, inward)
        inner_shards = jnp.concatenate([shard(grad_inner, j) for j in range(4)], axis=1)
        outward_shares = dot_tn(shard(branch), hidden)
        shares = [dot_tn(inner_shards, normed)] + [
            outward_shares[:, j * MODEL_WIDTH : (j + 1) * MODEL_WIDTH] for j in range(4)
        ]
        grad_input, grad_gain = norm_backward(stream, gain_row, grad_normed)
        return grad + grad_input, grad_gain, shares

    x1, enc_saved = attention(
        source_stream, gain_rows[0], None, enc_attention, source_span, source_row, source_column, False, bias_source
    )
    x2, enc_feed_saved = feed(x1, gain_rows[1], enc_feed)
    encoded = root_norm(x2, gain_rows[2]).astype(jnp.bfloat16)
    encoded, target_stream = lax.optimization_barrier((encoded, target_stream))
    target_stream = target_stream.astype(jnp.float32)
    y1, self_saved = attention(
        target_stream, gain_rows[3], None, dec_self, target_span, target_row, target_column, True, bias_target
    )
    y2, cross_saved = attention(
        y1, gain_rows[4], encoded, dec_cross, cross_span, target_row, source_column, False, None
    )
    y3, dec_feed_saved = feed(y2, gain_rows[5], dec_feed)
    final_rows = (root_norm(y3, gain_rows[6]) * MODEL_WIDTH ** (-0.5)).astype(jnp.bfloat16)

    grad_final, grad_logits, token_loss = head(final_rows)

    grad, gain_final = norm_backward(y3, gain_rows[6], grad_final * MODEL_WIDTH ** (-0.5))
    grad, gain_feed, feed_shares = feed_back(grad, y2, gain_rows[5], dec_feed, dec_feed_saved)
    grad, gain_cross, cross_shares, _, grad_encoded = attention_back(
        grad, y1, gain_rows[4], True, dec_cross, cross_saved, cross_span, target_row, source_column, False, None
    )
    target_grad, gain_self, self_shares, table_target, _ = attention_back(
        grad, target_stream, gain_rows[3], False, dec_self, self_saved, target_span, target_row, target_column, True, bias_target
    )
    grad, gain_encoded = norm_backward(x2, gain_rows[2], grad_encoded)
    grad, gain_enc_feed, enc_feed_shares = feed_back(grad, x1, gain_rows[1], enc_feed, enc_feed_saved)
    source_grad, gain_enc, enc_shares, table_source, _ = attention_back(
        grad, source_stream, gain_rows[0], False, enc_attention, enc_saved, source_span, source_row, source_column, False, bias_source
    )
    gains = jnp.stack(
        [gain_enc, gain_enc_feed, gain_encoded, gain_self, gain_cross, gain_feed, gain_final]
    )
    tables = jnp.stack(
        [
            bias_grad(table_source[0], False),
            bias_grad(table_target[0], True),
        ]
    )
    shares = jnp.concatenate(
        enc_shares + enc_feed_shares + self_shares + cross_shares + feed_shares
    ).reshape(-1, column_width, MODEL_WIDTH)
    return shares, gains, tables, source_grad, target_grad, final_rows, grad_logits, token_loss


def orthonormal_kernel(factor_ref, out_ref):
    rank = factor_ref.shape[0]
    for r in range(rank):
        out_ref[r] = factor_ref[r]
    for r in range(rank):
        row = out_ref[r]
        row = row * lax.rsqrt(jnp.sum(row * row, axis=-1, keepdims=True))
        out_ref[r] = row
        for s in range(r + 1, rank):
            other = out_ref[s]
            out_ref[s] = other - row * jnp.sum(row * other, axis=-1, keepdims=True)


def orthonormal_rows(factor):
    return pl.pallas_call(
        orthonormal_kernel,
        out_shape=jax.ShapeDtypeStruct(factor.shape, jnp.float32),
        name="orthonormal",
    )(factor)


def local(
    source_ids,
    targets,
    source_lengths,
    target_lengths,
    task_ids,
    task_counts,
    blocks,
    blocks_momentum,
    embedding,
    embed_momentum,
    gain_rows,
    gain_momentum,
    position_bias,
    bias_momentum,
    right_blocks,
    right_embed,
    error_blocks,
    error_embed,
):
    fsdp_rank = lax.axis_index("fsdp")
    cuts_rank = lax.axis_index("cuts")
    cuts_count = lax.axis_size("cuts")
    seq_count, source_len = source_ids.shape
    target_len = targets.shape[1]
    number = seq_count * lax.axis_size("fsdp")
    room_source = min(ROOM_SOURCE, source_len * number)
    room_target = min(ROOM_TARGET, target_len * number)
    fewest = min(room_source // source_len, room_target // target_len)
    shares_of = sorted({number, -(-number // 2), fewest}, reverse=True)
    vocab_rows = embedding.shape[0]
    vocab_start = fsdp_rank * vocab_rows
    once = (fsdp_rank == 0).astype(jnp.float32)

    stored_vocab = embedding.T.astype(jnp.bfloat16)
    steps = len(spread_ways())
    bands = max(n for n in range(1, max(steps, 1) + 1) if stored_vocab.shape[0] % (16 * n) == 0 or n == 1)
    vocab_shares = spread_begin(stored_vocab.reshape(bands, -1, vocab_rows))
    stored = jnp.transpose(blocks, (1, 0, 2)).astype(jnp.bfloat16)
    group = lax.all_gather(
        jnp.concatenate(
            [source_ids, targets, source_lengths[:, None], target_lengths[:, None]], axis=1
        ),
        "fsdp",
        axis=0,
        tiled=True,
    )
    group_source = group[:, :source_len]
    group_target = group[:, source_len : source_len + target_len]
    lengths = group[:, -2:]

    def fullest(share):
        padded = jnp.pad(lengths, ((0, -number % share), (0, 0)))
        return jnp.max(jnp.sum(padded.reshape(-1, share, 2), axis=1), axis=0)

    needs = lax.all_gather(
        jnp.concatenate([jnp.sum(lengths, axis=0)] + [fullest(share) for share in shares_of]),
        "cuts",
        axis=0,
    )
    for step in range(steps):
        if step:
            vocab_shares, needs = spread_tied(vocab_shares, needs)
        vocab_shares = spread_step(vocab_shares, step)
    stored, needs = lax.optimization_barrier((stored, needs))
    first_columns = jnp.concatenate(gather_fsdp(stored[:12], fsdp_rank), axis=2)
    errors = jnp.transpose(error_blocks[0], (1, 2, 0))
    vocab_shares, first_columns = spread_tied(vocab_shares, first_columns)
    first_shares = spread_begin(first_columns)
    first_shares = spread_step(first_shares, 0) if steps else first_shares
    vocab_pieces = spread_end(vocab_shares)
    piece_arrays = [[array for _, array in held] for _, held in vocab_pieces]
    first_arrays = [array for _, array in first_shares]
    given = (group, needs, piece_arrays, first_arrays, stored[12:], errors)

    def one_round(state):
        _, turn, _, _, left_blocks, left_embed, gains_sum, table_sum, loss_sum = state
        turn, group, needs, piece_arrays, first_arrays, stored_rest, errors = (
            lax.optimization_barrier((turn, *given))
        )
        group_source = group[:, :source_len]
        group_target = group[:, source_len : source_len + target_len]
        lengths = group[:, -2:]
        total_count = jnp.sum(needs[:, 1]).astype(jnp.float32)
        most = jnp.max(needs[:, 2:], axis=0)
        share = jnp.int32(shares_of[-1])
        for index in range(len(shares_of) - 2, -1, -1):
            fits = (most[2 * index] <= room_source) & (most[2 * index + 1] <= room_target)
            share = jnp.where(fits, shares_of[index], share)
        members = jnp.arange(number, dtype=jnp.int32)
        taken = (members >= turn * share) & (members < (turn + 1) * share)
        source_taken = jnp.where(taken, lengths[:, 0], 0)
        target_taken = jnp.where(taken, lengths[:, 1], 0)
        more = (turn + 1) * share < number

        chosen = jnp.sum(
            jnp.where(
                task_ids[:, None] == jnp.arange(TASKS, dtype=jnp.int32)[None, :],
                task_counts[None, :],
                0,
            ),
            axis=1,
        ).astype(jnp.float32)
        slice_weight = jnp.sum(
            jnp.where(
                jnp.arange(cuts_count, dtype=jnp.int32) == cuts_rank,
                cuts_count * chosen / jnp.sum(chosen),
                0.0,
            )
        )

        pieces = [
            (first, [(bits, array) for (bits, _), array in zip(held, own)])
            for (first, held), own in zip(vocab_pieces, piece_arrays)
        ]
        (vocab,) = place_pieces(pieces, ((tuple(range(bands)), "mixed"),), cuts_rank)
        shares = [(bits, array) for (bits, _), array in zip(first_shares, first_arrays)]
        rest_parts = [stored_rest] + [
            shifted(stored_rest, distance) for distance in range(1, lax.axis_size("fsdp"))
        ]
        for step in range(1, steps):
            shares = spread_step(shares, step)

        def attention_groups(first):
            return (
                ((first,), "columns"),
                ((first + 1, first + 2), "columns"),
                ((first + 3,), "columns"),
            )

        def feed_groups(first):
            return (
                (tuple(range(first, first + 4)), "columns"),
                (tuple(range(first + 4, first + 8)), "rows"),
            )

        source_segment, source_place, source_starts, source_ends = packing(source_taken, room_source)
        target_segment, target_place, target_starts, target_ends = packing(target_taken, room_target)
        source_real = source_segment < number
        target_real = target_segment < number
        packed_source = jnp.take(
            group_source.reshape(-1),
            jnp.where(source_real, source_segment * source_len + source_place, 0),
        )
        group_input = jnp.concatenate(
            [jnp.zeros_like(group_target[:, :1]), group_target[:, :-1]], axis=1
        )
        target_from = jnp.where(target_real, target_segment * target_len + target_place, 0)
        packed_target = jnp.take(group_target.reshape(-1), target_from)
        packed_input = jnp.take(group_input.reshape(-1), target_from)
        packed_ids = jnp.concatenate([packed_source, packed_input])
        packed_real = jnp.concatenate([source_real, target_real])
        vocab_places = jnp.arange(vocab_rows, dtype=jnp.int32)
        local_ids = jnp.where(packed_real, packed_ids - vocab_start, -1)
        source_total, target_total = jnp.sum(source_taken), jnp.sum(target_taken)
        chunk = 2 * TILE
        local_ids = jnp.pad(local_ids, (0, -local_ids.shape[0] % chunk), constant_values=-1)
        spans = jnp.stack(
            [
                jnp.minimum((source_total + chunk - 1) // chunk, room_source // chunk),
                jnp.int32(room_source // chunk),
                jnp.minimum(
                    (room_source + target_total + chunk - 1) // chunk,
                    local_ids.shape[0] // chunk,
                ),
            ]
        )
        rows = lookup_rows(local_ids, spans, vocab)
        shares, rows = spread_tied(shares, rows)
        first_placed = place_pieces(
            spread_end(shares), attention_groups(0) + feed_groups(4), cuts_rank
        )
        sizes = [room_source * part // 5 for part in (2, 3, 4, 5)]
        fullest_source = jnp.int32(room_source)
        for index in range(len(shares_of) - 1, -1, -1):
            fullest_source = jnp.where(share == shares_of[index], most[2 * index], fullest_source)
        source_rows = lax.switch(
            sum((fullest_source > size).astype(jnp.int32) for size in sizes[:-1]),
            [
                lambda table, size=size: jnp.pad(
                    lax.psum(table[:size], "fsdp"), ((0, room_source - size), (0, 0))
                )
                for size in sizes
            ],
            rows[:room_source],
        )
        source_rows, target_rows, table, rest_parts = lax.optimization_barrier(
            (source_rows, rows[room_source : room_source + room_target], position_bias, rest_parts)
        )
        rest_columns = jnp.concatenate(in_order(rest_parts, fsdp_rank), axis=2)
        rest_shares, first_placed = spread_tied(spread_begin(rest_columns), first_placed)
        for step in range(steps):
            rest_shares = spread_step(rest_shares, step)
        rest_pieces = spread_end(rest_shares)
        rest_attention = place_pieces(
            rest_pieces, attention_groups(0) + attention_groups(4), cuts_rank
        )
        rest_feed = place_pieces(rest_pieces, feed_groups(8), cuts_rank)
        weights = (
            first_placed[:3],
            first_placed[3:],
            rest_attention[:3],
            rest_attention[3:],
            rest_feed,
        )
        target_rows = lax.psum(target_rows, "fsdp")
        source_stream = source_rows.astype(jnp.float32)
        target_stream = target_rows
        layout = (
            key_span(source_segment, source_total, source_starts, source_ends),
            key_span(target_segment, target_total, target_starts, target_ends),
            key_span(target_segment, target_total, source_starts, source_ends),
            source_segment[None, :],
            source_segment[:, None],
            target_segment[None, :],
            target_segment[:, None],
        )

        token_mask = target_real.astype(jnp.float32)
        token_weight = token_mask * (slice_weight / total_count)
        target_hit = vocab_places[None, :] == (packed_target - vocab_start)[:, None]

        def head(final_rows):
            logits = dot(final_rows, vocab)
            highest = jnp.max(logits, axis=1)
            total_exp = jnp.sum(jnp.exp(logits - highest[:, None]), axis=1)
            picked = jnp.sum(jnp.where(target_hit, logits, 0.0), axis=1)
            stats = lax.all_gather(jnp.stack([highest, total_exp, picked]), "fsdp", axis=0)
            top = jnp.max(stats[:, 0], axis=0)
            log_total = top + jnp.log(
                jnp.sum(stats[:, 1] * jnp.exp(stats[:, 0] - top[None, :]), axis=0)
            )
            token_loss = (log_total - jnp.sum(stats[:, 2], axis=0)) * token_mask
            grad_logits = (
                (jnp.exp(logits - log_total[:, None]) - target_hit.astype(jnp.float32))
                * token_weight[:, None]
            ).astype(jnp.bfloat16)
            grad_rows = sum_fsdp(dot_nt(grad_logits, vocab), fsdp_rank)
            return grad_rows, grad_logits, token_loss

        shares, gains, table_found, source_grad, target_grad, final_rows, grad_logits, token_loss = (
            packed_gradients(
                source_stream,
                target_stream,
                gain_rows,
                table,
                weights,
                layout,
                head,
                fsdp_rank * blocks.shape[2],
                blocks.shape[2],
            )
        )
        lookups = jnp.concatenate([source_grad, target_grad]).astype(jnp.bfloat16)
        lookups = jnp.pad(lookups, ((0, local_ids.shape[0] - lookups.shape[0]), (0, 0)))
        left_embed = vocab_grad(
            error_embed[0], left_embed, turn, local_ids, spans, lookups, grad_logits, final_rows
        )
        before = jnp.where(turn == 0, errors, left_blocks)
        return (
            more,
            turn + 1,
            total_count,
            slice_weight,
            before + shares,
            left_embed,
            gains_sum + gains,
            table_sum + table_found,
            loss_sum + jnp.sum(token_loss),
        )

    zero = jnp.zeros((), jnp.float32)
    _, _, total_count, slice_weight, left_blocks, left_embed, gains_grad, table_grad, loss_local = (
        lax.while_loop(
            lambda state: state[0],
            one_round,
            (
                jnp.ones((), jnp.bool_),
                jnp.zeros((), jnp.int32),
                zero,
                zero,
                unset((blocks.shape[1], blocks.shape[2], MODEL_WIDTH)),
                unset((vocab_rows, MODEL_WIDTH)),
                jnp.zeros_like(gain_rows),
                jnp.zeros_like(position_bias),
                zero,
            ),
        )
    )

    left_factor = jnp.einsum("kji,kjr->rki", left_blocks, right_blocks, precision=lax.Precision.HIGH)
    embed_factor = jnp.einsum("vd,vr->rd", left_embed, right_embed, precision=lax.Precision.HIGH)
    rank, count = left_factor.shape[:2]
    small = jnp.concatenate(
        [
            gains_grad * once,
            (table_grad * once).reshape(-1, MODEL_WIDTH),
            jnp.full((1, MODEL_WIDTH), loss_local * slice_weight * once),
        ]
    )
    factor = jnp.concatenate([left_factor, embed_factor[:, None]], axis=1)
    packed = jnp.concatenate([factor.reshape(-1, MODEL_WIDTH), small])
    packed = jnp.pad(packed, ((0, -packed.shape[0] % (8 * cuts_count)), (0, 0)))
    packed = sum_everywhere(packed, cuts_rank)
    factor = packed[: rank * (count + 1)].reshape(factor.shape)
    small = packed[rank * (count + 1) :]
    gains_grad = small[: gain_rows.shape[0]]
    table_rows = position_bias.size // MODEL_WIDTH
    table_grad = small[gain_rows.shape[0] :][:table_rows].reshape(position_bias.shape)
    loss_total = small[gain_rows.shape[0] + table_rows, 0]
    factor = orthonormal_rows(factor)
    left_factor, embed_factor = factor[:, :-1], factor[:, -1]
    factors_blocks = jnp.einsum("kji,rki->rkj", left_blocks, left_factor, precision=lax.Precision.HIGH)
    factors_embed = jnp.einsum("vd,rd->rv", left_embed, embed_factor, precision=lax.Precision.HIGH)
    both = sum_cuts(jnp.concatenate([factors_blocks.reshape(rank, -1), factors_embed], axis=1))
    factors_embed = both[:, -vocab_rows:]
    factors_blocks = both[:, :-vocab_rows].reshape(factors_blocks.shape)
    gram_blocks = jnp.einsum("rki,ski->krs", left_factor, left_factor, precision=TOP_PRECISION)
    gram_embed = jnp.einsum("rd,sd->rs", embed_factor, embed_factor, precision=TOP_PRECISION)
    squares = jnp.sum(
        factors_blocks
        * jnp.einsum("krs,skj->rkj", gram_blocks, factors_blocks, precision=lax.Precision.HIGH)
    ) + jnp.sum(factors_embed * jnp.dot(gram_embed, factors_embed, precision=lax.Precision.HIGH))
    squares = lax.psum(squares, "fsdp")
    full_blocks = jnp.einsum("rki,rkj->kji", left_factor, factors_blocks, precision=lax.Precision.HIGH)
    full_embed = jnp.einsum("rv,rd->vd", factors_embed, embed_factor, precision=lax.Precision.HIGH)
    owned_rows = blocks.shape[0]
    owned_columns = embedding.shape[1]
    own_left = lax.dynamic_slice_in_dim(left_factor, cuts_rank * owned_rows, owned_rows, 2)
    own_right = lax.dynamic_slice_in_dim(embed_factor, cuts_rank * owned_columns, owned_columns, 1)
    own_blocks = jnp.einsum("rki,rkj->ikj", own_left, factors_blocks, precision=lax.Precision.HIGH)
    own_embed = jnp.einsum("rv,rd->vd", factors_embed, own_right, precision=lax.Precision.HIGH)
    small_squares = jnp.sum(gains_grad * gains_grad) + jnp.sum(table_grad * table_grad)
    grad_norm = jnp.sqrt(squares + small_squares)
    clip_factor = jnp.minimum(1.0, CLIP_NORM / grad_norm)
    step_size = STEP_RATE * math.sqrt(PARAMS / MODEL_WIDTH) / CLIP_NORM
    embed_step = step_size * EMBED_SHARE * math.sqrt(MODEL_WIDTH)
    small_step = step_size * SMALL_SHARE * math.sqrt(MODEL_WIDTH)
    momentum_blocks = MOMENTUM_DECAY * blocks_momentum + (1.0 - MOMENTUM_DECAY) * (
        clip_factor * own_blocks
    )
    momentum_embed = MOMENTUM_DECAY * embed_momentum + (1.0 - MOMENTUM_DECAY) * (
        clip_factor * own_embed
    )
    momentum_gains = MOMENTUM_DECAY * gain_momentum + (1.0 - MOMENTUM_DECAY) * (
        clip_factor * gains_grad
    )
    momentum_bias = MOMENTUM_DECAY * bias_momentum + (1.0 - MOMENTUM_DECAY) * (
        clip_factor * table_grad
    )
    return (
        loss_total,
        total_count,
        grad_norm,
        blocks - step_size * momentum_blocks,
        momentum_blocks,
        embedding - embed_step * momentum_embed,
        momentum_embed,
        gain_rows - small_step * momentum_gains,
        momentum_gains,
        position_bias - small_step * momentum_bias,
        momentum_bias,
        jnp.transpose(factors_blocks, (1, 2, 0)),
        factors_embed.T,
        jnp.transpose(left_blocks - full_blocks, (2, 0, 1))[None],
        (left_embed - full_embed)[None],
    )


def solution(mesh):
    return jax.shard_map(
        local,
        mesh=mesh,
        in_specs=(
            P(("cuts", "fsdp"), None),
            P(("cuts", "fsdp"), None),
            P(("cuts", "fsdp")),
            P(("cuts", "fsdp")),
            P(),
            P(),
            P("cuts", None, "fsdp"),
            P("cuts", None, "fsdp"),
            P("fsdp", "cuts"),
            P("fsdp", "cuts"),
            P(),
            P(),
            P(),
            P(),
            P(None, "fsdp", None),
            P("fsdp", None),
            P("cuts", None, None, "fsdp"),
            P("cuts", "fsdp", None),
        ),
        out_specs=(
            P(),
            P(),
            P(),
            P("cuts", None, "fsdp"),
            P("cuts", None, "fsdp"),
            P("fsdp", "cuts"),
            P("fsdp", "cuts"),
            P(),
            P(),
            P(),
            P(),
            P(None, "fsdp", None),
            P("fsdp", None),
            P("cuts", None, None, "fsdp"),
            P("cuts", "fsdp", None),
        ),
        check_vma=False,
    )
```

```python
import itertools
import math

import jax
import jax.numpy as jnp
from jax import lax
from jax.experimental import pallas as pl
from jax.experimental.layout import Layout, with_layout_constraint
from jax.experimental.pallas import tpu as pltpu
from jax.sharding import PartitionSpec as P

MODEL_WIDTH = 768
H = 12
DH = 64
FEED_UNITS = 3072
NBK = 32
TASKS = 8
PARAMS = 41189376


EPSILON = 1e-06
MASKED = -1000000000.0
CLIP_NORM = 0.05
MOMENTUM_DECAY = 0.9
STEP_RATE = 5.0
EMBED_SHARE = 50.0
SMALL_SHARE = 1.0 / 7.0
TOP_PRECISION = lax.Precision.HIGHEST
TILE = 128
ROOM_SOURCE = 1280
ROOM_TARGET = 384
ENCODER_EDGES = (12, 16, 23, 32, 46, 64, 91)
DECODER_EDGES = (19, 21, 24, 27, 31, 35, 40, 46, 52, 59, 67, 77, 87, 99, 113)


def root_norm(stream, gain_row):
    return (
        stream * lax.rsqrt(jnp.mean(stream * stream, axis=-1, keepdims=True) + EPSILON) * gain_row
    )


def norm_backward(stream, gain_row, grad_normed):
    _, pull_back = jax.vjp(root_norm, stream, gain_row)
    return pull_back(grad_normed)


def dot(left, right):
    return jnp.dot(left, right, preferred_element_type=jnp.float32)


def dot_nt(left, right):
    return lax.dot_general(left, right, (((1,), (1,)), ((), ())), preferred_element_type=jnp.float32)


def dot_tn(left, right):
    return lax.dot_general(left, right, (((0,), (0,)), ((), ())), preferred_element_type=jnp.float32)


def exchange(array, mask):
    return lax.ppermute(array, "cuts", [(i, i ^ mask) for i in range(lax.axis_size("cuts"))])


def shifted(array, distance):
    count = lax.axis_size("fsdp")
    return lax.ppermute(array, "fsdp", [(i, (i + distance) % count) for i in range(count)])


def in_order(pieces, rank):
    count = len(pieces)
    ordered = []
    for place in range(count):
        chosen = pieces[-place % count]
        for own in range(1, count):
            chosen = jnp.where(rank == own, pieces[(own - place) % count], chosen)
        ordered.append(chosen)
    return ordered


def gather_fsdp(part, rank):
    count = lax.axis_size("fsdp")
    return in_order([part] + [shifted(part, distance) for distance in range(1, count)], rank)


def sum_fsdp(part, rank):
    count = lax.axis_size("fsdp")
    rows = part.shape[0] // count
    low = part.astype(jnp.bfloat16)
    total = lax.dynamic_slice_in_dim(part, rank * rows, rows, 0)
    for distance in range(1, count):
        piece = lax.dynamic_slice_in_dim(low, (rank + distance) % count * rows, rows, 0)
        total = total + shifted(piece, distance).astype(jnp.float32)
    return jnp.concatenate(gather_fsdp(total.astype(jnp.bfloat16), rank), axis=0).astype(jnp.float32)


def sum_everywhere(part, cuts_rank):
    count = lax.axis_size("cuts")
    masks = [1 << bit for bit in range(count.bit_length() - 1)]
    if count & (count - 1) or part.shape[0] % count:
        return lax.psum(part, ("cuts", "fsdp"))
    bits = [(cuts_rank // mask) % 2 for mask in masks]
    for mask, bit in zip(masks, bits):
        half = part.shape[0] // 2
        away = lax.dynamic_slice_in_dim(part, (1 - bit) * half, half, 0)
        part = lax.dynamic_slice_in_dim(part, bit * half, half, 0) + exchange(away, mask)
    part = jnp.sum(lax.all_gather(part, "fsdp", axis=0), axis=0)
    for mask, bit in zip(masks[::-1], bits[::-1]):
        other = exchange(part, mask)
        part = jnp.where(
            bit == 1, jnp.concatenate([other, part], axis=0), jnp.concatenate([part, other], axis=0)
        )
    return part


def sum_cuts(part):
    count = lax.axis_size("cuts")
    if count & (count - 1):
        return lax.psum(part.astype(jnp.bfloat16), "cuts").astype(jnp.float32)
    for bit in range(count.bit_length() - 1):
        low = part.astype(jnp.bfloat16)
        part = low.astype(jnp.float32) + exchange(low, 1 << bit).astype(jnp.float32)
    return part


def spread_ways():
    return [1 << bit for bit in range(1, lax.axis_size("cuts").bit_length() - 1)]


def spread_begin(part):
    number = max(min(len(spread_ways()), part.shape[0]), 1)
    ends = [part.shape[0] * turn // number for turn in range(number + 1)]
    return [([0], part[None, begin:end]) for begin, end in zip(ends, ends[1:])]


def spread_step(shares, step):
    ways = spread_ways()
    after = []
    for turn, (bits, held) in enumerate(shares):
        mask = ways[(turn + step) % len(ways)]
        after.append(
            (bits + [bit ^ mask for bit in bits], jnp.concatenate([held, exchange(held, mask)]))
        )
    return after


def spread_end(shares):
    found, first = [], 0
    for bits, held in shares:
        found.append((first, [(bits, held), ([bit ^ 1 for bit in bits], exchange(held, 1))]))
        first += held.shape[1]
    return found


def spread_tied(shares, *others):
    arrays, others = lax.optimization_barrier(([held for _, held in shares], others))
    return [(bits, held) for (bits, _), held in zip(shares, arrays)], *others


def cost(flops, moved, powers=0):
    return pl.CostEstimate(flops=int(flops), bytes_accessed=int(moved), transcendentals=int(powers))


def place_kernel(moves, number, rank_ref, *refs):
    sources, outs, sem = refs[:number], refs[number:-1], refs[-1]
    rank = rank_ref[0]
    copies = []
    for source, piece, index, bits, (out, pitch, row, column), shape in moves:
        rows = pl.ds(pl.multiple_of((rank ^ bits) * pitch + row, 16), shape[0])
        copies.append(
            pltpu.make_async_copy(
                sources[source].at[piece, index],
                outs[out].at[rows, pl.ds(column, shape[1])],
                sem.at[len(copies)],
            )
        )
    for copy in copies:
        copy.start()
    for copy in copies:
        copy.wait()


def place_pieces(found, groups, rank):
    count = lax.axis_size("cuts")
    height, width = found[0][1][0][1].shape[2:]
    where = {}
    shapes = []
    for out, (members, how) in enumerate(groups):
        for order, matrix in enumerate(members):
            row = {"columns": 0, "rows": order * count * height, "mixed": order * height}[how]
            pitch = height * (len(members) if how == "mixed" else 1)
            where[matrix] = (out, pitch, row, order * width if how == "columns" else 0)
        tall, wide = (1, len(members)) if how == "columns" else (len(members), 1)
        shapes.append((tall * count * height, wide * width))
    sources, moves = [], []
    for first, held in found:
        for bits, array in held:
            for piece, index in itertools.product(range(array.shape[0]), range(array.shape[1])):
                if first + index in where:
                    moves.append(
                        (len(sources), piece, index, bits[piece], where[first + index], (height, width))
                    )
            sources.append(array)
    space = pl.BlockSpec(memory_space=pl.ANY)
    return pl.pallas_call(
        lambda *refs: place_kernel(moves, len(sources), *refs),
        in_specs=[pl.BlockSpec(memory_space=pltpu.SMEM)] + [space] * len(sources),
        out_specs=[pl.BlockSpec(memory_space=pltpu.VMEM)] * len(shapes),
        out_shape=[jax.ShapeDtypeStruct(shape, sources[0].dtype) for shape in shapes],
        scratch_shapes=[pltpu.SemaphoreType.DMA((len(moves),))],
        compiler_params=pltpu.CompilerParams(vmem_limit_bytes=40 << 20),
        cost_estimate=cost(0, 5 * sum(math.prod(shape) for shape in shapes)),
        name="place",
    )(rank[None], *sources)


def unset_kernel(out_ref):
    pass


def unset(shape):
    return pl.pallas_call(
        unset_kernel,
        out_specs=pl.BlockSpec(memory_space=pl.ANY),
        out_shape=jax.ShapeDtypeStruct(shape, jnp.float32),
        name="unset",
    )()


PAIRS = H // 2
WIDE = 2 * TILE


def offset_buckets(causal, offset):
    if causal:
        distance = jnp.maximum(-offset, 0)
        farther = 16 + sum(((distance >= boundary).astype(jnp.int32) for boundary in DECODER_EDGES))
        bucket = jnp.where(distance < 16, distance, farther)
    else:
        distance = jnp.abs(offset)
        farther = 8 + sum(((distance >= boundary).astype(jnp.int32) for boundary in ENCODER_EDGES))
        bucket = jnp.where(distance < 8, distance, farther) + jnp.where(offset > 0, 16, 0)
    return (bucket[..., None] == jnp.arange(NBK, dtype=jnp.int32)).astype(jnp.float32)


def bias_kernel(row_ref, out_ref):
    for head in range(H):
        row = jnp.broadcast_to(row_ref[0, head : head + 1, :], (TILE, WIDE))
        tile = pltpu.roll(row, 0, 1, stride=1, stride_axis=0)[:, :TILE]
        out_ref[0, head // 2, :, (head % 2) * TILE : (head % 2 + 1) * TILE] = tile


def bias_tiles(causal, table):
    lane = jnp.arange(WIDE, dtype=jnp.int32)
    offset = (jnp.arange(5, dtype=jnp.int32)[:, None] - 2) * TILE + jnp.where(
        lane < TILE, -lane, WIDE - lane
    )
    rows = jnp.einsum(
        "tqb,bh->thq", offset_buckets(causal, offset), table, precision=TOP_PRECISION
    )
    return pl.pallas_call(
        bias_kernel,
        grid=(5,),
        in_specs=[pl.BlockSpec((1, 16, WIDE), lambda i: (i, 0, 0))],
        out_specs=pl.BlockSpec((1, PAIRS, TILE, WIDE), lambda i: (i, 0, 0, 0)),
        out_shape=jax.ShapeDtypeStruct((5, PAIRS, TILE, WIDE), jnp.float32),
        name="bias",
    )(jnp.pad(rows, ((0, 0), (0, 16 - H), (0, 0))))


def bias_grad(tiles, causal):
    places = jnp.arange(TILE, dtype=jnp.int32)
    offset = (
        (jnp.arange(5, dtype=jnp.int32)[:, None, None] - 2) * TILE
        + places[None, :, None]
        - places[None, None, :]
    )
    hot = offset_buckets(causal, offset)
    found = [
        jnp.einsum("tpkq,tkqb->bp", tiles[..., half], hot, precision=lax.Precision.HIGH)
        for half in (slice(0, TILE), slice(TILE, WIDE))
    ]
    return jnp.stack(found, axis=-1).reshape(NBK, H)


def stack_heads(pair):
    half = lax.broadcasted_iota(jnp.int32, (TILE, TILE), 1) // DH
    return jnp.concatenate(
        [jnp.where(half == which, pair, jnp.zeros_like(pair)) for which in range(2)], axis=0
    )


def own_features(wide):
    return jnp.concatenate([wide[:DH, :TILE], wide[DH:, TILE:]], axis=0)


def kept(segment_column, segment_row, key_tile, query_tile, causal):
    keep = segment_column == jnp.concatenate([segment_row, segment_row], axis=1)
    if causal:
        key_place = key_tile * TILE + lax.broadcasted_iota(jnp.int32, (TILE, WIDE), 0)
        query_place = query_tile * TILE + lax.broadcasted_iota(jnp.int32, (TILE, WIDE), 1) % TILE
        keep = keep & (key_place <= query_place)
    return keep


def tile_scores(keys, queries, keep, bias):
    scores = dot_nt(keys, queries)
    if bias is not None:
        scores = scores + bias
    return jnp.where(keep, scores, MASKED)


def forward_kernel(
    causal, biased, first_ref, last_ref, q_ref, k_ref, v_ref, row_ref, column_ref, *rest
):
    bias_ref = rest[0] if biased else None
    out_ref, level_ref, stack_ref, top_ref, sum_ref, total_ref = rest[1:] if biased else rest
    here = pl.program_id(0)
    top_ref[...] = jnp.full_like(top_ref, -1e30)
    sum_ref[...] = jnp.zeros_like(sum_ref)
    total_ref[...] = jnp.zeros_like(total_ref)
    segment_row = row_ref[...]
    for pair in range(PAIRS):
        stack_ref[pair] = stack_heads(q_ref[:, pair * TILE : (pair + 1) * TILE])

    def step(there, carry):
        rows = pl.ds(pl.multiple_of(there * TILE, TILE), TILE)
        keep = kept(column_ref[rows, :], segment_row, there, here, causal)
        offset = jnp.clip(there - here, -2, 2) + 2
        before, sums = top_ref[...], sum_ref[...]
        tops, sums_after = [], []
        for pair in range(PAIRS):
            lanes = slice(pair * TILE, (pair + 1) * TILE)
            scores = tile_scores(
                k_ref[rows, lanes], stack_ref[pair], keep, bias_ref[offset, pair] if biased else None
            )
            old = before[pair : pair + 1, :]
            top = jnp.maximum(old, jnp.max(scores, axis=0, keepdims=True))
            weights = jnp.exp(scores - top)
            scale = jnp.exp(old - top)
            tops.append(top)
            sums_after.append(
                sums[pair : pair + 1, :] * scale + jnp.sum(weights, axis=0, keepdims=True)
            )
            total_ref[pair] = total_ref[pair] * scale + dot(
                v_ref[rows, lanes].T, weights.astype(jnp.bfloat16)
            )
        for pair in range(PAIRS):
            top_ref[pair : pair + 1, :] = tops[pair]
            sum_ref[pair : pair + 1, :] = sums_after[pair]
        return carry

    lax.fori_loop(first_ref[here], last_ref[here], step, 0)
    seen = sum_ref[...] > 0.0
    divisor = jnp.where(seen, sum_ref[...], 1.0)
    level_ref[...] = jnp.where(seen, top_ref[...] + jnp.log(divisor), 0.0)
    for pair in range(PAIRS):
        lanes = slice(pair * TILE, (pair + 1) * TILE)
        wide = total_ref[pair] / divisor[pair : pair + 1, :]
        out_ref[:, lanes] = own_features(wide).T.astype(jnp.bfloat16)


def backward_kernel(
    causal, biased, first_ref, last_ref, q_ref, o_ref, k_ref, v_ref, level_ref, row_ref, column_ref, *rest
):
    bias_ref = rest[0] if biased else None
    rest = rest[1:] if biased else rest
    gq_ref, gkv_ref = rest[:2]
    gb_ref = rest[2] if biased else None
    weight_ref, slope_ref, mean_ref, stack_ref, arrive_ref, tq_ref, tk_ref, tv_ref = rest[-8:]
    here = pl.program_id(0)

    @pl.when(here == 0)
    def _():
        tk_ref[...] = jnp.zeros_like(tk_ref)
        tv_ref[...] = jnp.zeros_like(tv_ref)
        if biased:
            gb_ref[...] = jnp.zeros_like(gb_ref)

    mean_ref[...] = jnp.zeros_like(mean_ref)
    tq_ref[...] = jnp.zeros_like(tq_ref)
    segment_row = row_ref[...]
    first = first_ref[here]
    last = last_ref[here]
    for pair in range(PAIRS):
        lanes = slice(pair * TILE, (pair + 1) * TILE)
        stack_ref[pair] = stack_heads(q_ref[:, lanes])
        arrive_ref[pair] = stack_heads(o_ref[:, lanes])

    def look(there, carry):
        rows = pl.ds(pl.multiple_of(there * TILE, TILE), TILE)
        keep = kept(column_ref[rows, :], segment_row, there, here, causal)
        offset = jnp.clip(there - here, -2, 2) + 2
        means = mean_ref[...]
        sums = []
        for pair in range(PAIRS):
            lanes = slice(pair * TILE, (pair + 1) * TILE)
            scores = tile_scores(
                k_ref[rows, lanes], stack_ref[pair], keep, bias_ref[offset, pair] if biased else None
            )
            weights = jnp.exp(scores - level_ref[pair : pair + 1, :])
            slopes = dot_nt(v_ref[rows, lanes], arrive_ref[pair])
            sums.append(
                means[pair : pair + 1, :] + jnp.sum(weights * slopes, axis=0, keepdims=True)
            )
            weight_ref[there - first, pair] = weights
            slope_ref[there - first, pair] = slopes
            tv_ref[rows, lanes] = tv_ref[rows, lanes] + dot(
                weights.astype(jnp.bfloat16), arrive_ref[pair]
            )
        for pair in range(PAIRS):
            mean_ref[pair : pair + 1, :] = sums[pair]
        return carry

    def push(there, carry):
        rows = pl.ds(pl.multiple_of(there * TILE, TILE), TILE)
        offset = jnp.clip(there - here, -2, 2) + 2
        for pair in range(PAIRS):
            lanes = slice(pair * TILE, (pair + 1) * TILE)
            slopes = (
                weight_ref[there - first, pair]
                * (slope_ref[there - first, pair] - mean_ref[pair : pair + 1, :])
            ).astype(jnp.bfloat16)
            if biased:
                gb_ref[offset, pair] = gb_ref[offset, pair] + slopes.astype(jnp.float32)
            tq_ref[pair] = tq_ref[pair] + dot(k_ref[rows, lanes].T, slopes)
            tk_ref[rows, lanes] = tk_ref[rows, lanes] + dot(slopes, stack_ref[pair])
        return carry

    lax.fori_loop(first, last, look, 0)
    lax.fori_loop(first, last, push, 0)
    for pair in range(PAIRS):
        lanes = slice(pair * TILE, (pair + 1) * TILE)
        gq_ref[:, lanes] = own_features(tq_ref[pair]).T.astype(jnp.bfloat16)

    @pl.when(here == pl.num_programs(0) - 1)
    def _():
        gkv_ref[:, :MODEL_WIDTH] = tk_ref[...].astype(jnp.bfloat16)
        gkv_ref[:, MODEL_WIDTH:] = tv_ref[...].astype(jnp.bfloat16)


def whole_block(shape):
    return pl.BlockSpec(shape, lambda i, *_: (0,) * len(shape))


def column_block(rows, index):
    return pl.BlockSpec((rows, MODEL_WIDTH), lambda i, *_: (0, index))


def packed_forward(queries, pair_rows, span, segment_row, segment_column, causal, bias):
    count, other = queries.shape[0], pair_rows.shape[0]
    biased = bias is not None
    tile = pl.BlockSpec((TILE, MODEL_WIDTH), lambda i, *_: (i, 0))
    return pl.pallas_call(
        lambda *refs: forward_kernel(causal, biased, *refs),
        grid_spec=pltpu.PrefetchScalarGridSpec(
            num_scalar_prefetch=2,
            grid=(count // TILE,),
            in_specs=[
                tile,
                column_block(other, 0),
                column_block(other, 1),
                pl.BlockSpec((1, TILE), lambda i, *_: (0, i)),
                whole_block((other, 1)),
            ]
            + ([whole_block((5, PAIRS, TILE, WIDE))] if biased else []),
            out_specs=[tile, pl.BlockSpec((8, WIDE), lambda i, *_: (0, i))],
            scratch_shapes=[
                pltpu.VMEM((PAIRS, WIDE, TILE), jnp.bfloat16),
                pltpu.VMEM((8, WIDE), jnp.float32),
                pltpu.VMEM((8, WIDE), jnp.float32),
                pltpu.VMEM((PAIRS, TILE, WIDE), jnp.float32),
            ],
        ),
        out_shape=[
            jax.ShapeDtypeStruct((count, MODEL_WIDTH), jnp.bfloat16),
            jax.ShapeDtypeStruct((8, 2 * count), jnp.float32),
        ],
        compiler_params=pltpu.CompilerParams(vmem_limit_bytes=40 << 20),
        cost_estimate=cost(8 * count * other * MODEL_WIDTH, 20 << 20),
        name="attend",
    )(*span, queries, pair_rows, pair_rows, segment_row, segment_column, *([bias] if biased else []))


def packed_backward(
    queries, grad_out, pair_rows, levels, span, segment_row, segment_column, causal, bias
):
    count, other = queries.shape[0], pair_rows.shape[0]
    biased = bias is not None
    reach = min(other // TILE, 9) if biased else other // TILE
    tile = pl.BlockSpec((TILE, MODEL_WIDTH), lambda i, *_: (i, 0))
    table = (5, PAIRS, TILE, WIDE)
    return pl.pallas_call(
        lambda *refs: backward_kernel(causal, biased, *refs),
        grid_spec=pltpu.PrefetchScalarGridSpec(
            num_scalar_prefetch=2,
            grid=(count // TILE,),
            in_specs=[
                tile,
                tile,
                column_block(other, 0),
                column_block(other, 1),
                pl.BlockSpec((8, WIDE), lambda i, *_: (0, i)),
                pl.BlockSpec((1, TILE), lambda i, *_: (0, i)),
                whole_block((other, 1)),
            ]
            + ([whole_block(table)] if biased else []),
            out_specs=[tile, whole_block((other, 2 * MODEL_WIDTH))]
            + ([whole_block(table)] if biased else []),
            scratch_shapes=[
                pltpu.VMEM((reach, PAIRS, TILE, WIDE), jnp.float32),
                pltpu.VMEM((reach, PAIRS, TILE, WIDE), jnp.float32),
                pltpu.VMEM((8, WIDE), jnp.float32),
                pltpu.VMEM((PAIRS, WIDE, TILE), jnp.bfloat16),
                pltpu.VMEM((PAIRS, WIDE, TILE), jnp.bfloat16),
                pltpu.VMEM((PAIRS, TILE, WIDE), jnp.float32),
                pltpu.VMEM((other, MODEL_WIDTH), jnp.float32),
                pltpu.VMEM((other, MODEL_WIDTH), jnp.float32),
            ],
        ),
        out_shape=[
            jax.ShapeDtypeStruct((count, MODEL_WIDTH), jnp.bfloat16),
            jax.ShapeDtypeStruct((other, 2 * MODEL_WIDTH), jnp.bfloat16),
        ]
        + ([jax.ShapeDtypeStruct(table, jnp.float32)] if biased else []),
        compiler_params=pltpu.CompilerParams(vmem_limit_bytes=58 << 20),
        cost_estimate=cost(20 * count * other * MODEL_WIDTH, 40 << 20),
        name="attend_back",
    )(
        *span,
        queries,
        grad_out,
        pair_rows,
        pair_rows,
        levels,
        segment_row,
        segment_column,
        *([bias] if biased else []),
    )


def lookup_kernel(rows_in, blocks_ref, id_ref, vocab_ref, out_ref, total_ref):
    step = pl.program_id(0)
    width = vocab_ref.shape[1]
    chunk = 2 * TILE

    @pl.when(step == 0)
    def _():
        total_ref[...] = jnp.zeros_like(total_ref)

    inside = step * width + lax.broadcasted_iota(jnp.int32, (1, width), 1) < rows_in
    table = jnp.where(inside, vocab_ref[...], jnp.zeros_like(vocab_ref[...]))
    places = step * width + lax.broadcasted_iota(jnp.int32, (chunk, width), 1)

    def one(index, carry):
        rows = pl.ds(pl.multiple_of(index * chunk, chunk), chunk)
        hot = (id_ref[rows, :] == places).astype(jnp.bfloat16)
        total_ref[rows, :] = total_ref[rows, :] + dot_nt(hot, table)
        return carry

    lax.fori_loop(0, blocks_ref[0], one, 0)
    lax.fori_loop(blocks_ref[1], blocks_ref[2], one, 0)

    @pl.when(step == pl.num_programs(0) - 1)
    def _():
        out_ref[...] = total_ref[...].astype(jnp.bfloat16)


def lookup_rows(local_ids, spans, vocab):
    count, width = local_ids.shape[0], 4 * TILE
    rows_in = vocab.shape[1]
    return pl.pallas_call(
        lambda *refs: lookup_kernel(rows_in, *refs),
        grid_spec=pltpu.PrefetchScalarGridSpec(
            num_scalar_prefetch=1,
            grid=(pl.cdiv(rows_in, width),),
            in_specs=[
                whole_block((count, 1)),
                pl.BlockSpec((MODEL_WIDTH, width), lambda i, *_: (0, i)),
            ],
            out_specs=whole_block((count, MODEL_WIDTH)),
            scratch_shapes=[pltpu.VMEM((count, MODEL_WIDTH), jnp.float32)],
        ),
        out_shape=jax.ShapeDtypeStruct((count, MODEL_WIDTH), jnp.bfloat16),
        compiler_params=pltpu.CompilerParams(vmem_limit_bytes=40 << 20),
        cost_estimate=cost(2 * count * rows_in * MODEL_WIDTH, 90 << 20),
        name="lookup",
    )(spans, local_ids[:, None], vocab)


def vocab_grad_kernel(blocks_ref, id_ref, grad_ref, logit_ref, final_ref, start_ref, left_ref, out_ref):
    step = pl.program_id(0)
    width = left_ref.shape[0]
    chunk = 2 * TILE
    before = jnp.where(blocks_ref[3] == 0, start_ref[...], left_ref[...])
    out_ref[...] = before + dot_tn(logit_ref[...], final_ref[...])
    places = step * width + lax.broadcasted_iota(jnp.int32, (width, chunk), 0)

    def one(index, carry):
        rows = pl.ds(pl.multiple_of(index * chunk, chunk), chunk)
        hot = (places == id_ref[:, rows]).astype(jnp.bfloat16)
        out_ref[...] = out_ref[...] + dot(hot, grad_ref[rows, :])
        return carry

    lax.fori_loop(0, blocks_ref[0], one, 0)
    lax.fori_loop(blocks_ref[1], blocks_ref[2], one, 0)


def vocab_grad(start, left, turn, local_ids, spans, lookups, grad_logits, final_rows):
    count, width = local_ids.shape[0], 4 * TILE
    rows_in = left.shape[0]
    block = pl.BlockSpec((width, MODEL_WIDTH), lambda i, *_: (i, 0))
    return pl.pallas_call(
        vocab_grad_kernel,
        grid_spec=pltpu.PrefetchScalarGridSpec(
            num_scalar_prefetch=1,
            grid=(pl.cdiv(rows_in, width),),
            in_specs=[
                whole_block((1, count)),
                whole_block((count, MODEL_WIDTH)),
                pl.BlockSpec((grad_logits.shape[0], width), lambda i, *_: (0, i)),
                whole_block(final_rows.shape),
                pl.BlockSpec((width, MODEL_WIDTH), lambda i, s: (jnp.where(s[3] == 0, i, 0), 0)),
                pl.BlockSpec((width, MODEL_WIDTH), lambda i, s: (jnp.where(s[3] == 0, 0, i), 0)),
            ],
            out_specs=block,
        ),
        out_shape=jax.ShapeDtypeStruct(left.shape, jnp.float32),
        input_output_aliases={6: 0},
        compiler_params=pltpu.CompilerParams(vmem_limit_bytes=40 << 20),
        cost_estimate=cost(2 * (count + 384) * rows_in * MODEL_WIDTH, 100 << 20),
        name="vocab_grad",
    )(
        jnp.concatenate([spans, turn[None]]),
        local_ids[None, :],
        lookups,
        grad_logits,
        final_rows,
        start,
        left,
    )


def logit_places(step, rows_in, width):
    return step * width + lax.broadcasted_iota(jnp.int32, (TILE, width), 1)


def logit_kernel(rows_in, tiles_ref, row_ref, vocab_ref, id_ref, logit_ref, stat_ref, top_ref, sum_ref, hit_ref):
    step = pl.program_id(0)
    width = vocab_ref.shape[1]

    @pl.when(step == 0)
    def _():
        top_ref[...] = jnp.full_like(top_ref, -1e30)
        sum_ref[...] = jnp.zeros_like(sum_ref)
        hit_ref[...] = jnp.zeros_like(hit_ref)

    places = logit_places(step, rows_in, width)

    def one(index, carry):
        rows = pl.ds(pl.multiple_of(index * TILE, TILE), TILE)
        logits = dot(row_ref[rows, :], vocab_ref[...])
        logit_ref[rows, :] = logits
        inside = places < rows_in
        hits = jnp.where(inside & (places == id_ref[rows, :]), logits, 0.0)
        logits = jnp.where(inside, logits, -1e30)
        parts = [slice(begin, begin + TILE) for begin in range(0, width, TILE)]
        before = top_ref[rows, :]
        top = before
        for part in parts:
            top = jnp.maximum(top, logits[:, part])
        total = sum_ref[rows, :] * jnp.exp(before - top)
        hit = hit_ref[rows, :]
        for part in parts:
            total = total + jnp.exp(logits[:, part] - top)
            hit = hit + hits[:, part]
        top_ref[rows, :] = top
        sum_ref[rows, :] = total
        hit_ref[rows, :] = hit
        return carry

    lax.fori_loop(0, tiles_ref[0], one, 0)

    @pl.when(step == pl.num_programs(0) - 1)
    def _():
        top = jnp.max(top_ref[...], axis=1, keepdims=True)
        total = jnp.sum(sum_ref[...] * jnp.exp(top_ref[...] - top), axis=1, keepdims=True)
        hit = jnp.sum(hit_ref[...], axis=1, keepdims=True)
        lane = lax.broadcasted_iota(jnp.int32, stat_ref.shape, 1)
        seen = jnp.where(total > 0.0, total, 1.0)
        stat_ref[...] = jnp.where(lane == 0, top, jnp.where(lane == 1, seen, hit))


def logit_stats(final_rows, vocab, ids, tiles):
    count, rows_in, width = final_rows.shape[0], vocab.shape[1], 4 * TILE
    return pl.pallas_call(
        lambda *refs: logit_kernel(rows_in, *refs),
        grid_spec=pltpu.PrefetchScalarGridSpec(
            num_scalar_prefetch=1,
            grid=(pl.cdiv(rows_in, width),),
            in_specs=[
                whole_block((count, MODEL_WIDTH)),
                pl.BlockSpec((MODEL_WIDTH, width), lambda i, *_: (0, i)),
                whole_block((count, 1)),
            ],
            out_specs=[
                pl.BlockSpec((count, width), lambda i, *_: (0, i)),
                whole_block((count, TILE)),
            ],
            scratch_shapes=[pltpu.VMEM((count, TILE), jnp.float32)] * 3,
        ),
        out_shape=[
            jax.ShapeDtypeStruct((count, rows_in), jnp.float32),
            jax.ShapeDtypeStruct((count, TILE), jnp.float32),
        ],
        compiler_params=pltpu.CompilerParams(vmem_limit_bytes=40 << 20),
        cost_estimate=cost(2 * count * rows_in * MODEL_WIDTH, 40 << 20, count * rows_in),
        name="logits",
    )(tiles, final_rows, vocab, ids)


def logit_grad_kernel(
    rows_in, tiles_ref, logit_ref, vocab_ref, id_ref, level_ref, weight_ref, grad_ref, row_ref
):
    step = pl.program_id(0)
    width = vocab_ref.shape[1]

    @pl.when(step == 0)
    def _():
        row_ref[...] = jnp.zeros_like(row_ref)

    grad_ref[...] = jnp.zeros_like(grad_ref)
    places = logit_places(step, rows_in, width)
    inside = step * width + lax.broadcasted_iota(jnp.int32, (1, width), 1) < rows_in
    table = jnp.where(inside, vocab_ref[...], jnp.zeros_like(vocab_ref[...]))

    def one(index, carry):
        rows = pl.ds(pl.multiple_of(index * TILE, TILE), TILE)
        hit = (places == id_ref[rows, :]).astype(jnp.float32)
        grads = (jnp.exp(logit_ref[rows, :] - level_ref[rows, :]) - hit) * weight_ref[rows, :]
        grads = jnp.where(places < rows_in, grads, 0.0).astype(jnp.bfloat16)
        grad_ref[rows, :] = grads
        row_ref[rows, :] = row_ref[rows, :] + dot_nt(grads, table)
        return carry

    lax.fori_loop(0, tiles_ref[0], one, 0)


def logit_grads(logits, vocab, ids, tiles, levels, weights):
    count, rows_in = logits.shape
    width = 4 * TILE
    block = pl.BlockSpec((count, width), lambda i, *_: (0, i))
    return pl.pallas_call(
        lambda *refs: logit_grad_kernel(rows_in, *refs),
        grid_spec=pltpu.PrefetchScalarGridSpec(
            num_scalar_prefetch=1,
            grid=(pl.cdiv(rows_in, width),),
            in_specs=[
                block,
                pl.BlockSpec((MODEL_WIDTH, width), lambda i, *_: (0, i)),
                whole_block((count, 1)),
                whole_block((count, 1)),
                whole_block((count, 1)),
            ],
            out_specs=[block, whole_block((count, MODEL_WIDTH))],
        ),
        out_shape=[
            jax.ShapeDtypeStruct((count, rows_in), jnp.bfloat16),
            jax.ShapeDtypeStruct((count, MODEL_WIDTH), jnp.float32),
        ],
        compiler_params=pltpu.CompilerParams(vmem_limit_bytes=40 << 20),
        cost_estimate=cost(2 * count * rows_in * MODEL_WIDTH, 40 << 20, count * rows_in),
        name="logit_grads",
    )(tiles, logits, vocab, ids, levels[:, None], weights[:, None])


def packing(lengths, room):
    ends = jnp.cumsum(lengths)
    starts = ends - lengths
    places = jnp.arange(room, dtype=jnp.int32)
    segment = jnp.sum((places[:, None] >= ends[None, :]).astype(jnp.int32), axis=1)
    inside = segment[:, None] == jnp.arange(lengths.shape[0], dtype=jnp.int32)[None, :]
    position = places - jnp.sum(jnp.where(inside, starts[None, :], 0), axis=1)
    return segment, position, jnp.minimum(starts, room), jnp.minimum(ends, room)


def key_span(query_segment, query_total, key_starts, key_ends):
    number = key_starts.shape[0]
    count = query_segment.shape[0] // TILE
    begins = jnp.arange(count, dtype=jnp.int32) * TILE
    last_real = jnp.clip(query_total - 1, 0, query_segment.shape[0] - 1)
    finals = jnp.minimum(begins + TILE - 1, last_real)

    def pick(table, places):
        chosen = jnp.sum(
            jnp.where(
                jnp.arange(query_segment.shape[0], dtype=jnp.int32)[None, :] == places[:, None],
                query_segment[None, :],
                0,
            ),
            axis=1,
        )
        return jnp.sum(
            jnp.where(
                chosen[:, None] == jnp.arange(number, dtype=jnp.int32)[None, :], table[None, :], 0
            ),
            axis=1,
        )

    some = begins < query_total
    first = jnp.where(some, pick(key_starts, begins) // TILE, 0)
    last = jnp.where(some, (pick(key_ends, finals) + TILE - 1) // TILE, 0)
    return first, jnp.maximum(first, last)


def packed_gradients(
    source_stream, target_stream, gain_rows, biases, weights, layout, head, column_start, column_width
):
    enc_attention, enc_feed, dec_self, dec_cross, dec_feed = weights
    (
        source_span,
        target_span,
        cross_span,
        source_row,
        source_column,
        target_row,
        target_column,
    ) = layout
    bias_source, bias_target = biases

    def shard(grad, which=0):
        return lax.dynamic_slice_in_dim(grad, which * MODEL_WIDTH + column_start, column_width, 1)

    def attention(stream, gain_row, context, matrices, span, row, column, causal, bias):
        to_query, to_pair, outward = matrices
        normed = root_norm(stream, gain_row).astype(jnp.bfloat16)
        context = normed if context is None else context
        queries = dot(normed, to_query).astype(jnp.bfloat16)
        pair_rows = dot(context, to_pair).astype(jnp.bfloat16)
        attended, levels = packed_forward(queries, pair_rows, span, row, column, causal, bias)
        return stream + dot(attended, outward), (
            normed,
            context,
            queries,
            pair_rows,
            attended,
            levels,
        )

    def attention_back(grad, stream, gain_row, crossed, matrices, saved, span, row, column, causal, bias):
        to_query, to_pair, outward = matrices
        normed, context, queries, pair_rows, attended, levels = saved
        branch = grad.astype(jnp.bfloat16)
        arriving = dot_nt(branch, outward).astype(jnp.bfloat16)
        grads = packed_backward(
            queries, arriving, pair_rows, levels, span, row, column, causal, bias
        )
        grad_queries, grad_pair = grads[:2]
        pair_shards = [shard(grad_pair), shard(grad_pair, 1)]
        if crossed:
            shares = [
                dot_tn(shard(grad_queries), normed),
                dot_tn(jnp.concatenate(pair_shards, axis=1), context),
                dot_tn(shard(branch), attended),
            ]
        else:
            shares = [
                dot_tn(jnp.concatenate([shard(grad_queries)] + pair_shards, axis=1), normed),
                dot_tn(shard(branch), attended),
            ]
        grad_normed = dot_nt(grad_queries, to_query)
        grad_context = dot_nt(grad_pair, to_pair)
        if not crossed:
            grad_normed = grad_normed + grad_context
        grad_input, grad_gain = norm_backward(stream, gain_row, grad_normed)
        return grad + grad_input, grad_gain, shares, grads[2:], grad_context

    def feed(stream, gain_row, matrices):
        inward, outward = matrices
        normed = root_norm(stream, gain_row).astype(jnp.bfloat16)
        inner = dot(normed, inward)
        hidden = jax.nn.gelu(inner).astype(jnp.bfloat16)
        return stream + dot(hidden, outward), (normed, inner, hidden)

    def feed_back(grad, stream, gain_row, matrices, saved):
        inward, outward = matrices
        normed, inner, hidden = saved
        branch = grad.astype(jnp.bfloat16)
        grad_inner = jax.vjp(jax.nn.gelu, inner)[1](dot_nt(branch, outward))[0].astype(jnp.bfloat16)
        grad_normed = dot_nt(grad_inner, inward)
        inner_shards = jnp.concatenate([shard(grad_inner, j) for j in range(4)], axis=1)
        outward_shares = dot_tn(shard(branch), hidden)
        shares = [dot_tn(inner_shards, normed)] + [
            outward_shares[:, j * MODEL_WIDTH : (j + 1) * MODEL_WIDTH] for j in range(4)
        ]
        grad_input, grad_gain = norm_backward(stream, gain_row, grad_normed)
        return grad + grad_input, grad_gain, shares

    x1, enc_saved = attention(
        source_stream, gain_rows[0], None, enc_attention, source_span, source_row, source_column, False, bias_source
    )
    x2, enc_feed_saved = feed(x1, gain_rows[1], enc_feed)
    encoded = root_norm(x2, gain_rows[2]).astype(jnp.bfloat16)
    encoded, target_stream = lax.optimization_barrier((encoded, target_stream))
    target_stream = target_stream.astype(jnp.float32)
    y1, self_saved = attention(
        target_stream, gain_rows[3], None, dec_self, target_span, target_row, target_column, True, bias_target
    )
    y2, cross_saved = attention(
        y1, gain_rows[4], encoded, dec_cross, cross_span, target_row, source_column, False, None
    )
    y3, dec_feed_saved = feed(y2, gain_rows[5], dec_feed)
    final_rows = (root_norm(y3, gain_rows[6]) * MODEL_WIDTH ** (-0.5)).astype(jnp.bfloat16)

    grad_final, grad_logits, token_loss = head(final_rows)

    grad, gain_final = norm_backward(y3, gain_rows[6], grad_final * MODEL_WIDTH ** (-0.5))
    grad, gain_feed, feed_shares = feed_back(grad, y2, gain_rows[5], dec_feed, dec_feed_saved)
    grad, gain_cross, cross_shares, _, grad_encoded = attention_back(
        grad, y1, gain_rows[4], True, dec_cross, cross_saved, cross_span, target_row, source_column, False, None
    )
    target_grad, gain_self, self_shares, table_target, _ = attention_back(
        grad, target_stream, gain_rows[3], False, dec_self, self_saved, target_span, target_row, target_column, True, bias_target
    )
    grad, gain_encoded = norm_backward(x2, gain_rows[2], grad_encoded)
    grad, gain_enc_feed, enc_feed_shares = feed_back(grad, x1, gain_rows[1], enc_feed, enc_feed_saved)
    source_grad, gain_enc, enc_shares, table_source, _ = attention_back(
        grad, source_stream, gain_rows[0], False, enc_attention, enc_saved, source_span, source_row, source_column, False, bias_source
    )
    gains = jnp.stack(
        [gain_enc, gain_enc_feed, gain_encoded, gain_self, gain_cross, gain_feed, gain_final]
    )
    tables = jnp.stack(
        [
            bias_grad(table_source[0], False),
            bias_grad(table_target[0], True),
        ]
    )
    shares = jnp.concatenate(
        enc_shares + enc_feed_shares + self_shares + cross_shares + feed_shares
    ).reshape(-1, column_width, MODEL_WIDTH)
    return shares, gains, tables, source_grad, target_grad, final_rows, grad_logits, token_loss


def orthonormal_kernel(factor_ref, out_ref):
    rank = factor_ref.shape[0]
    for r in range(rank):
        out_ref[r] = factor_ref[r]
    for r in range(rank):
        row = out_ref[r]
        row = row * lax.rsqrt(jnp.sum(row * row, axis=-1, keepdims=True))
        out_ref[r] = row
        for s in range(r + 1, rank):
            other = out_ref[s]
            out_ref[s] = other - row * jnp.sum(row * other, axis=-1, keepdims=True)


def orthonormal_rows(factor):
    return pl.pallas_call(
        orthonormal_kernel,
        out_shape=jax.ShapeDtypeStruct(factor.shape, jnp.float32),
        name="orthonormal",
    )(factor)


def local(
    source_ids,
    targets,
    source_lengths,
    target_lengths,
    task_ids,
    task_counts,
    blocks,
    blocks_momentum,
    embedding,
    embed_momentum,
    gain_rows,
    gain_momentum,
    position_bias,
    bias_momentum,
    right_blocks,
    right_embed,
    error_blocks,
    error_embed,
):
    fsdp_rank = lax.axis_index("fsdp")
    cuts_rank = lax.axis_index("cuts")
    cuts_count = lax.axis_size("cuts")
    seq_count, source_len = source_ids.shape
    target_len = targets.shape[1]
    number = seq_count * lax.axis_size("fsdp")
    room_source = min(ROOM_SOURCE, source_len * number)
    room_target = min(ROOM_TARGET, target_len * number)
    fewest = min(room_source // source_len, room_target // target_len)
    shares_of = sorted({number, -(-number // 2), fewest}, reverse=True)
    vocab_rows = embedding.shape[0]
    vocab_start = fsdp_rank * vocab_rows
    once = (fsdp_rank == 0).astype(jnp.float32)

    stored_vocab = embedding.T.astype(jnp.bfloat16)
    steps = len(spread_ways())
    bands = max(n for n in range(1, max(steps, 1) + 1) if stored_vocab.shape[0] % (16 * n) == 0 or n == 1)
    vocab_shares = spread_begin(stored_vocab.reshape(bands, -1, vocab_rows))
    stored = jnp.transpose(blocks, (1, 0, 2)).astype(jnp.bfloat16)
    group = lax.all_gather(
        jnp.concatenate(
            [source_ids, targets, source_lengths[:, None], target_lengths[:, None]], axis=1
        ),
        "fsdp",
        axis=0,
        tiled=True,
    )
    group_source = group[:, :source_len]
    group_target = group[:, source_len : source_len + target_len]
    lengths = group[:, -2:]

    def fullest(share):
        padded = jnp.pad(lengths, ((0, -number % share), (0, 0)))
        return jnp.max(jnp.sum(padded.reshape(-1, share, 2), axis=1), axis=0)

    needs = lax.all_gather(
        jnp.concatenate([jnp.sum(lengths, axis=0)] + [fullest(share) for share in shares_of]),
        "cuts",
        axis=0,
    )
    for step in range(steps):
        if step:
            vocab_shares, needs = spread_tied(vocab_shares, needs)
        vocab_shares = spread_step(vocab_shares, step)
    stored, needs = lax.optimization_barrier((stored, needs))
    first_columns = jnp.concatenate(gather_fsdp(stored[:12], fsdp_rank), axis=2)
    errors = jnp.transpose(error_blocks[0], (1, 2, 0))
    biases = (bias_tiles(False, position_bias[0]), bias_tiles(True, position_bias[1]))
    vocab_shares, first_columns, biases = spread_tied(vocab_shares, first_columns, biases)
    first_shares = spread_begin(first_columns)
    first_shares = spread_step(first_shares, 0) if steps else first_shares
    vocab_pieces = spread_end(vocab_shares)
    piece_arrays = [[array for _, array in held] for _, held in vocab_pieces]
    first_arrays = [array for _, array in first_shares]
    given = (group, needs, piece_arrays, first_arrays, stored[12:], errors, biases)

    def one_round(state):
        _, turn, _, _, left_blocks, left_embed, gains_sum, table_sum, loss_sum = state
        turn, group, needs, piece_arrays, first_arrays, stored_rest, errors, biases = (
            lax.optimization_barrier((turn, *given))
        )
        group_source = group[:, :source_len]
        group_target = group[:, source_len : source_len + target_len]
        lengths = group[:, -2:]
        total_count = jnp.sum(needs[:, 1]).astype(jnp.float32)
        most = jnp.max(needs[:, 2:], axis=0)
        share = jnp.int32(shares_of[-1])
        for index in range(len(shares_of) - 2, -1, -1):
            fits = (most[2 * index] <= room_source) & (most[2 * index + 1] <= room_target)
            share = jnp.where(fits, shares_of[index], share)
        members = jnp.arange(number, dtype=jnp.int32)
        taken = (members >= turn * share) & (members < (turn + 1) * share)
        source_taken = jnp.where(taken, lengths[:, 0], 0)
        target_taken = jnp.where(taken, lengths[:, 1], 0)
        more = (turn + 1) * share < number

        chosen = jnp.sum(
            jnp.where(
                task_ids[:, None] == jnp.arange(TASKS, dtype=jnp.int32)[None, :],
                task_counts[None, :],
                0,
            ),
            axis=1,
        ).astype(jnp.float32)
        slice_weight = jnp.sum(
            jnp.where(
                jnp.arange(cuts_count, dtype=jnp.int32) == cuts_rank,
                cuts_count * chosen / jnp.sum(chosen),
                0.0,
            )
        )

        pieces = [
            (first, [(bits, array) for (bits, _), array in zip(held, own)])
            for (first, held), own in zip(vocab_pieces, piece_arrays)
        ]
        (vocab,) = place_pieces(pieces, ((tuple(range(bands)), "mixed"),), cuts_rank)
        shares = [(bits, array) for (bits, _), array in zip(first_shares, first_arrays)]
        rest_parts = [stored_rest] + [
            shifted(stored_rest, distance) for distance in range(1, lax.axis_size("fsdp"))
        ]
        for step in range(1, steps):
            shares = spread_step(shares, step)

        def attention_groups(first):
            return (
                ((first,), "columns"),
                ((first + 1, first + 2), "columns"),
                ((first + 3,), "columns"),
            )

        def feed_groups(first):
            return (
                (tuple(range(first, first + 4)), "columns"),
                (tuple(range(first + 4, first + 8)), "rows"),
            )

        source_segment, source_place, source_starts, source_ends = packing(source_taken, room_source)
        target_segment, target_place, target_starts, target_ends = packing(target_taken, room_target)
        source_real = source_segment < number
        target_real = target_segment < number
        packed_source = jnp.take(
            group_source.reshape(-1),
            jnp.where(source_real, source_segment * source_len + source_place, 0),
        )
        group_input = jnp.concatenate(
            [jnp.zeros_like(group_target[:, :1]), group_target[:, :-1]], axis=1
        )
        target_from = jnp.where(target_real, target_segment * target_len + target_place, 0)
        packed_target = jnp.take(group_target.reshape(-1), target_from)
        packed_input = jnp.take(group_input.reshape(-1), target_from)
        packed_ids = jnp.concatenate([packed_source, packed_input])
        packed_real = jnp.concatenate([source_real, target_real])
        local_ids = jnp.where(packed_real, packed_ids - vocab_start, -1)
        source_total, target_total = jnp.sum(source_taken), jnp.sum(target_taken)
        chunk = 2 * TILE
        local_ids = jnp.pad(local_ids, (0, -local_ids.shape[0] % chunk), constant_values=-1)
        spans = jnp.stack(
            [
                jnp.minimum((source_total + chunk - 1) // chunk, room_source // chunk),
                jnp.int32(room_source // chunk),
                jnp.minimum(
                    (room_source + target_total + chunk - 1) // chunk,
                    local_ids.shape[0] // chunk,
                ),
            ]
        )
        rows = lookup_rows(local_ids, spans, vocab)
        shares, rows = spread_tied(shares, rows)
        first_placed = place_pieces(
            spread_end(shares), attention_groups(0) + feed_groups(4), cuts_rank
        )
        sizes = [room_source * part // 5 for part in (2, 3, 4, 5)]
        fullest_source = jnp.int32(room_source)
        for index in range(len(shares_of) - 1, -1, -1):
            fullest_source = jnp.where(share == shares_of[index], most[2 * index], fullest_source)
        source_rows = lax.switch(
            sum((fullest_source > size).astype(jnp.int32) for size in sizes[:-1]),
            [
                lambda table, size=size: jnp.pad(
                    lax.psum(table[:size], "fsdp"), ((0, room_source - size), (0, 0))
                )
                for size in sizes
            ],
            rows[:room_source],
        )
        source_rows, target_rows, rest_parts = lax.optimization_barrier(
            (source_rows, rows[room_source : room_source + room_target], rest_parts)
        )
        rest_columns = jnp.concatenate(in_order(rest_parts, fsdp_rank), axis=2)
        rest_shares, first_placed = spread_tied(spread_begin(rest_columns), first_placed)
        for step in range(steps):
            rest_shares = spread_step(rest_shares, step)
        rest_pieces = spread_end(rest_shares)
        rest_attention = place_pieces(
            rest_pieces, attention_groups(0) + attention_groups(4), cuts_rank
        )
        rest_feed = place_pieces(rest_pieces, feed_groups(8), cuts_rank)
        weights = (
            first_placed[:3],
            first_placed[3:],
            rest_attention[:3],
            rest_attention[3:],
            rest_feed,
        )
        target_rows = lax.psum(target_rows, "fsdp")
        source_stream = source_rows.astype(jnp.float32)
        target_stream = target_rows
        layout = (
            key_span(source_segment, source_total, source_starts, source_ends),
            key_span(target_segment, target_total, target_starts, target_ends),
            key_span(target_segment, target_total, source_starts, source_ends),
            source_segment[None, :],
            source_segment[:, None],
            target_segment[None, :],
            target_segment[:, None],
        )

        token_mask = target_real.astype(jnp.float32)
        token_weight = token_mask * (slice_weight / total_count)
        target_ids = (packed_target - vocab_start)[:, None]
        target_tiles = ((target_total + TILE - 1) // TILE)[None]

        def head(final_rows):
            logits, own_stats = logit_stats(final_rows, vocab, target_ids, target_tiles)
            stats = lax.all_gather(own_stats[:, :3].T, "fsdp", axis=0)
            top = jnp.max(stats[:, 0], axis=0)
            log_total = top + jnp.log(
                jnp.sum(stats[:, 1] * jnp.exp(stats[:, 0] - top[None, :]), axis=0)
            )
            token_loss = (log_total - jnp.sum(stats[:, 2], axis=0)) * token_mask
            grad_logits, grad_rows = logit_grads(
                logits, vocab, target_ids, target_tiles, log_total, token_weight
            )
            grad_rows = sum_fsdp(grad_rows, fsdp_rank)
            return grad_rows, grad_logits, token_loss

        shares, gains, table_found, source_grad, target_grad, final_rows, grad_logits, token_loss = (
            packed_gradients(
                source_stream,
                target_stream,
                gain_rows,
                biases,
                weights,
                layout,
                head,
                fsdp_rank * blocks.shape[2],
                blocks.shape[2],
            )
        )
        lookups = jnp.concatenate([source_grad, target_grad]).astype(jnp.bfloat16)
        lookups = jnp.pad(lookups, ((0, local_ids.shape[0] - lookups.shape[0]), (0, 0)))
        left_embed = vocab_grad(
            error_embed[0], left_embed, turn, local_ids, spans, lookups, grad_logits, final_rows
        )
        before = jnp.where(turn == 0, errors, left_blocks)
        return (
            more,
            turn + 1,
            total_count,
            slice_weight,
            before + shares,
            left_embed,
            gains_sum + gains,
            table_sum + table_found,
            loss_sum + jnp.sum(token_loss),
        )

    zero = jnp.zeros((), jnp.float32)
    _, _, total_count, slice_weight, left_blocks, left_embed, gains_grad, table_grad, loss_local = (
        lax.while_loop(
            lambda state: state[0],
            one_round,
            (
                jnp.ones((), jnp.bool_),
                jnp.zeros((), jnp.int32),
                zero,
                zero,
                unset((blocks.shape[1], blocks.shape[2], MODEL_WIDTH)),
                unset((vocab_rows, MODEL_WIDTH)),
                jnp.zeros_like(gain_rows),
                jnp.zeros_like(position_bias),
                zero,
            ),
        )
    )

    left_factor = jnp.einsum("kji,kjr->rki", left_blocks, right_blocks, precision=lax.Precision.HIGH)
    embed_factor = jnp.einsum("vd,vr->rd", left_embed, right_embed, precision=lax.Precision.HIGH)
    rank, count = left_factor.shape[:2]
    small = jnp.concatenate(
        [
            gains_grad * once,
            (table_grad * once).reshape(-1, MODEL_WIDTH),
            jnp.full((1, MODEL_WIDTH), loss_local * slice_weight * once),
        ]
    )
    factor = jnp.concatenate([left_factor, embed_factor[:, None]], axis=1)
    packed = jnp.concatenate([factor.reshape(-1, MODEL_WIDTH), small])
    packed = jnp.pad(packed, ((0, -packed.shape[0] % (8 * cuts_count)), (0, 0)))
    packed = sum_everywhere(packed, cuts_rank)
    factor = packed[: rank * (count + 1)].reshape(factor.shape)
    small = packed[rank * (count + 1) :]
    gains_grad = small[: gain_rows.shape[0]]
    table_rows = position_bias.size // MODEL_WIDTH
    table_grad = small[gain_rows.shape[0] :][:table_rows].reshape(position_bias.shape)
    loss_total = small[gain_rows.shape[0] + table_rows, 0]
    factor = orthonormal_rows(factor)
    left_factor, embed_factor = factor[:, :-1], factor[:, -1]
    factors_blocks = jnp.einsum("kji,rki->rkj", left_blocks, left_factor, precision=lax.Precision.DEFAULT)
    factors_embed = jnp.einsum("vd,rd->rv", left_embed, embed_factor, precision=lax.Precision.DEFAULT)
    both = sum_cuts(jnp.concatenate([factors_blocks.reshape(rank, -1), factors_embed], axis=1))
    factors_embed = both[:, -vocab_rows:]
    factors_blocks = both[:, :-vocab_rows].reshape(factors_blocks.shape)
    gram_blocks = jnp.einsum("rki,ski->krs", left_factor, left_factor, precision=TOP_PRECISION)
    gram_embed = jnp.einsum("rd,sd->rs", embed_factor, embed_factor, precision=TOP_PRECISION)
    squares = jnp.sum(
        factors_blocks
        * jnp.einsum("krs,skj->rkj", gram_blocks, factors_blocks, precision=lax.Precision.HIGH)
    ) + jnp.sum(factors_embed * jnp.dot(gram_embed, factors_embed, precision=lax.Precision.HIGH))
    squares = lax.psum(squares, "fsdp")
    full_blocks = jnp.einsum("rki,rkj->kji", left_factor, factors_blocks, precision=lax.Precision.DEFAULT)
    full_embed = jnp.einsum("rv,rd->vd", factors_embed, embed_factor, precision=lax.Precision.DEFAULT)
    owned_rows = blocks.shape[0]
    owned_columns = embedding.shape[1]
    own_left = lax.dynamic_slice_in_dim(left_factor, cuts_rank * owned_rows, owned_rows, 2)
    own_right = lax.dynamic_slice_in_dim(embed_factor, cuts_rank * owned_columns, owned_columns, 1)
    own_blocks = jnp.einsum("rki,rkj->ikj", own_left, factors_blocks, precision=lax.Precision.DEFAULT)
    own_embed = jnp.einsum("rv,rd->vd", factors_embed, own_right, precision=lax.Precision.DEFAULT)
    small_squares = jnp.sum(gains_grad * gains_grad) + jnp.sum(table_grad * table_grad)
    grad_norm = jnp.sqrt(squares + small_squares)
    clip_factor = jnp.minimum(1.0, CLIP_NORM / grad_norm)
    step_size = STEP_RATE * math.sqrt(PARAMS / MODEL_WIDTH) / CLIP_NORM
    embed_step = step_size * EMBED_SHARE * math.sqrt(MODEL_WIDTH)
    small_step = step_size * SMALL_SHARE * math.sqrt(MODEL_WIDTH)
    momentum_blocks = MOMENTUM_DECAY * blocks_momentum + (1.0 - MOMENTUM_DECAY) * (
        clip_factor * own_blocks
    )
    momentum_embed = MOMENTUM_DECAY * embed_momentum + (1.0 - MOMENTUM_DECAY) * (
        clip_factor * own_embed
    )
    momentum_gains = MOMENTUM_DECAY * gain_momentum + (1.0 - MOMENTUM_DECAY) * (
        clip_factor * gains_grad
    )
    momentum_bias = MOMENTUM_DECAY * bias_momentum + (1.0 - MOMENTUM_DECAY) * (
        clip_factor * table_grad
    )
    return (
        loss_total,
        total_count,
        grad_norm,
        blocks - step_size * momentum_blocks,
        momentum_blocks,
        embedding - embed_step * momentum_embed,
        momentum_embed,
        gain_rows - small_step * momentum_gains,
        momentum_gains,
        position_bias - small_step * momentum_bias,
        momentum_bias,
        jnp.transpose(factors_blocks, (1, 2, 0)),
        factors_embed.T,
        jnp.transpose(left_blocks - full_blocks, (2, 0, 1))[None],
        (left_embed - full_embed)[None],
    )


def solution(mesh):
    return jax.shard_map(
        local,
        mesh=mesh,
        in_specs=(
            P(("cuts", "fsdp"), None),
            P(("cuts", "fsdp"), None),
            P(("cuts", "fsdp")),
            P(("cuts", "fsdp")),
            P(),
            P(),
            P("cuts", None, "fsdp"),
            P("cuts", None, "fsdp"),
            P("fsdp", "cuts"),
            P("fsdp", "cuts"),
            P(),
            P(),
            P(),
            P(),
            P(None, "fsdp", None),
            P("fsdp", None),
            P("cuts", None, None, "fsdp"),
            P("cuts", "fsdp", None),
        ),
        out_specs=(
            P(),
            P(),
            P(),
            P("cuts", None, "fsdp"),
            P("cuts", None, "fsdp"),
            P("fsdp", "cuts"),
            P("fsdp", "cuts"),
            P(),
            P(),
            P(),
            P(),
            P(None, "fsdp", None),
            P("fsdp", None),
            P("cuts", None, None, "fsdp"),
            P("cuts", "fsdp", None),
        ),
        check_vma=False,
    )
```

```python
import itertools
import math

import jax
import jax.numpy as jnp
from jax import lax
from jax.experimental import pallas as pl
from jax.experimental.layout import Layout, with_layout_constraint
from jax.experimental.pallas import tpu as pltpu
from jax.sharding import PartitionSpec as P

MODEL_WIDTH = 768
H = 12
DH = 64
FEED_UNITS = 3072
NBK = 32
TASKS = 8
PARAMS = 41189376


EPSILON = 1e-06
MASKED = -1000000000.0
CLIP_NORM = 0.05
MOMENTUM_DECAY = 0.9
STEP_RATE = 5.0
EMBED_SHARE = 50.0
SMALL_SHARE = 1.0 / 7.0
TOP_PRECISION = lax.Precision.HIGHEST
TILE = 128
ROOM_SOURCE = 1280
ROOM_TARGET = 384
ENCODER_EDGES = (12, 16, 23, 32, 46, 64, 91)
DECODER_EDGES = (19, 21, 24, 27, 31, 35, 40, 46, 52, 59, 67, 77, 87, 99, 113)


def root_norm(stream, gain_row):
    return (
        stream * lax.rsqrt(jnp.mean(stream * stream, axis=-1, keepdims=True) + EPSILON) * gain_row
    )


def norm_backward(stream, gain_row, grad_normed):
    _, pull_back = jax.vjp(root_norm, stream, gain_row)
    return pull_back(grad_normed)


def dot(left, right):
    return jnp.dot(left, right, preferred_element_type=jnp.float32)


def dot_nt(left, right):
    return lax.dot_general(left, right, (((1,), (1,)), ((), ())), preferred_element_type=jnp.float32)


def dot_tn(left, right):
    return lax.dot_general(left, right, (((0,), (0,)), ((), ())), preferred_element_type=jnp.float32)


def exchange(array, mask):
    return lax.ppermute(array, "cuts", [(i, i ^ mask) for i in range(lax.axis_size("cuts"))])


def shifted(array, distance):
    count = lax.axis_size("fsdp")
    return lax.ppermute(array, "fsdp", [(i, (i + distance) % count) for i in range(count)])


def in_order(pieces, rank):
    count = len(pieces)
    ordered = []
    for place in range(count):
        chosen = pieces[-place % count]
        for own in range(1, count):
            chosen = jnp.where(rank == own, pieces[(own - place) % count], chosen)
        ordered.append(chosen)
    return ordered


def gather_fsdp(part, rank):
    count = lax.axis_size("fsdp")
    return in_order([part] + [shifted(part, distance) for distance in range(1, count)], rank)


def sum_fsdp(part, rank):
    count = lax.axis_size("fsdp")
    rows = part.shape[0] // count
    low = part.astype(jnp.bfloat16)
    total = lax.dynamic_slice_in_dim(part, rank * rows, rows, 0)
    for distance in range(1, count):
        piece = lax.dynamic_slice_in_dim(low, (rank + distance) % count * rows, rows, 0)
        total = total + shifted(piece, distance).astype(jnp.float32)
    return jnp.concatenate(gather_fsdp(total.astype(jnp.bfloat16), rank), axis=0).astype(jnp.float32)


def sum_everywhere(part, cuts_rank):
    count = lax.axis_size("cuts")
    masks = [1 << bit for bit in range(count.bit_length() - 1)]
    if count & (count - 1) or part.shape[0] % count:
        return lax.psum(part, ("cuts", "fsdp"))
    bits = [(cuts_rank // mask) % 2 for mask in masks]
    for mask, bit in zip(masks, bits):
        half = part.shape[0] // 2
        away = lax.dynamic_slice_in_dim(part, (1 - bit) * half, half, 0)
        part = lax.dynamic_slice_in_dim(part, bit * half, half, 0) + exchange(away, mask)
    part = jnp.sum(lax.all_gather(part, "fsdp", axis=0), axis=0)
    for mask, bit in zip(masks[::-1], bits[::-1]):
        other = exchange(part, mask)
        part = jnp.where(
            bit == 1, jnp.concatenate([other, part], axis=0), jnp.concatenate([part, other], axis=0)
        )
    return part


def sum_cuts(part):
    count = lax.axis_size("cuts")
    if count & (count - 1):
        return lax.psum(part.astype(jnp.bfloat16), "cuts").astype(jnp.float32)
    for bit in range(count.bit_length() - 1):
        low = part.astype(jnp.bfloat16)
        part = low.astype(jnp.float32) + exchange(low, 1 << bit).astype(jnp.float32)
    return part


def spread_ways():
    return [1 << bit for bit in range(1, lax.axis_size("cuts").bit_length() - 1)]


def spread_begin(part):
    number = max(min(len(spread_ways()), part.shape[0]), 1)
    ends = [part.shape[0] * turn // number for turn in range(number + 1)]
    return [([0], part[None, begin:end]) for begin, end in zip(ends, ends[1:])]


def spread_send(shares, step):
    ways = spread_ways()
    return [
        exchange(held, ways[(turn + step) % len(ways)]) for turn, (_, held) in enumerate(shares)
    ]


def spread_receive(shares, arriving, step):
    ways = spread_ways()
    after = []
    for turn, ((bits, held), array) in enumerate(zip(shares, arriving)):
        mask = ways[(turn + step) % len(ways)]
        after.append((bits + [bit ^ mask for bit in bits], jnp.concatenate([held, array])))
    return after


def spread_step(shares, step):
    return spread_receive(shares, spread_send(shares, step), step)


def spread_end(shares):
    found, first = [], 0
    for bits, held in shares:
        found.append((first, [(bits, held), ([bit ^ 1 for bit in bits], exchange(held, 1))]))
        first += held.shape[1]
    return found


def spread_tied(shares, *others):
    arrays, others = lax.optimization_barrier(([held for _, held in shares], others))
    return [(bits, held) for (bits, _), held in zip(shares, arrays)], *others


def cost(flops, moved, powers=0):
    return pl.CostEstimate(flops=int(flops), bytes_accessed=int(moved), transcendentals=int(powers))


def place_kernel(moves, number, rank_ref, *refs):
    sources, outs, sem = refs[:number], refs[number:-1], refs[-1]
    rank = rank_ref[0]
    copies = []
    for source, piece, index, bits, (out, pitch, row, column), shape in moves:
        rows = pl.ds(pl.multiple_of((rank ^ bits) * pitch + row, 16), shape[0])
        copies.append(
            pltpu.make_async_copy(
                sources[source].at[piece, index],
                outs[out].at[rows, pl.ds(column, shape[1])],
                sem.at[len(copies)],
            )
        )
    for copy in copies:
        copy.start()
    for copy in copies:
        copy.wait()


def place_pieces(found, groups, rank):
    count = lax.axis_size("cuts")
    height, width = found[0][1][0][1].shape[2:]
    where = {}
    shapes = []
    for out, (members, how) in enumerate(groups):
        for order, matrix in enumerate(members):
            row = {"columns": 0, "rows": order * count * height, "mixed": order * height}[how]
            pitch = height * (len(members) if how == "mixed" else 1)
            where[matrix] = (out, pitch, row, order * width if how == "columns" else 0)
        tall, wide = (1, len(members)) if how == "columns" else (len(members), 1)
        shapes.append((tall * count * height, wide * width))
    sources, moves = [], []
    for first, held in found:
        for bits, array in held:
            for piece, index in itertools.product(range(array.shape[0]), range(array.shape[1])):
                if first + index in where:
                    moves.append(
                        (len(sources), piece, index, bits[piece], where[first + index], (height, width))
                    )
            sources.append(array)
    space = pl.BlockSpec(memory_space=pl.ANY)
    return pl.pallas_call(
        lambda *refs: place_kernel(moves, len(sources), *refs),
        in_specs=[pl.BlockSpec(memory_space=pltpu.SMEM)] + [space] * len(sources),
        out_specs=[pl.BlockSpec(memory_space=pltpu.VMEM)] * len(shapes),
        out_shape=[jax.ShapeDtypeStruct(shape, sources[0].dtype) for shape in shapes],
        scratch_shapes=[pltpu.SemaphoreType.DMA((len(moves),))],
        compiler_params=pltpu.CompilerParams(vmem_limit_bytes=40 << 20),
        cost_estimate=cost(0, 5 * sum(math.prod(shape) for shape in shapes)),
        name="place",
    )(rank[None], *sources)


def unset_kernel(out_ref):
    pass


def unset(shape):
    return pl.pallas_call(
        unset_kernel,
        out_specs=pl.BlockSpec(memory_space=pl.ANY),
        out_shape=jax.ShapeDtypeStruct(shape, jnp.float32),
        name="unset",
    )()


PAIRS = H // 2
WIDE = 2 * TILE


def offset_buckets(causal, offset):
    if causal:
        distance = jnp.maximum(-offset, 0)
        farther = 16 + sum(((distance >= boundary).astype(jnp.int32) for boundary in DECODER_EDGES))
        bucket = jnp.where(distance < 16, distance, farther)
    else:
        distance = jnp.abs(offset)
        farther = 8 + sum(((distance >= boundary).astype(jnp.int32) for boundary in ENCODER_EDGES))
        bucket = jnp.where(distance < 8, distance, farther) + jnp.where(offset > 0, 16, 0)
    return (bucket[..., None] == jnp.arange(NBK, dtype=jnp.int32)).astype(jnp.float32)


def bias_kernel(row_ref, out_ref):
    for head in range(H):
        row = jnp.broadcast_to(row_ref[0, head : head + 1, :], (TILE, WIDE))
        tile = pltpu.roll(row, 0, 1, stride=1, stride_axis=0)[:, :TILE]
        out_ref[0, head // 2, :, (head % 2) * TILE : (head % 2 + 1) * TILE] = tile


def bias_tiles(causal, table):
    lane = jnp.arange(WIDE, dtype=jnp.int32)
    offset = (jnp.arange(5, dtype=jnp.int32)[:, None] - 2) * TILE + jnp.where(
        lane < TILE, -lane, WIDE - lane
    )
    rows = jnp.einsum(
        "tqb,bh->thq", offset_buckets(causal, offset), table, precision=TOP_PRECISION
    )
    return pl.pallas_call(
        bias_kernel,
        grid=(5,),
        in_specs=[pl.BlockSpec((1, 16, WIDE), lambda i: (i, 0, 0))],
        out_specs=pl.BlockSpec((1, PAIRS, TILE, WIDE), lambda i: (i, 0, 0, 0)),
        out_shape=jax.ShapeDtypeStruct((5, PAIRS, TILE, WIDE), jnp.float32),
        name="bias",
    )(jnp.pad(rows, ((0, 0), (0, 16 - H), (0, 0))))


def bias_grad(tiles, causal):
    places = jnp.arange(TILE, dtype=jnp.int32)
    offset = (
        (jnp.arange(5, dtype=jnp.int32)[:, None, None] - 2) * TILE
        + places[None, :, None]
        - places[None, None, :]
    )
    hot = offset_buckets(causal, offset)
    found = [
        jnp.einsum("tpkq,tkqb->bp", tiles[..., half], hot, precision=lax.Precision.HIGH)
        for half in (slice(0, TILE), slice(TILE, WIDE))
    ]
    return jnp.stack(found, axis=-1).reshape(NBK, H)


def stack_heads(pair):
    half = lax.broadcasted_iota(jnp.int32, (TILE, TILE), 1) // DH
    return jnp.concatenate(
        [jnp.where(half == which, pair, jnp.zeros_like(pair)) for which in range(2)], axis=0
    )


def own_features(wide):
    return jnp.concatenate([wide[:DH, :TILE], wide[DH:, TILE:]], axis=0)


def kept(segment_column, segment_row, key_tile, query_tile, causal):
    keep = segment_column == jnp.concatenate([segment_row, segment_row], axis=1)
    if causal:
        key_place = key_tile * TILE + lax.broadcasted_iota(jnp.int32, (TILE, WIDE), 0)
        query_place = query_tile * TILE + lax.broadcasted_iota(jnp.int32, (TILE, WIDE), 1) % TILE
        keep = keep & (key_place <= query_place)
    return keep


def tile_scores(keys, queries, keep, bias):
    scores = dot_nt(keys, queries)
    if bias is not None:
        scores = scores + bias
    return jnp.where(keep, scores, MASKED)


def forward_kernel(
    causal, biased, first_ref, last_ref, q_ref, k_ref, v_ref, row_ref, column_ref, *rest
):
    bias_ref = rest[0] if biased else None
    out_ref, level_ref, stack_ref, top_ref, sum_ref, total_ref = rest[1:] if biased else rest
    here = pl.program_id(0)
    top_ref[...] = jnp.full_like(top_ref, -1e30)
    sum_ref[...] = jnp.zeros_like(sum_ref)
    total_ref[...] = jnp.zeros_like(total_ref)
    segment_row = row_ref[...]
    for pair in range(PAIRS):
        stack_ref[pair] = stack_heads(q_ref[:, pair * TILE : (pair + 1) * TILE])

    def step(there, carry):
        rows = pl.ds(pl.multiple_of(there * TILE, TILE), TILE)
        keep = kept(column_ref[rows, :], segment_row, there, here, causal)
        offset = jnp.clip(there - here, -2, 2) + 2
        before, sums = top_ref[...], sum_ref[...]
        tops, sums_after = [], []
        for pair in range(PAIRS):
            lanes = slice(pair * TILE, (pair + 1) * TILE)
            scores = tile_scores(
                k_ref[rows, lanes], stack_ref[pair], keep, bias_ref[offset, pair] if biased else None
            )
            old = before[pair : pair + 1, :]
            top = jnp.maximum(old, jnp.max(scores, axis=0, keepdims=True))
            weights = jnp.exp(scores - top)
            scale = jnp.exp(old - top)
            tops.append(top)
            sums_after.append(
                sums[pair : pair + 1, :] * scale + jnp.sum(weights, axis=0, keepdims=True)
            )
            total_ref[pair] = total_ref[pair] * scale + dot(
                v_ref[rows, lanes].T, weights.astype(jnp.bfloat16)
            )
        for pair in range(PAIRS):
            top_ref[pair : pair + 1, :] = tops[pair]
            sum_ref[pair : pair + 1, :] = sums_after[pair]
        return carry

    lax.fori_loop(first_ref[here], last_ref[here], step, 0)
    seen = sum_ref[...] > 0.0
    divisor = jnp.where(seen, sum_ref[...], 1.0)
    level_ref[...] = jnp.where(seen, top_ref[...] + jnp.log(divisor), 0.0)
    for pair in range(PAIRS):
        lanes = slice(pair * TILE, (pair + 1) * TILE)
        wide = total_ref[pair] / divisor[pair : pair + 1, :]
        out_ref[:, lanes] = own_features(wide).T.astype(jnp.bfloat16)


def backward_kernel(
    causal, biased, first_ref, last_ref, q_ref, o_ref, k_ref, v_ref, level_ref, row_ref, column_ref, *rest
):
    bias_ref = rest[0] if biased else None
    rest = rest[1:] if biased else rest
    gq_ref, gkv_ref = rest[:2]
    gb_ref = rest[2] if biased else None
    weight_ref, slope_ref, mean_ref, stack_ref, arrive_ref, tq_ref, tk_ref, tv_ref = rest[-8:]
    here = pl.program_id(0)

    @pl.when(here == 0)
    def _():
        tk_ref[...] = jnp.zeros_like(tk_ref)
        tv_ref[...] = jnp.zeros_like(tv_ref)
        if biased:
            gb_ref[...] = jnp.zeros_like(gb_ref)

    mean_ref[...] = jnp.zeros_like(mean_ref)
    tq_ref[...] = jnp.zeros_like(tq_ref)
    segment_row = row_ref[...]
    first = first_ref[here]
    last = last_ref[here]
    for pair in range(PAIRS):
        lanes = slice(pair * TILE, (pair + 1) * TILE)
        stack_ref[pair] = stack_heads(q_ref[:, lanes])
        arrive_ref[pair] = stack_heads(o_ref[:, lanes])

    def look(there, carry):
        rows = pl.ds(pl.multiple_of(there * TILE, TILE), TILE)
        keep = kept(column_ref[rows, :], segment_row, there, here, causal)
        offset = jnp.clip(there - here, -2, 2) + 2
        means = mean_ref[...]
        sums = []
        for pair in range(PAIRS):
            lanes = slice(pair * TILE, (pair + 1) * TILE)
            scores = tile_scores(
                k_ref[rows, lanes], stack_ref[pair], keep, bias_ref[offset, pair] if biased else None
            )
            weights = jnp.exp(scores - level_ref[pair : pair + 1, :])
            slopes = dot_nt(v_ref[rows, lanes], arrive_ref[pair])
            sums.append(
                means[pair : pair + 1, :] + jnp.sum(weights * slopes, axis=0, keepdims=True)
            )
            weight_ref[there - first, pair] = weights
            slope_ref[there - first, pair] = slopes
            tv_ref[rows, lanes] = tv_ref[rows, lanes] + dot(
                weights.astype(jnp.bfloat16), arrive_ref[pair]
            )
        for pair in range(PAIRS):
            mean_ref[pair : pair + 1, :] = sums[pair]
        return carry

    def push(there, carry):
        rows = pl.ds(pl.multiple_of(there * TILE, TILE), TILE)
        offset = jnp.clip(there - here, -2, 2) + 2
        for pair in range(PAIRS):
            lanes = slice(pair * TILE, (pair + 1) * TILE)
            slopes = (
                weight_ref[there - first, pair]
                * (slope_ref[there - first, pair] - mean_ref[pair : pair + 1, :])
            ).astype(jnp.bfloat16)
            if biased:
                gb_ref[offset, pair] = gb_ref[offset, pair] + slopes.astype(jnp.float32)
            tq_ref[pair] = tq_ref[pair] + dot(k_ref[rows, lanes].T, slopes)
            tk_ref[rows, lanes] = tk_ref[rows, lanes] + dot(slopes, stack_ref[pair])
        return carry

    lax.fori_loop(first, last, look, 0)
    lax.fori_loop(first, last, push, 0)
    for pair in range(PAIRS):
        lanes = slice(pair * TILE, (pair + 1) * TILE)
        gq_ref[:, lanes] = own_features(tq_ref[pair]).T.astype(jnp.bfloat16)

    @pl.when(here == pl.num_programs(0) - 1)
    def _():
        gkv_ref[:, :MODEL_WIDTH] = tk_ref[...].astype(jnp.bfloat16)
        gkv_ref[:, MODEL_WIDTH:] = tv_ref[...].astype(jnp.bfloat16)


def whole_block(shape):
    return pl.BlockSpec(shape, lambda i, *_: (0,) * len(shape))


def column_block(rows, index):
    return pl.BlockSpec((rows, MODEL_WIDTH), lambda i, *_: (0, index))


def packed_forward(queries, pair_rows, span, segment_row, segment_column, causal, bias):
    count, other = queries.shape[0], pair_rows.shape[0]
    biased = bias is not None
    tile = pl.BlockSpec((TILE, MODEL_WIDTH), lambda i, *_: (i, 0))
    return pl.pallas_call(
        lambda *refs: forward_kernel(causal, biased, *refs),
        grid_spec=pltpu.PrefetchScalarGridSpec(
            num_scalar_prefetch=2,
            grid=(count // TILE,),
            in_specs=[
                tile,
                column_block(other, 0),
                column_block(other, 1),
                pl.BlockSpec((1, TILE), lambda i, *_: (0, i)),
                whole_block((other, 1)),
            ]
            + ([whole_block((5, PAIRS, TILE, WIDE))] if biased else []),
            out_specs=[tile, pl.BlockSpec((8, WIDE), lambda i, *_: (0, i))],
            scratch_shapes=[
                pltpu.VMEM((PAIRS, WIDE, TILE), jnp.bfloat16),
                pltpu.VMEM((8, WIDE), jnp.float32),
                pltpu.VMEM((8, WIDE), jnp.float32),
                pltpu.VMEM((PAIRS, TILE, WIDE), jnp.float32),
            ],
        ),
        out_shape=[
            jax.ShapeDtypeStruct((count, MODEL_WIDTH), jnp.bfloat16),
            jax.ShapeDtypeStruct((8, 2 * count), jnp.float32),
        ],
        compiler_params=pltpu.CompilerParams(vmem_limit_bytes=40 << 20),
        cost_estimate=cost(8 * count * other * MODEL_WIDTH, 20 << 20),
        name="attend",
    )(*span, queries, pair_rows, pair_rows, segment_row, segment_column, *([bias] if biased else []))


def packed_backward(
    queries, grad_out, pair_rows, levels, span, segment_row, segment_column, causal, bias
):
    count, other = queries.shape[0], pair_rows.shape[0]
    biased = bias is not None
    reach = min(other // TILE, 9) if biased else other // TILE
    tile = pl.BlockSpec((TILE, MODEL_WIDTH), lambda i, *_: (i, 0))
    table = (5, PAIRS, TILE, WIDE)
    return pl.pallas_call(
        lambda *refs: backward_kernel(causal, biased, *refs),
        grid_spec=pltpu.PrefetchScalarGridSpec(
            num_scalar_prefetch=2,
            grid=(count // TILE,),
            in_specs=[
                tile,
                tile,
                column_block(other, 0),
                column_block(other, 1),
                pl.BlockSpec((8, WIDE), lambda i, *_: (0, i)),
                pl.BlockSpec((1, TILE), lambda i, *_: (0, i)),
                whole_block((other, 1)),
            ]
            + ([whole_block(table)] if biased else []),
            out_specs=[tile, whole_block((other, 2 * MODEL_WIDTH))]
            + ([whole_block(table)] if biased else []),
            scratch_shapes=[
                pltpu.VMEM((reach, PAIRS, TILE, WIDE), jnp.float32),
                pltpu.VMEM((reach, PAIRS, TILE, WIDE), jnp.float32),
                pltpu.VMEM((8, WIDE), jnp.float32),
                pltpu.VMEM((PAIRS, WIDE, TILE), jnp.bfloat16),
                pltpu.VMEM((PAIRS, WIDE, TILE), jnp.bfloat16),
                pltpu.VMEM((PAIRS, TILE, WIDE), jnp.float32),
                pltpu.VMEM((other, MODEL_WIDTH), jnp.float32),
                pltpu.VMEM((other, MODEL_WIDTH), jnp.float32),
            ],
        ),
        out_shape=[
            jax.ShapeDtypeStruct((count, MODEL_WIDTH), jnp.bfloat16),
            jax.ShapeDtypeStruct((other, 2 * MODEL_WIDTH), jnp.bfloat16),
        ]
        + ([jax.ShapeDtypeStruct(table, jnp.float32)] if biased else []),
        compiler_params=pltpu.CompilerParams(vmem_limit_bytes=58 << 20),
        cost_estimate=cost(20 * count * other * MODEL_WIDTH, 40 << 20),
        name="attend_back",
    )(
        *span,
        queries,
        grad_out,
        pair_rows,
        pair_rows,
        levels,
        segment_row,
        segment_column,
        *([bias] if biased else []),
    )


def lookup_kernel(rows_in, blocks_ref, id_ref, vocab_ref, out_ref, total_ref):
    step = pl.program_id(0)
    width = vocab_ref.shape[1]
    chunk = 2 * TILE

    @pl.when(step == 0)
    def _():
        total_ref[...] = jnp.zeros_like(total_ref)

    inside = step * width + lax.broadcasted_iota(jnp.int32, (1, width), 1) < rows_in
    table = jnp.where(inside, vocab_ref[...], jnp.zeros_like(vocab_ref[...]))
    places = step * width + lax.broadcasted_iota(jnp.int32, (chunk, width), 1)

    def one(index, carry):
        rows = pl.ds(pl.multiple_of(index * chunk, chunk), chunk)
        hot = (id_ref[rows, :] == places).astype(jnp.bfloat16)
        total_ref[rows, :] = total_ref[rows, :] + dot_nt(hot, table)
        return carry

    lax.fori_loop(0, blocks_ref[0], one, 0)
    lax.fori_loop(blocks_ref[1], blocks_ref[2], one, 0)

    @pl.when(step == pl.num_programs(0) - 1)
    def _():
        out_ref[...] = total_ref[...].astype(jnp.bfloat16)


def lookup_rows(local_ids, spans, vocab):
    count, width = local_ids.shape[0], 4 * TILE
    rows_in = vocab.shape[1]
    return pl.pallas_call(
        lambda *refs: lookup_kernel(rows_in, *refs),
        grid_spec=pltpu.PrefetchScalarGridSpec(
            num_scalar_prefetch=1,
            grid=(pl.cdiv(rows_in, width),),
            in_specs=[
                whole_block((count, 1)),
                pl.BlockSpec((MODEL_WIDTH, width), lambda i, *_: (0, i)),
            ],
            out_specs=whole_block((count, MODEL_WIDTH)),
            scratch_shapes=[pltpu.VMEM((count, MODEL_WIDTH), jnp.float32)],
        ),
        out_shape=jax.ShapeDtypeStruct((count, MODEL_WIDTH), jnp.bfloat16),
        compiler_params=pltpu.CompilerParams(vmem_limit_bytes=40 << 20),
        cost_estimate=cost(2 * count * rows_in * MODEL_WIDTH, 90 << 20),
        name="lookup",
    )(spans, local_ids[:, None], vocab)


def vocab_grad_kernel(blocks_ref, id_ref, grad_ref, logit_ref, final_ref, start_ref, left_ref, out_ref):
    step = pl.program_id(0)
    width = left_ref.shape[0]
    chunk = 2 * TILE
    before = jnp.where(blocks_ref[3] == 0, start_ref[...], left_ref[...])
    out_ref[...] = before + dot_tn(logit_ref[...], final_ref[...])
    places = step * width + lax.broadcasted_iota(jnp.int32, (width, chunk), 0)

    def one(index, carry):
        rows = pl.ds(pl.multiple_of(index * chunk, chunk), chunk)
        hot = (places == id_ref[:, rows]).astype(jnp.bfloat16)
        out_ref[...] = out_ref[...] + dot(hot, grad_ref[rows, :])
        return carry

    lax.fori_loop(0, blocks_ref[0], one, 0)
    lax.fori_loop(blocks_ref[1], blocks_ref[2], one, 0)


def vocab_grad(start, left, turn, local_ids, spans, lookups, grad_logits, final_rows):
    count, width = local_ids.shape[0], 4 * TILE
    rows_in = left.shape[0]
    block = pl.BlockSpec((width, MODEL_WIDTH), lambda i, *_: (i, 0))
    return pl.pallas_call(
        vocab_grad_kernel,
        grid_spec=pltpu.PrefetchScalarGridSpec(
            num_scalar_prefetch=1,
            grid=(pl.cdiv(rows_in, width),),
            in_specs=[
                whole_block((1, count)),
                whole_block((count, MODEL_WIDTH)),
                pl.BlockSpec((grad_logits.shape[0], width), lambda i, *_: (0, i)),
                whole_block(final_rows.shape),
                pl.BlockSpec((width, MODEL_WIDTH), lambda i, s: (jnp.where(s[3] == 0, i, 0), 0)),
                pl.BlockSpec((width, MODEL_WIDTH), lambda i, s: (jnp.where(s[3] == 0, 0, i), 0)),
            ],
            out_specs=block,
        ),
        out_shape=jax.ShapeDtypeStruct(left.shape, jnp.float32),
        input_output_aliases={6: 0},
        compiler_params=pltpu.CompilerParams(vmem_limit_bytes=40 << 20),
        cost_estimate=cost(2 * (count + 384) * rows_in * MODEL_WIDTH, 100 << 20),
        name="vocab_grad",
    )(
        jnp.concatenate([spans, turn[None]]),
        local_ids[None, :],
        lookups,
        grad_logits,
        final_rows,
        start,
        left,
    )


def logit_places(step, rows_in, width):
    return step * width + lax.broadcasted_iota(jnp.int32, (TILE, width), 1)


def logit_kernel(rows_in, tiles_ref, row_ref, vocab_ref, id_ref, logit_ref, stat_ref, top_ref, sum_ref, hit_ref):
    step = pl.program_id(0)
    width = vocab_ref.shape[1]

    @pl.when(step == 0)
    def _():
        top_ref[...] = jnp.full_like(top_ref, -1e30)
        sum_ref[...] = jnp.zeros_like(sum_ref)
        hit_ref[...] = jnp.zeros_like(hit_ref)

    places = logit_places(step, rows_in, width)

    def one(index, carry):
        rows = pl.ds(pl.multiple_of(index * TILE, TILE), TILE)
        logits = dot(row_ref[rows, :], vocab_ref[...])
        logit_ref[rows, :] = logits
        inside = places < rows_in
        hits = jnp.where(inside & (places == id_ref[rows, :]), logits, 0.0)
        logits = jnp.where(inside, logits, -1e30)
        parts = [slice(begin, begin + TILE) for begin in range(0, width, TILE)]
        before = top_ref[rows, :]
        top = before
        for part in parts:
            top = jnp.maximum(top, logits[:, part])
        total = sum_ref[rows, :] * jnp.exp(before - top)
        hit = hit_ref[rows, :]
        for part in parts:
            total = total + jnp.exp(logits[:, part] - top)
            hit = hit + hits[:, part]
        top_ref[rows, :] = top
        sum_ref[rows, :] = total
        hit_ref[rows, :] = hit
        return carry

    lax.fori_loop(0, tiles_ref[0], one, 0)

    @pl.when(step == pl.num_programs(0) - 1)
    def _():
        top = jnp.max(top_ref[...], axis=1, keepdims=True)
        total = jnp.sum(sum_ref[...] * jnp.exp(top_ref[...] - top), axis=1, keepdims=True)
        hit = jnp.sum(hit_ref[...], axis=1, keepdims=True)
        lane = lax.broadcasted_iota(jnp.int32, stat_ref.shape, 1)
        seen = jnp.where(total > 0.0, total, 1.0)
        stat_ref[...] = jnp.where(lane == 0, top, jnp.where(lane == 1, seen, hit))


def logit_stats(final_rows, vocab, ids, tiles):
    count, rows_in, width = final_rows.shape[0], vocab.shape[1], 4 * TILE
    return pl.pallas_call(
        lambda *refs: logit_kernel(rows_in, *refs),
        grid_spec=pltpu.PrefetchScalarGridSpec(
            num_scalar_prefetch=1,
            grid=(pl.cdiv(rows_in, width),),
            in_specs=[
                whole_block((count, MODEL_WIDTH)),
                pl.BlockSpec((MODEL_WIDTH, width), lambda i, *_: (0, i)),
                whole_block((count, 1)),
            ],
            out_specs=[
                pl.BlockSpec((count, width), lambda i, *_: (0, i)),
                whole_block((count, TILE)),
            ],
            scratch_shapes=[pltpu.VMEM((count, TILE), jnp.float32)] * 3,
        ),
        out_shape=[
            jax.ShapeDtypeStruct((count, rows_in), jnp.float32),
            jax.ShapeDtypeStruct((count, TILE), jnp.float32),
        ],
        compiler_params=pltpu.CompilerParams(vmem_limit_bytes=40 << 20),
        cost_estimate=cost(2 * count * rows_in * MODEL_WIDTH, 40 << 20, count * rows_in),
        name="logits",
    )(tiles, final_rows, vocab, ids)


def logit_grad_kernel(
    rows_in, tiles_ref, logit_ref, vocab_ref, id_ref, level_ref, weight_ref, grad_ref, row_ref
):
    step = pl.program_id(0)
    width = vocab_ref.shape[1]

    @pl.when(step == 0)
    def _():
        row_ref[...] = jnp.zeros_like(row_ref)

    grad_ref[...] = jnp.zeros_like(grad_ref)
    places = logit_places(step, rows_in, width)
    inside = step * width + lax.broadcasted_iota(jnp.int32, (1, width), 1) < rows_in
    table = jnp.where(inside, vocab_ref[...], jnp.zeros_like(vocab_ref[...]))

    def one(index, carry):
        rows = pl.ds(pl.multiple_of(index * TILE, TILE), TILE)
        hit = (places == id_ref[rows, :]).astype(jnp.float32)
        grads = (jnp.exp(logit_ref[rows, :] - level_ref[rows, :]) - hit) * weight_ref[rows, :]
        grads = jnp.where(places < rows_in, grads, 0.0).astype(jnp.bfloat16)
        grad_ref[rows, :] = grads
        row_ref[rows, :] = row_ref[rows, :] + dot_nt(grads, table)
        return carry

    lax.fori_loop(0, tiles_ref[0], one, 0)


def logit_grads(logits, vocab, ids, tiles, levels, weights):
    count, rows_in = logits.shape
    width = 4 * TILE
    block = pl.BlockSpec((count, width), lambda i, *_: (0, i))
    return pl.pallas_call(
        lambda *refs: logit_grad_kernel(rows_in, *refs),
        grid_spec=pltpu.PrefetchScalarGridSpec(
            num_scalar_prefetch=1,
            grid=(pl.cdiv(rows_in, width),),
            in_specs=[
                block,
                pl.BlockSpec((MODEL_WIDTH, width), lambda i, *_: (0, i)),
                whole_block((count, 1)),
                whole_block((count, 1)),
                whole_block((count, 1)),
            ],
            out_specs=[block, whole_block((count, MODEL_WIDTH))],
        ),
        out_shape=[
            jax.ShapeDtypeStruct((count, rows_in), jnp.bfloat16),
            jax.ShapeDtypeStruct((count, MODEL_WIDTH), jnp.float32),
        ],
        compiler_params=pltpu.CompilerParams(vmem_limit_bytes=40 << 20),
        cost_estimate=cost(2 * count * rows_in * MODEL_WIDTH, 40 << 20, count * rows_in),
        name="logit_grads",
    )(tiles, logits, vocab, ids, levels[:, None], weights[:, None])


def packing(lengths, room):
    ends = jnp.cumsum(lengths)
    starts = ends - lengths
    places = jnp.arange(room, dtype=jnp.int32)
    segment = jnp.sum((places[:, None] >= ends[None, :]).astype(jnp.int32), axis=1)
    inside = segment[:, None] == jnp.arange(lengths.shape[0], dtype=jnp.int32)[None, :]
    position = places - jnp.sum(jnp.where(inside, starts[None, :], 0), axis=1)
    return segment, position, jnp.minimum(starts, room), jnp.minimum(ends, room)


def key_span(query_segment, query_total, key_starts, key_ends):
    number = key_starts.shape[0]
    count = query_segment.shape[0] // TILE
    begins = jnp.arange(count, dtype=jnp.int32) * TILE
    last_real = jnp.clip(query_total - 1, 0, query_segment.shape[0] - 1)
    finals = jnp.minimum(begins + TILE - 1, last_real)

    def pick(table, places):
        chosen = jnp.sum(
            jnp.where(
                jnp.arange(query_segment.shape[0], dtype=jnp.int32)[None, :] == places[:, None],
                query_segment[None, :],
                0,
            ),
            axis=1,
        )
        return jnp.sum(
            jnp.where(
                chosen[:, None] == jnp.arange(number, dtype=jnp.int32)[None, :], table[None, :], 0
            ),
            axis=1,
        )

    some = begins < query_total
    first = jnp.where(some, pick(key_starts, begins) // TILE, 0)
    last = jnp.where(some, (pick(key_ends, finals) + TILE - 1) // TILE, 0)
    return first, jnp.maximum(first, last)


def packed_gradients(
    source_stream, target_stream, gain_rows, biases, weights, later, layout, head, column_start, column_width
):
    enc_attention, enc_feed = weights[:3], weights[3:]
    (
        source_span,
        target_span,
        cross_span,
        source_row,
        source_column,
        target_row,
        target_column,
    ) = layout
    bias_source, bias_target = biases

    def shard(grad, which=0):
        return lax.dynamic_slice_in_dim(grad, which * MODEL_WIDTH + column_start, column_width, 1)

    def attention(stream, gain_row, context, matrices, span, row, column, causal, bias):
        to_query, to_pair, outward = matrices
        normed = root_norm(stream, gain_row).astype(jnp.bfloat16)
        context = normed if context is None else context
        queries = dot(normed, to_query).astype(jnp.bfloat16)
        pair_rows = dot(context, to_pair).astype(jnp.bfloat16)
        attended, levels = packed_forward(queries, pair_rows, span, row, column, causal, bias)
        return stream + dot(attended, outward), (
            normed,
            context,
            queries,
            pair_rows,
            attended,
            levels,
        )

    def attention_back(grad, stream, gain_row, crossed, matrices, saved, span, row, column, causal, bias):
        to_query, to_pair, outward = matrices
        normed, context, queries, pair_rows, attended, levels = saved
        branch = grad.astype(jnp.bfloat16)
        arriving = dot_nt(branch, outward).astype(jnp.bfloat16)
        grads = packed_backward(
            queries, arriving, pair_rows, levels, span, row, column, causal, bias
        )
        grad_queries, grad_pair = grads[:2]
        pair_shards = [shard(grad_pair), shard(grad_pair, 1)]
        if crossed:
            shares = [
                dot_tn(shard(grad_queries), normed),
                dot_tn(jnp.concatenate(pair_shards, axis=1), context),
                dot_tn(shard(branch), attended),
            ]
        else:
            shares = [
                dot_tn(jnp.concatenate([shard(grad_queries)] + pair_shards, axis=1), normed),
                dot_tn(shard(branch), attended),
            ]
        grad_normed = dot_nt(grad_queries, to_query)
        grad_context = dot_nt(grad_pair, to_pair)
        if not crossed:
            grad_normed = grad_normed + grad_context
        grad_input, grad_gain = norm_backward(stream, gain_row, grad_normed)
        return grad + grad_input, grad_gain, shares, grads[2:], grad_context

    def feed(stream, gain_row, matrices):
        inward, outward = matrices
        normed = root_norm(stream, gain_row).astype(jnp.bfloat16)
        inner = dot(normed, inward)
        hidden = jax.nn.gelu(inner).astype(jnp.bfloat16)
        return stream + dot(hidden, outward), (normed, inner, hidden)

    def feed_back(grad, stream, gain_row, matrices, saved):
        inward, outward = matrices
        normed, inner, hidden = saved
        branch = grad.astype(jnp.bfloat16)
        grad_inner = jax.vjp(jax.nn.gelu, inner)[1](dot_nt(branch, outward))[0].astype(jnp.bfloat16)
        grad_normed = dot_nt(grad_inner, inward)
        inner_shards = jnp.concatenate([shard(grad_inner, j) for j in range(4)], axis=1)
        outward_shares = dot_tn(shard(branch), hidden)
        shares = [dot_tn(inner_shards, normed)] + [
            outward_shares[:, j * MODEL_WIDTH : (j + 1) * MODEL_WIDTH] for j in range(4)
        ]
        grad_input, grad_gain = norm_backward(stream, gain_row, grad_normed)
        return grad + grad_input, grad_gain, shares

    x1, enc_saved = attention(
        source_stream, gain_rows[0], None, enc_attention, source_span, source_row, source_column, False, bias_source
    )
    x1, dec_self, dec_cross, dec_feed = later(x1)
    x2, enc_feed_saved = feed(x1, gain_rows[1], enc_feed)
    encoded = root_norm(x2, gain_rows[2]).astype(jnp.bfloat16)
    encoded, target_stream = lax.optimization_barrier((encoded, target_stream))
    target_stream = target_stream.astype(jnp.float32)
    y1, self_saved = attention(
        target_stream, gain_rows[3], None, dec_self, target_span, target_row, target_column, True, bias_target
    )
    y2, cross_saved = attention(
        y1, gain_rows[4], encoded, dec_cross, cross_span, target_row, source_column, False, None
    )
    y3, dec_feed_saved = feed(y2, gain_rows[5], dec_feed)
    final_rows = (root_norm(y3, gain_rows[6]) * MODEL_WIDTH ** (-0.5)).astype(jnp.bfloat16)

    grad_final, grad_logits, token_loss = head(final_rows)

    grad, gain_final = norm_backward(y3, gain_rows[6], grad_final * MODEL_WIDTH ** (-0.5))
    grad, gain_feed, feed_shares = feed_back(grad, y2, gain_rows[5], dec_feed, dec_feed_saved)
    grad, gain_cross, cross_shares, _, grad_encoded = attention_back(
        grad, y1, gain_rows[4], True, dec_cross, cross_saved, cross_span, target_row, source_column, False, None
    )
    target_grad, gain_self, self_shares, table_target, _ = attention_back(
        grad, target_stream, gain_rows[3], False, dec_self, self_saved, target_span, target_row, target_column, True, bias_target
    )
    grad, gain_encoded = norm_backward(x2, gain_rows[2], grad_encoded)
    grad, gain_enc_feed, enc_feed_shares = feed_back(grad, x1, gain_rows[1], enc_feed, enc_feed_saved)
    source_grad, gain_enc, enc_shares, table_source, _ = attention_back(
        grad, source_stream, gain_rows[0], False, enc_attention, enc_saved, source_span, source_row, source_column, False, bias_source
    )
    gains = jnp.stack(
        [gain_enc, gain_enc_feed, gain_encoded, gain_self, gain_cross, gain_feed, gain_final]
    )
    tables = jnp.stack(
        [
            bias_grad(table_source[0], False),
            bias_grad(table_target[0], True),
        ]
    )
    shares = jnp.concatenate(
        enc_shares + enc_feed_shares + self_shares + cross_shares + feed_shares
    ).reshape(-1, column_width, MODEL_WIDTH)
    return shares, gains, tables, source_grad, target_grad, final_rows, grad_logits, token_loss


def orthonormal_kernel(factor_ref, out_ref):
    rank = factor_ref.shape[0]
    for r in range(rank):
        out_ref[r] = factor_ref[r]
    for r in range(rank):
        row = out_ref[r]
        row = row * lax.rsqrt(jnp.sum(row * row, axis=-1, keepdims=True))
        out_ref[r] = row
        for s in range(r + 1, rank):
            other = out_ref[s]
            out_ref[s] = other - row * jnp.sum(row * other, axis=-1, keepdims=True)


def orthonormal_rows(factor):
    return pl.pallas_call(
        orthonormal_kernel,
        out_shape=jax.ShapeDtypeStruct(factor.shape, jnp.float32),
        name="orthonormal",
    )(factor)


def local(
    source_ids,
    targets,
    source_lengths,
    target_lengths,
    task_ids,
    task_counts,
    blocks,
    blocks_momentum,
    embedding,
    embed_momentum,
    gain_rows,
    gain_momentum,
    position_bias,
    bias_momentum,
    right_blocks,
    right_embed,
    error_blocks,
    error_embed,
):
    fsdp_rank = lax.axis_index("fsdp")
    cuts_rank = lax.axis_index("cuts")
    cuts_count = lax.axis_size("cuts")
    seq_count, source_len = source_ids.shape
    target_len = targets.shape[1]
    number = seq_count * lax.axis_size("fsdp")
    room_source = min(ROOM_SOURCE, source_len * number)
    room_target = min(ROOM_TARGET, target_len * number)
    fewest = min(room_source // source_len, room_target // target_len)
    shares_of = sorted({number, -(-number // 2), fewest}, reverse=True)
    vocab_rows = embedding.shape[0]
    vocab_start = fsdp_rank * vocab_rows
    once = (fsdp_rank == 0).astype(jnp.float32)

    stored_vocab = embedding.T.astype(jnp.bfloat16)
    steps = len(spread_ways())
    bands = max(n for n in range(1, max(steps, 1) + 1) if stored_vocab.shape[0] % (16 * n) == 0 or n == 1)
    vocab_shares = spread_begin(stored_vocab.reshape(bands, -1, vocab_rows))
    stored = jnp.transpose(blocks, (1, 0, 2)).astype(jnp.bfloat16)
    group = lax.all_gather(
        jnp.concatenate(
            [source_ids, targets, source_lengths[:, None], target_lengths[:, None]], axis=1
        ),
        "fsdp",
        axis=0,
        tiled=True,
    )
    group_source = group[:, :source_len]
    group_target = group[:, source_len : source_len + target_len]
    lengths = group[:, -2:]

    def fullest(share):
        padded = jnp.pad(lengths, ((0, -number % share), (0, 0)))
        return jnp.max(jnp.sum(padded.reshape(-1, share, 2), axis=1), axis=0)

    needs = lax.all_gather(
        jnp.concatenate([jnp.sum(lengths, axis=0)] + [fullest(share) for share in shares_of]),
        "cuts",
        axis=0,
    )
    for step in range(steps):
        if step:
            vocab_shares, needs = spread_tied(vocab_shares, needs)
        vocab_shares = spread_step(vocab_shares, step)
    stored, needs = lax.optimization_barrier((stored, needs))
    first_columns = jnp.concatenate(gather_fsdp(stored[:12], fsdp_rank), axis=2)
    errors = jnp.transpose(error_blocks[0], (1, 2, 0))
    biases = (bias_tiles(False, position_bias[0]), bias_tiles(True, position_bias[1]))
    vocab_shares, first_columns, biases = spread_tied(vocab_shares, first_columns, biases)
    first_shares = spread_begin(first_columns)
    first_shares = spread_step(first_shares, 0) if steps else first_shares
    vocab_pieces = spread_end(vocab_shares)
    piece_arrays = [[array for _, array in held] for _, held in vocab_pieces]
    first_arrays = [array for _, array in first_shares]
    given = (group, needs, piece_arrays, first_arrays, stored[12:], errors, biases)

    def one_round(state):
        _, turn, _, _, left_blocks, left_embed, gains_sum, table_sum, loss_sum = state
        turn, group, needs, piece_arrays, first_arrays, stored_rest, errors, biases = (
            lax.optimization_barrier((turn, *given))
        )
        group_source = group[:, :source_len]
        group_target = group[:, source_len : source_len + target_len]
        lengths = group[:, -2:]
        total_count = jnp.sum(needs[:, 1]).astype(jnp.float32)
        most = jnp.max(needs[:, 2:], axis=0)
        share = jnp.int32(shares_of[-1])
        for index in range(len(shares_of) - 2, -1, -1):
            fits = (most[2 * index] <= room_source) & (most[2 * index + 1] <= room_target)
            share = jnp.where(fits, shares_of[index], share)
        members = jnp.arange(number, dtype=jnp.int32)
        taken = (members >= turn * share) & (members < (turn + 1) * share)
        source_taken = jnp.where(taken, lengths[:, 0], 0)
        target_taken = jnp.where(taken, lengths[:, 1], 0)
        more = (turn + 1) * share < number

        chosen = jnp.sum(
            jnp.where(
                task_ids[:, None] == jnp.arange(TASKS, dtype=jnp.int32)[None, :],
                task_counts[None, :],
                0,
            ),
            axis=1,
        ).astype(jnp.float32)
        slice_weight = jnp.sum(
            jnp.where(
                jnp.arange(cuts_count, dtype=jnp.int32) == cuts_rank,
                cuts_count * chosen / jnp.sum(chosen),
                0.0,
            )
        )

        pieces = [
            (first, [(bits, array) for (bits, _), array in zip(held, own)])
            for (first, held), own in zip(vocab_pieces, piece_arrays)
        ]
        (vocab,) = place_pieces(pieces, ((tuple(range(bands)), "mixed"),), cuts_rank)
        shares = [(bits, array) for (bits, _), array in zip(first_shares, first_arrays)]
        rest_parts = [stored_rest] + [
            shifted(stored_rest, distance) for distance in range(1, lax.axis_size("fsdp"))
        ]
        for step in range(1, steps):
            shares = spread_step(shares, step)

        def attention_groups(first):
            return (
                ((first,), "columns"),
                ((first + 1, first + 2), "columns"),
                ((first + 3,), "columns"),
            )

        def feed_groups(first):
            return (
                (tuple(range(first, first + 4)), "columns"),
                (tuple(range(first + 4, first + 8)), "rows"),
            )

        source_segment, source_place, source_starts, source_ends = packing(source_taken, room_source)
        target_segment, target_place, target_starts, target_ends = packing(target_taken, room_target)
        source_real = source_segment < number
        target_real = target_segment < number
        packed_source = jnp.take(
            group_source.reshape(-1),
            jnp.where(source_real, source_segment * source_len + source_place, 0),
        )
        group_input = jnp.concatenate(
            [jnp.zeros_like(group_target[:, :1]), group_target[:, :-1]], axis=1
        )
        target_from = jnp.where(target_real, target_segment * target_len + target_place, 0)
        packed_target = jnp.take(group_target.reshape(-1), target_from)
        packed_input = jnp.take(group_input.reshape(-1), target_from)
        packed_ids = jnp.concatenate([packed_source, packed_input])
        packed_real = jnp.concatenate([source_real, target_real])
        local_ids = jnp.where(packed_real, packed_ids - vocab_start, -1)
        source_total, target_total = jnp.sum(source_taken), jnp.sum(target_taken)
        chunk = 2 * TILE
        local_ids = jnp.pad(local_ids, (0, -local_ids.shape[0] % chunk), constant_values=-1)
        spans = jnp.stack(
            [
                jnp.minimum((source_total + chunk - 1) // chunk, room_source // chunk),
                jnp.int32(room_source // chunk),
                jnp.minimum(
                    (room_source + target_total + chunk - 1) // chunk,
                    local_ids.shape[0] // chunk,
                ),
            ]
        )
        rows = lookup_rows(local_ids, spans, vocab)
        shares, rows, rest_parts = spread_tied(shares, rows, rest_parts)
        rest_columns = jnp.concatenate(in_order(rest_parts, fsdp_rank), axis=2)
        rest_shares, rows = spread_tied(spread_begin(rest_columns), rows)
        if steps:
            rest_shares = spread_step(rest_shares, 0)
        first_placed = place_pieces(
            spread_end(shares), attention_groups(0) + feed_groups(4), cuts_rank
        )
        sizes = [room_source * part // 10 for part in (4, 5, 6, 7, 8, 10)]
        fullest_source = jnp.int32(room_source)
        for index in range(len(shares_of) - 1, -1, -1):
            fullest_source = jnp.where(share == shares_of[index], most[2 * index], fullest_source)
        source_rows = lax.switch(
            sum((fullest_source > size).astype(jnp.int32) for size in sizes[:-1]),
            [
                lambda table, size=size: jnp.pad(
                    lax.psum(table[:size], "fsdp"), ((0, room_source - size), (0, 0))
                )
                for size in sizes
            ],
            rows[:room_source],
        )
        rest_shares, source_rows, target_rows = spread_tied(
            rest_shares, source_rows, rows[room_source : room_source + room_target]
        )
        for step in range(1, steps - 1):
            rest_shares = spread_step(rest_shares, step)
        rest_arriving = spread_send(rest_shares, steps - 1) if steps > 1 else []

        def decoder_weights(stream):
            shares, arriving, stream = spread_tied(rest_shares, rest_arriving, stream)
            if steps > 1:
                shares = spread_receive(shares, arriving, steps - 1)
            pieces = spread_end(shares)
            attentions = place_pieces(pieces, attention_groups(0) + attention_groups(4), cuts_rank)
            feeds = place_pieces(pieces, feed_groups(8), cuts_rank)
            return stream, attentions[:3], attentions[3:], feeds

        target_rows = lax.psum(target_rows, "fsdp")
        source_stream = source_rows.astype(jnp.float32)
        target_stream = target_rows
        layout = (
            key_span(source_segment, source_total, source_starts, source_ends),
            key_span(target_segment, target_total, target_starts, target_ends),
            key_span(target_segment, target_total, source_starts, source_ends),
            source_segment[None, :],
            source_segment[:, None],
            target_segment[None, :],
            target_segment[:, None],
        )

        token_mask = target_real.astype(jnp.float32)
        token_weight = token_mask * (slice_weight / total_count)
        target_ids = (packed_target - vocab_start)[:, None]
        target_tiles = ((target_total + TILE - 1) // TILE)[None]

        def head(final_rows):
            logits, own_stats = logit_stats(final_rows, vocab, target_ids, target_tiles)
            stats = lax.all_gather(own_stats[:, :3].T, "fsdp", axis=0)
            top = jnp.max(stats[:, 0], axis=0)
            log_total = top + jnp.log(
                jnp.sum(stats[:, 1] * jnp.exp(stats[:, 0] - top[None, :]), axis=0)
            )
            token_loss = (log_total - jnp.sum(stats[:, 2], axis=0)) * token_mask
            grad_logits, grad_rows = logit_grads(
                logits, vocab, target_ids, target_tiles, log_total, token_weight
            )
            grad_rows = sum_fsdp(grad_rows, fsdp_rank)
            return grad_rows, grad_logits, token_loss

        shares, gains, table_found, source_grad, target_grad, final_rows, grad_logits, token_loss = (
            packed_gradients(
                source_stream,
                target_stream,
                gain_rows,
                biases,
                first_placed,
                decoder_weights,
                layout,
                head,
                fsdp_rank * blocks.shape[2],
                blocks.shape[2],
            )
        )
        lookups = jnp.concatenate([source_grad, target_grad]).astype(jnp.bfloat16)
        lookups = jnp.pad(lookups, ((0, local_ids.shape[0] - lookups.shape[0]), (0, 0)))
        left_embed = vocab_grad(
            error_embed[0], left_embed, turn, local_ids, spans, lookups, grad_logits, final_rows
        )
        before = jnp.where(turn == 0, errors, left_blocks)
        return (
            more,
            turn + 1,
            total_count,
            slice_weight,
            before + shares,
            left_embed,
            gains_sum + gains,
            table_sum + table_found,
            loss_sum + jnp.sum(token_loss),
        )

    zero = jnp.zeros((), jnp.float32)
    _, _, total_count, slice_weight, left_blocks, left_embed, gains_grad, table_grad, loss_local = (
        lax.while_loop(
            lambda state: state[0],
            one_round,
            (
                jnp.ones((), jnp.bool_),
                jnp.zeros((), jnp.int32),
                zero,
                zero,
                unset((blocks.shape[1], blocks.shape[2], MODEL_WIDTH)),
                unset((vocab_rows, MODEL_WIDTH)),
                jnp.zeros_like(gain_rows),
                jnp.zeros_like(position_bias),
                zero,
            ),
        )
    )

    left_factor = jnp.einsum("kji,kjr->rki", left_blocks, right_blocks, precision=lax.Precision.HIGH)
    embed_factor = jnp.einsum("vd,vr->rd", left_embed, right_embed, precision=lax.Precision.HIGH)
    rank, count = left_factor.shape[:2]
    small = jnp.concatenate(
        [
            gains_grad * once,
            (table_grad * once).reshape(-1, MODEL_WIDTH),
            jnp.full((1, MODEL_WIDTH), loss_local * slice_weight * once),
        ]
    )
    factor = jnp.concatenate([left_factor, embed_factor[:, None]], axis=1)
    packed = jnp.concatenate([factor.reshape(-1, MODEL_WIDTH), small])
    packed = jnp.pad(packed, ((0, -packed.shape[0] % (8 * cuts_count)), (0, 0)))
    packed = sum_everywhere(packed, cuts_rank)
    factor = packed[: rank * (count + 1)].reshape(factor.shape)
    small = packed[rank * (count + 1) :]
    gains_grad = small[: gain_rows.shape[0]]
    table_rows = position_bias.size // MODEL_WIDTH
    table_grad = small[gain_rows.shape[0] :][:table_rows].reshape(position_bias.shape)
    loss_total = small[gain_rows.shape[0] + table_rows, 0]
    factor = orthonormal_rows(factor)
    left_factor, embed_factor = factor[:, :-1], factor[:, -1]
    factors_blocks = jnp.einsum("kji,rki->rkj", left_blocks, left_factor, precision=lax.Precision.DEFAULT)
    factors_embed = jnp.einsum("vd,rd->rv", left_embed, embed_factor, precision=lax.Precision.DEFAULT)
    both = sum_cuts(jnp.concatenate([factors_blocks.reshape(rank, -1), factors_embed], axis=1))
    factors_embed = both[:, -vocab_rows:]
    factors_blocks = both[:, :-vocab_rows].reshape(factors_blocks.shape)
    gram_blocks = jnp.einsum("rki,ski->krs", left_factor, left_factor, precision=TOP_PRECISION)
    gram_embed = jnp.einsum("rd,sd->rs", embed_factor, embed_factor, precision=TOP_PRECISION)
    squares = jnp.sum(
        factors_blocks
        * jnp.einsum("krs,skj->rkj", gram_blocks, factors_blocks, precision=lax.Precision.HIGH)
    ) + jnp.sum(factors_embed * jnp.dot(gram_embed, factors_embed, precision=lax.Precision.HIGH))
    squares = lax.psum(squares, "fsdp")
    full_blocks = jnp.einsum("rki,rkj->kji", left_factor, factors_blocks, precision=lax.Precision.DEFAULT)
    full_embed = jnp.einsum("rv,rd->vd", factors_embed, embed_factor, precision=lax.Precision.DEFAULT)
    owned_rows = blocks.shape[0]
    owned_columns = embedding.shape[1]
    own_left = lax.dynamic_slice_in_dim(left_factor, cuts_rank * owned_rows, owned_rows, 2)
    own_right = lax.dynamic_slice_in_dim(embed_factor, cuts_rank * owned_columns, owned_columns, 1)
    own_blocks = jnp.einsum("rki,rkj->ikj", own_left, factors_blocks, precision=lax.Precision.DEFAULT)
    own_embed = jnp.einsum("rv,rd->vd", factors_embed, own_right, precision=lax.Precision.DEFAULT)
    small_squares = jnp.sum(gains_grad * gains_grad) + jnp.sum(table_grad * table_grad)
    grad_norm = jnp.sqrt(squares + small_squares)
    clip_factor = jnp.minimum(1.0, CLIP_NORM / grad_norm)
    step_size = STEP_RATE * math.sqrt(PARAMS / MODEL_WIDTH) / CLIP_NORM
    embed_step = step_size * EMBED_SHARE * math.sqrt(MODEL_WIDTH)
    small_step = step_size * SMALL_SHARE * math.sqrt(MODEL_WIDTH)
    momentum_blocks = MOMENTUM_DECAY * blocks_momentum + (1.0 - MOMENTUM_DECAY) * (
        clip_factor * own_blocks
    )
    momentum_embed = MOMENTUM_DECAY * embed_momentum + (1.0 - MOMENTUM_DECAY) * (
        clip_factor * own_embed
    )
    momentum_gains = MOMENTUM_DECAY * gain_momentum + (1.0 - MOMENTUM_DECAY) * (
        clip_factor * gains_grad
    )
    momentum_bias = MOMENTUM_DECAY * bias_momentum + (1.0 - MOMENTUM_DECAY) * (
        clip_factor * table_grad
    )
    return (
        loss_total,
        total_count,
        grad_norm,
        blocks - step_size * momentum_blocks,
        momentum_blocks,
        embedding - embed_step * momentum_embed,
        momentum_embed,
        gain_rows - small_step * momentum_gains,
        momentum_gains,
        position_bias - small_step * momentum_bias,
        momentum_bias,
        jnp.transpose(factors_blocks, (1, 2, 0)),
        factors_embed.T,
        jnp.transpose(left_blocks - full_blocks, (2, 0, 1))[None],
        (left_embed - full_embed)[None],
    )


def solution(mesh):
    return jax.shard_map(
        local,
        mesh=mesh,
        in_specs=(
            P(("cuts", "fsdp"), None),
            P(("cuts", "fsdp"), None),
            P(("cuts", "fsdp")),
            P(("cuts", "fsdp")),
            P(),
            P(),
            P("cuts", None, "fsdp"),
            P("cuts", None, "fsdp"),
            P("fsdp", "cuts"),
            P("fsdp", "cuts"),
            P(),
            P(),
            P(),
            P(),
            P(None, "fsdp", None),
            P("fsdp", None),
            P("cuts", None, None, "fsdp"),
            P("cuts", "fsdp", None),
        ),
        out_specs=(
            P(),
            P(),
            P(),
            P("cuts", None, "fsdp"),
            P("cuts", None, "fsdp"),
            P("fsdp", "cuts"),
            P("fsdp", "cuts"),
            P(),
            P(),
            P(),
            P(),
            P(None, "fsdp", None),
            P("fsdp", None),
            P("cuts", None, None, "fsdp"),
            P("cuts", "fsdp", None),
        ),
        check_vma=False,
    )
```

```python
import itertools
import math

import jax
import jax.numpy as jnp
from jax import lax
from jax.experimental import pallas as pl
from jax.experimental.layout import Layout, with_layout_constraint
from jax.experimental.pallas import tpu as pltpu
from jax.sharding import PartitionSpec as P

MODEL_WIDTH = 768
H = 12
DH = 64
FEED_UNITS = 3072
NBK = 32
TASKS = 8
PARAMS = 41189376


EPSILON = 1e-06
MASKED = -1000000000.0
CLIP_NORM = 0.05
MOMENTUM_DECAY = 0.9
STEP_RATE = 5.0
EMBED_SHARE = 50.0
SMALL_SHARE = 1.0 / 7.0
TOP_PRECISION = lax.Precision.HIGHEST
TILE = 128
ROOM_SOURCE = 1280
ROOM_TARGET = 384
ENCODER_EDGES = (12, 16, 23, 32, 46, 64, 91)
DECODER_EDGES = (19, 21, 24, 27, 31, 35, 40, 46, 52, 59, 67, 77, 87, 99, 113)


def root_norm(stream, gain_row):
    return (
        stream * lax.rsqrt(jnp.mean(stream * stream, axis=-1, keepdims=True) + EPSILON) * gain_row
    )


def norm_backward(stream, gain_row, grad_normed):
    _, pull_back = jax.vjp(root_norm, stream, gain_row)
    return pull_back(grad_normed)


def dot(left, right):
    return jnp.dot(left, right, preferred_element_type=jnp.float32)


def dot_nt(left, right):
    return lax.dot_general(left, right, (((1,), (1,)), ((), ())), preferred_element_type=jnp.float32)


def dot_tn(left, right):
    return lax.dot_general(left, right, (((0,), (0,)), ((), ())), preferred_element_type=jnp.float32)


def exchange(array, mask):
    return lax.ppermute(array, "cuts", [(i, i ^ mask) for i in range(lax.axis_size("cuts"))])


def shifted(array, distance):
    count = lax.axis_size("fsdp")
    return lax.ppermute(array, "fsdp", [(i, (i + distance) % count) for i in range(count)])


def in_order(pieces, rank):
    count = len(pieces)
    ordered = []
    for place in range(count):
        chosen = pieces[-place % count]
        for own in range(1, count):
            chosen = jnp.where(rank == own, pieces[(own - place) % count], chosen)
        ordered.append(chosen)
    return ordered


def gather_fsdp(part, rank):
    count = lax.axis_size("fsdp")
    return in_order([part] + [shifted(part, distance) for distance in range(1, count)], rank)


def sum_fsdp(part, rank):
    count = lax.axis_size("fsdp")
    rows = part.shape[0] // count
    low = part.astype(jnp.bfloat16)
    total = lax.dynamic_slice_in_dim(part, rank * rows, rows, 0)
    for distance in range(1, count):
        piece = lax.dynamic_slice_in_dim(low, (rank + distance) % count * rows, rows, 0)
        total = total + shifted(piece, distance).astype(jnp.float32)
    return jnp.concatenate(gather_fsdp(total.astype(jnp.bfloat16), rank), axis=0).astype(jnp.float32)


def sum_everywhere(part, cuts_rank):
    count = lax.axis_size("cuts")
    masks = [1 << bit for bit in range(count.bit_length() - 1)]
    if count & (count - 1) or part.shape[0] % count:
        return lax.psum(part, ("cuts", "fsdp"))
    bits = [(cuts_rank // mask) % 2 for mask in masks]
    for mask, bit in zip(masks, bits):
        half = part.shape[0] // 2
        away = lax.dynamic_slice_in_dim(part, (1 - bit) * half, half, 0)
        part = lax.dynamic_slice_in_dim(part, bit * half, half, 0) + exchange(away, mask)
    part = jnp.sum(lax.all_gather(part, "fsdp", axis=0), axis=0)
    for mask, bit in zip(masks[::-1], bits[::-1]):
        other = exchange(part, mask)
        part = jnp.where(
            bit == 1, jnp.concatenate([other, part], axis=0), jnp.concatenate([part, other], axis=0)
        )
    return part


def sum_cuts(part):
    count = lax.axis_size("cuts")
    if count & (count - 1):
        return lax.psum(part.astype(jnp.bfloat16), "cuts").astype(jnp.float32)
    for bit in range(count.bit_length() - 1):
        low = part.astype(jnp.bfloat16)
        part = low.astype(jnp.float32) + exchange(low, 1 << bit).astype(jnp.float32)
    return part


def spread_ways():
    return [1 << bit for bit in range(1, lax.axis_size("cuts").bit_length() - 1)]


def spread_begin(part):
    number = max(min(len(spread_ways()), part.shape[0]), 1)
    ends = [part.shape[0] * turn // number for turn in range(number + 1)]
    return [([0], part[None, begin:end]) for begin, end in zip(ends, ends[1:])]


def spread_send(shares, step):
    ways = spread_ways()
    return [
        exchange(held, ways[(turn + step) % len(ways)]) for turn, (_, held) in enumerate(shares)
    ]


def spread_receive(shares, arriving, step):
    ways = spread_ways()
    after = []
    for turn, ((bits, held), array) in enumerate(zip(shares, arriving)):
        mask = ways[(turn + step) % len(ways)]
        after.append((bits + [bit ^ mask for bit in bits], jnp.concatenate([held, array])))
    return after


def spread_step(shares, step):
    return spread_receive(shares, spread_send(shares, step), step)


def spread_end(shares):
    found, first = [], 0
    for bits, held in shares:
        found.append((first, [(bits, held), ([bit ^ 1 for bit in bits], exchange(held, 1))]))
        first += held.shape[1]
    return found


def spread_tied(shares, *others):
    arrays, others = lax.optimization_barrier(([held for _, held in shares], others))
    return [(bits, held) for (bits, _), held in zip(shares, arrays)], *others


def cost(flops, moved, powers=0):
    return pl.CostEstimate(flops=int(flops), bytes_accessed=int(moved), transcendentals=int(powers))


def place_kernel(moves, number, rank_ref, *refs):
    sources, outs, sem = refs[:number], refs[number:-1], refs[-1]
    rank = rank_ref[0]
    copies = []
    for source, piece, index, bits, (out, pitch, row, column), shape in moves:
        rows = pl.ds(pl.multiple_of((rank ^ bits) * pitch + row, 16), shape[0])
        copies.append(
            pltpu.make_async_copy(
                sources[source].at[piece, index],
                outs[out].at[rows, pl.ds(column, shape[1])],
                sem.at[len(copies)],
            )
        )
    for copy in copies:
        copy.start()
    for copy in copies:
        copy.wait()


def place_pieces(found, groups, rank):
    count = lax.axis_size("cuts")
    height, width = found[0][1][0][1].shape[2:]
    where = {}
    shapes = []
    for out, (members, how) in enumerate(groups):
        for order, matrix in enumerate(members):
            row = {"columns": 0, "rows": order * count * height, "mixed": order * height}[how]
            pitch = height * (len(members) if how == "mixed" else 1)
            where[matrix] = (out, pitch, row, order * width if how == "columns" else 0)
        tall, wide = (1, len(members)) if how == "columns" else (len(members), 1)
        shapes.append((tall * count * height, wide * width))
    sources, moves = [], []
    for first, held in found:
        for bits, array in held:
            for piece, index in itertools.product(range(array.shape[0]), range(array.shape[1])):
                if first + index in where:
                    moves.append(
                        (len(sources), piece, index, bits[piece], where[first + index], (height, width))
                    )
            sources.append(array)
    space = pl.BlockSpec(memory_space=pl.ANY)
    return pl.pallas_call(
        lambda *refs: place_kernel(moves, len(sources), *refs),
        in_specs=[pl.BlockSpec(memory_space=pltpu.SMEM)] + [space] * len(sources),
        out_specs=[pl.BlockSpec(memory_space=pltpu.VMEM)] * len(shapes),
        out_shape=[jax.ShapeDtypeStruct(shape, sources[0].dtype) for shape in shapes],
        scratch_shapes=[pltpu.SemaphoreType.DMA((len(moves),))],
        compiler_params=pltpu.CompilerParams(vmem_limit_bytes=40 << 20),
        cost_estimate=cost(0, 5 * sum(math.prod(shape) for shape in shapes)),
        name="place",
    )(rank[None], *sources)


def unset_kernel(out_ref):
    pass


def unset(shape):
    return pl.pallas_call(
        unset_kernel,
        out_specs=pl.BlockSpec(memory_space=pl.ANY),
        out_shape=jax.ShapeDtypeStruct(shape, jnp.float32),
        name="unset",
    )()


PAIRS = H // 2
WIDE = 2 * TILE


def offset_buckets(causal, offset):
    if causal:
        distance = jnp.maximum(-offset, 0)
        farther = 16 + sum(((distance >= boundary).astype(jnp.int32) for boundary in DECODER_EDGES))
        bucket = jnp.where(distance < 16, distance, farther)
    else:
        distance = jnp.abs(offset)
        farther = 8 + sum(((distance >= boundary).astype(jnp.int32) for boundary in ENCODER_EDGES))
        bucket = jnp.where(distance < 8, distance, farther) + jnp.where(offset > 0, 16, 0)
    return (bucket[..., None] == jnp.arange(NBK, dtype=jnp.int32)).astype(jnp.float32)


def bias_kernel(row_ref, out_ref):
    for head in range(H):
        row = jnp.broadcast_to(row_ref[0, head : head + 1, :], (TILE, WIDE))
        tile = pltpu.roll(row, 0, 1, stride=1, stride_axis=0)[:, :TILE]
        out_ref[0, head // 2, :, (head % 2) * TILE : (head % 2 + 1) * TILE] = tile


def bias_tiles(causal, table):
    lane = jnp.arange(WIDE, dtype=jnp.int32)
    offset = (jnp.arange(5, dtype=jnp.int32)[:, None] - 2) * TILE + jnp.where(
        lane < TILE, -lane, WIDE - lane
    )
    rows = jnp.einsum(
        "tqb,bh->thq", offset_buckets(causal, offset), table, precision=TOP_PRECISION
    )
    return pl.pallas_call(
        bias_kernel,
        grid=(5,),
        in_specs=[pl.BlockSpec((1, 16, WIDE), lambda i: (i, 0, 0))],
        out_specs=pl.BlockSpec((1, PAIRS, TILE, WIDE), lambda i: (i, 0, 0, 0)),
        out_shape=jax.ShapeDtypeStruct((5, PAIRS, TILE, WIDE), jnp.float32),
        name="bias",
    )(jnp.pad(rows, ((0, 0), (0, 16 - H), (0, 0))))


def bias_grad(tiles, causal):
    places = jnp.arange(TILE, dtype=jnp.int32)
    offset = (
        (jnp.arange(5, dtype=jnp.int32)[:, None, None] - 2) * TILE
        + places[None, :, None]
        - places[None, None, :]
    )
    hot = offset_buckets(causal, offset)
    found = [
        jnp.einsum("tpkq,tkqb->bp", tiles[..., half], hot, precision=lax.Precision.HIGH)
        for half in (slice(0, TILE), slice(TILE, WIDE))
    ]
    return jnp.stack(found, axis=-1).reshape(NBK, H)


def stack_heads(pair):
    half = lax.broadcasted_iota(jnp.int32, (TILE, TILE), 1) // DH
    return jnp.concatenate(
        [jnp.where(half == which, pair, jnp.zeros_like(pair)) for which in range(2)], axis=0
    )


def own_features(wide):
    return jnp.concatenate([wide[:DH, :TILE], wide[DH:, TILE:]], axis=0)


def kept(segment_column, segment_row, key_tile, query_tile, causal):
    keep = segment_column == jnp.concatenate([segment_row, segment_row], axis=1)
    if causal:
        key_place = key_tile * TILE + lax.broadcasted_iota(jnp.int32, (TILE, WIDE), 0)
        query_place = query_tile * TILE + lax.broadcasted_iota(jnp.int32, (TILE, WIDE), 1) % TILE
        keep = keep & (key_place <= query_place)
    return keep


def tile_scores(keys, queries, keep, bias):
    scores = dot_nt(keys, queries)
    if bias is not None:
        scores = scores + bias
    return jnp.where(keep, scores, MASKED)


def forward_kernel(
    causal, biased, first_ref, last_ref, q_ref, k_ref, v_ref, row_ref, column_ref, *rest
):
    bias_ref = rest[0] if biased else None
    out_ref, level_ref, stack_ref, top_ref, sum_ref, total_ref = rest[1:] if biased else rest
    here = pl.program_id(0)
    top_ref[...] = jnp.full_like(top_ref, -1e30)
    sum_ref[...] = jnp.zeros_like(sum_ref)
    total_ref[...] = jnp.zeros_like(total_ref)
    segment_row = row_ref[...]
    for pair in range(PAIRS):
        stack_ref[pair] = stack_heads(q_ref[:, pair * TILE : (pair + 1) * TILE])

    def step(there, carry):
        rows = pl.ds(pl.multiple_of(there * TILE, TILE), TILE)
        keep = kept(column_ref[rows, :], segment_row, there, here, causal)
        offset = jnp.clip(there - here, -2, 2) + 2
        before, sums = top_ref[...], sum_ref[...]
        tops, sums_after = [], []
        for pair in range(PAIRS):
            lanes = slice(pair * TILE, (pair + 1) * TILE)
            scores = tile_scores(
                k_ref[rows, lanes], stack_ref[pair], keep, bias_ref[offset, pair] if biased else None
            )
            old = before[pair : pair + 1, :]
            top = jnp.maximum(old, jnp.max(scores, axis=0, keepdims=True))
            weights = jnp.exp(scores - top)
            scale = jnp.exp(old - top)
            tops.append(top)
            sums_after.append(
                sums[pair : pair + 1, :] * scale + jnp.sum(weights, axis=0, keepdims=True)
            )
            total_ref[pair] = total_ref[pair] * scale + dot(
                v_ref[rows, lanes].T, weights.astype(jnp.bfloat16)
            )
        for pair in range(PAIRS):
            top_ref[pair : pair + 1, :] = tops[pair]
            sum_ref[pair : pair + 1, :] = sums_after[pair]
        return carry

    lax.fori_loop(first_ref[here], last_ref[here], step, 0)
    seen = sum_ref[...] > 0.0
    divisor = jnp.where(seen, sum_ref[...], 1.0)
    level_ref[...] = jnp.where(seen, top_ref[...] + jnp.log(divisor), 0.0)
    for pair in range(PAIRS):
        lanes = slice(pair * TILE, (pair + 1) * TILE)
        wide = total_ref[pair] / divisor[pair : pair + 1, :]
        out_ref[:, lanes] = own_features(wide).T.astype(jnp.bfloat16)


def backward_kernel(
    causal, biased, first_ref, last_ref, q_ref, o_ref, k_ref, v_ref, level_ref, row_ref, column_ref, *rest
):
    bias_ref = rest[0] if biased else None
    rest = rest[1:] if biased else rest
    gq_ref, gkv_ref = rest[:2]
    gb_ref = rest[2] if biased else None
    weight_ref, slope_ref, mean_ref, stack_ref, arrive_ref, tq_ref, tk_ref, tv_ref = rest[-8:]
    here = pl.program_id(0)

    @pl.when(here == 0)
    def _():
        tk_ref[...] = jnp.zeros_like(tk_ref)
        tv_ref[...] = jnp.zeros_like(tv_ref)
        if biased:
            gb_ref[...] = jnp.zeros_like(gb_ref)

    mean_ref[...] = jnp.zeros_like(mean_ref)
    tq_ref[...] = jnp.zeros_like(tq_ref)
    segment_row = row_ref[...]
    first = first_ref[here]
    last = last_ref[here]
    for pair in range(PAIRS):
        lanes = slice(pair * TILE, (pair + 1) * TILE)
        stack_ref[pair] = stack_heads(q_ref[:, lanes])
        arrive_ref[pair] = stack_heads(o_ref[:, lanes])

    def look(there, carry):
        rows = pl.ds(pl.multiple_of(there * TILE, TILE), TILE)
        keep = kept(column_ref[rows, :], segment_row, there, here, causal)
        offset = jnp.clip(there - here, -2, 2) + 2
        means = mean_ref[...]
        sums = []
        for pair in range(PAIRS):
            lanes = slice(pair * TILE, (pair + 1) * TILE)
            scores = tile_scores(
                k_ref[rows, lanes], stack_ref[pair], keep, bias_ref[offset, pair] if biased else None
            )
            weights = jnp.exp(scores - level_ref[pair : pair + 1, :])
            slopes = dot_nt(v_ref[rows, lanes], arrive_ref[pair])
            sums.append(
                means[pair : pair + 1, :] + jnp.sum(weights * slopes, axis=0, keepdims=True)
            )
            weight_ref[there - first, pair] = weights
            slope_ref[there - first, pair] = slopes
            tv_ref[rows, lanes] = tv_ref[rows, lanes] + dot(
                weights.astype(jnp.bfloat16), arrive_ref[pair]
            )
        for pair in range(PAIRS):
            mean_ref[pair : pair + 1, :] = sums[pair]
        return carry

    def push(there, carry):
        rows = pl.ds(pl.multiple_of(there * TILE, TILE), TILE)
        offset = jnp.clip(there - here, -2, 2) + 2
        for pair in range(PAIRS):
            lanes = slice(pair * TILE, (pair + 1) * TILE)
            slopes = (
                weight_ref[there - first, pair]
                * (slope_ref[there - first, pair] - mean_ref[pair : pair + 1, :])
            ).astype(jnp.bfloat16)
            if biased:
                gb_ref[offset, pair] = gb_ref[offset, pair] + slopes.astype(jnp.float32)
            tq_ref[pair] = tq_ref[pair] + dot(k_ref[rows, lanes].T, slopes)
            tk_ref[rows, lanes] = tk_ref[rows, lanes] + dot(slopes, stack_ref[pair])
        return carry

    lax.fori_loop(first, last, look, 0)
    lax.fori_loop(first, last, push, 0)
    for pair in range(PAIRS):
        lanes = slice(pair * TILE, (pair + 1) * TILE)
        gq_ref[:, lanes] = own_features(tq_ref[pair]).T.astype(jnp.bfloat16)

    @pl.when(here == pl.num_programs(0) - 1)
    def _():
        gkv_ref[:, :MODEL_WIDTH] = tk_ref[...].astype(jnp.bfloat16)
        gkv_ref[:, MODEL_WIDTH:] = tv_ref[...].astype(jnp.bfloat16)


def whole_block(shape):
    return pl.BlockSpec(shape, lambda i, *_: (0,) * len(shape))


def column_block(rows, index):
    return pl.BlockSpec((rows, MODEL_WIDTH), lambda i, *_: (0, index))


def packed_forward(queries, pair_rows, span, segment_row, segment_column, causal, bias):
    count, other = queries.shape[0], pair_rows.shape[0]
    biased = bias is not None
    tile = pl.BlockSpec((TILE, MODEL_WIDTH), lambda i, *_: (i, 0))
    return pl.pallas_call(
        lambda *refs: forward_kernel(causal, biased, *refs),
        grid_spec=pltpu.PrefetchScalarGridSpec(
            num_scalar_prefetch=2,
            grid=(count // TILE,),
            in_specs=[
                tile,
                column_block(other, 0),
                column_block(other, 1),
                pl.BlockSpec((1, TILE), lambda i, *_: (0, i)),
                whole_block((other, 1)),
            ]
            + ([whole_block((5, PAIRS, TILE, WIDE))] if biased else []),
            out_specs=[tile, pl.BlockSpec((8, WIDE), lambda i, *_: (0, i))],
            scratch_shapes=[
                pltpu.VMEM((PAIRS, WIDE, TILE), jnp.bfloat16),
                pltpu.VMEM((8, WIDE), jnp.float32),
                pltpu.VMEM((8, WIDE), jnp.float32),
                pltpu.VMEM((PAIRS, TILE, WIDE), jnp.float32),
            ],
        ),
        out_shape=[
            jax.ShapeDtypeStruct((count, MODEL_WIDTH), jnp.bfloat16),
            jax.ShapeDtypeStruct((8, 2 * count), jnp.float32),
        ],
        compiler_params=pltpu.CompilerParams(vmem_limit_bytes=40 << 20),
        cost_estimate=cost(8 * count * other * MODEL_WIDTH, 20 << 20),
        name="attend",
    )(*span, queries, pair_rows, pair_rows, segment_row, segment_column, *([bias] if biased else []))


def packed_backward(
    queries, grad_out, pair_rows, levels, span, segment_row, segment_column, causal, bias
):
    count, other = queries.shape[0], pair_rows.shape[0]
    biased = bias is not None
    reach = min(other // TILE, 9) if biased else other // TILE
    tile = pl.BlockSpec((TILE, MODEL_WIDTH), lambda i, *_: (i, 0))
    table = (5, PAIRS, TILE, WIDE)
    return pl.pallas_call(
        lambda *refs: backward_kernel(causal, biased, *refs),
        grid_spec=pltpu.PrefetchScalarGridSpec(
            num_scalar_prefetch=2,
            grid=(count // TILE,),
            in_specs=[
                tile,
                tile,
                column_block(other, 0),
                column_block(other, 1),
                pl.BlockSpec((8, WIDE), lambda i, *_: (0, i)),
                pl.BlockSpec((1, TILE), lambda i, *_: (0, i)),
                whole_block((other, 1)),
            ]
            + ([whole_block(table)] if biased else []),
            out_specs=[tile, whole_block((other, 2 * MODEL_WIDTH))]
            + ([whole_block(table)] if biased else []),
            scratch_shapes=[
                pltpu.VMEM((reach, PAIRS, TILE, WIDE), jnp.float32),
                pltpu.VMEM((reach, PAIRS, TILE, WIDE), jnp.float32),
                pltpu.VMEM((8, WIDE), jnp.float32),
                pltpu.VMEM((PAIRS, WIDE, TILE), jnp.bfloat16),
                pltpu.VMEM((PAIRS, WIDE, TILE), jnp.bfloat16),
                pltpu.VMEM((PAIRS, TILE, WIDE), jnp.float32),
                pltpu.VMEM((other, MODEL_WIDTH), jnp.float32),
                pltpu.VMEM((other, MODEL_WIDTH), jnp.float32),
            ],
        ),
        out_shape=[
            jax.ShapeDtypeStruct((count, MODEL_WIDTH), jnp.bfloat16),
            jax.ShapeDtypeStruct((other, 2 * MODEL_WIDTH), jnp.bfloat16),
        ]
        + ([jax.ShapeDtypeStruct(table, jnp.float32)] if biased else []),
        compiler_params=pltpu.CompilerParams(vmem_limit_bytes=58 << 20),
        cost_estimate=cost(20 * count * other * MODEL_WIDTH, 40 << 20),
        name="attend_back",
    )(
        *span,
        queries,
        grad_out,
        pair_rows,
        pair_rows,
        levels,
        segment_row,
        segment_column,
        *([bias] if biased else []),
    )


def lookup_kernel(rows_in, blocks_ref, id_ref, vocab_ref, out_ref, total_ref):
    step = pl.program_id(0)
    width = vocab_ref.shape[1]
    chunk = 2 * TILE

    @pl.when(step == 0)
    def _():
        total_ref[...] = jnp.zeros_like(total_ref)

    inside = step * width + lax.broadcasted_iota(jnp.int32, (1, width), 1) < rows_in
    table = jnp.where(inside, vocab_ref[...], jnp.zeros_like(vocab_ref[...]))
    places = step * width + lax.broadcasted_iota(jnp.int32, (chunk, width), 1)

    def one(index, carry):
        rows = pl.ds(pl.multiple_of(index * chunk, chunk), chunk)
        hot = (id_ref[rows, :] == places).astype(jnp.bfloat16)
        total_ref[rows, :] = total_ref[rows, :] + dot_nt(hot, table)
        return carry

    lax.fori_loop(0, blocks_ref[0], one, 0)
    lax.fori_loop(blocks_ref[1], blocks_ref[2], one, 0)

    @pl.when(step == pl.num_programs(0) - 1)
    def _():
        out_ref[...] = total_ref[...].astype(jnp.bfloat16)


def lookup_rows(local_ids, spans, vocab):
    count, width = local_ids.shape[0], 8 * TILE
    rows_in = vocab.shape[1]
    return pl.pallas_call(
        lambda *refs: lookup_kernel(rows_in, *refs),
        grid_spec=pltpu.PrefetchScalarGridSpec(
            num_scalar_prefetch=1,
            grid=(pl.cdiv(rows_in, width),),
            in_specs=[
                whole_block((count, 1)),
                pl.BlockSpec((MODEL_WIDTH, width), lambda i, *_: (0, i)),
            ],
            out_specs=whole_block((count, MODEL_WIDTH)),
            scratch_shapes=[pltpu.VMEM((count, MODEL_WIDTH), jnp.float32)],
        ),
        out_shape=jax.ShapeDtypeStruct((count, MODEL_WIDTH), jnp.bfloat16),
        compiler_params=pltpu.CompilerParams(vmem_limit_bytes=40 << 20),
        cost_estimate=cost(2 * count * rows_in * MODEL_WIDTH, 90 << 20),
        name="lookup",
    )(spans, local_ids[:, None], vocab)


def vocab_grad_kernel(blocks_ref, id_ref, grad_ref, logit_ref, final_ref, start_ref, left_ref, out_ref):
    step = pl.program_id(0)
    width = left_ref.shape[0]
    chunk = 2 * TILE
    before = jnp.where(blocks_ref[3] == 0, start_ref[...], left_ref[...])
    out_ref[...] = before + dot_tn(logit_ref[...], final_ref[...])
    places = step * width + lax.broadcasted_iota(jnp.int32, (width, chunk), 0)

    def one(index, carry):
        rows = pl.ds(pl.multiple_of(index * chunk, chunk), chunk)
        hot = (places == id_ref[:, rows]).astype(jnp.bfloat16)
        out_ref[...] = out_ref[...] + dot(hot, grad_ref[rows, :])
        return carry

    lax.fori_loop(0, blocks_ref[0], one, 0)
    lax.fori_loop(blocks_ref[1], blocks_ref[2], one, 0)


def vocab_grad(start, left, turn, local_ids, spans, lookups, grad_logits, final_rows):
    count, width = local_ids.shape[0], 8 * TILE
    rows_in = left.shape[0]
    block = pl.BlockSpec((width, MODEL_WIDTH), lambda i, *_: (i, 0))
    return pl.pallas_call(
        vocab_grad_kernel,
        grid_spec=pltpu.PrefetchScalarGridSpec(
            num_scalar_prefetch=1,
            grid=(pl.cdiv(rows_in, width),),
            in_specs=[
                whole_block((1, count)),
                whole_block((count, MODEL_WIDTH)),
                pl.BlockSpec((grad_logits.shape[0], width), lambda i, *_: (0, i)),
                whole_block(final_rows.shape),
                pl.BlockSpec((width, MODEL_WIDTH), lambda i, s: (jnp.where(s[3] == 0, i, 0), 0)),
                pl.BlockSpec((width, MODEL_WIDTH), lambda i, s: (jnp.where(s[3] == 0, 0, i), 0)),
            ],
            out_specs=block,
        ),
        out_shape=jax.ShapeDtypeStruct(left.shape, jnp.float32),
        input_output_aliases={6: 0},
        compiler_params=pltpu.CompilerParams(vmem_limit_bytes=40 << 20),
        cost_estimate=cost(2 * (count + 384) * rows_in * MODEL_WIDTH, 100 << 20),
        name="vocab_grad",
    )(
        jnp.concatenate([spans, turn[None]]),
        local_ids[None, :],
        lookups,
        grad_logits,
        final_rows,
        start,
        left,
    )


def logit_places(step, rows_in, width):
    return step * width + lax.broadcasted_iota(jnp.int32, (TILE, width), 1)


def logit_kernel(rows_in, tiles_ref, row_ref, vocab_ref, id_ref, logit_ref, stat_ref, top_ref, sum_ref, hit_ref):
    step = pl.program_id(0)
    width = vocab_ref.shape[1]

    @pl.when(step == 0)
    def _():
        top_ref[...] = jnp.full_like(top_ref, -1e30)
        sum_ref[...] = jnp.zeros_like(sum_ref)
        hit_ref[...] = jnp.zeros_like(hit_ref)

    places = logit_places(step, rows_in, width)

    def one(index, carry):
        rows = pl.ds(pl.multiple_of(index * TILE, TILE), TILE)
        logits = dot(row_ref[rows, :], vocab_ref[...])
        logit_ref[rows, :] = logits
        inside = places < rows_in
        hits = jnp.where(inside & (places == id_ref[rows, :]), logits, 0.0)
        logits = jnp.where(inside, logits, -1e30)
        parts = [slice(begin, begin + TILE) for begin in range(0, width, TILE)]
        before = top_ref[rows, :]
        top = before
        for part in parts:
            top = jnp.maximum(top, logits[:, part])
        total = sum_ref[rows, :] * jnp.exp(before - top)
        hit = hit_ref[rows, :]
        for part in parts:
            total = total + jnp.exp(logits[:, part] - top)
            hit = hit + hits[:, part]
        top_ref[rows, :] = top
        sum_ref[rows, :] = total
        hit_ref[rows, :] = hit
        return carry

    lax.fori_loop(0, tiles_ref[0], one, 0)

    @pl.when(step == pl.num_programs(0) - 1)
    def _():
        top = jnp.max(top_ref[...], axis=1, keepdims=True)
        total = jnp.sum(sum_ref[...] * jnp.exp(top_ref[...] - top), axis=1, keepdims=True)
        hit = jnp.sum(hit_ref[...], axis=1, keepdims=True)
        lane = lax.broadcasted_iota(jnp.int32, stat_ref.shape, 1)
        seen = jnp.where(total > 0.0, total, 1.0)
        stat_ref[...] = jnp.where(lane == 0, top, jnp.where(lane == 1, seen, hit))


def logit_stats(final_rows, vocab, ids, tiles):
    count, rows_in, width = final_rows.shape[0], vocab.shape[1], 4 * TILE
    return pl.pallas_call(
        lambda *refs: logit_kernel(rows_in, *refs),
        grid_spec=pltpu.PrefetchScalarGridSpec(
            num_scalar_prefetch=1,
            grid=(pl.cdiv(rows_in, width),),
            in_specs=[
                whole_block((count, MODEL_WIDTH)),
                pl.BlockSpec((MODEL_WIDTH, width), lambda i, *_: (0, i)),
                whole_block((count, 1)),
            ],
            out_specs=[
                pl.BlockSpec((count, width), lambda i, *_: (0, i)),
                whole_block((count, TILE)),
            ],
            scratch_shapes=[pltpu.VMEM((count, TILE), jnp.float32)] * 3,
        ),
        out_shape=[
            jax.ShapeDtypeStruct((count, rows_in), jnp.float32),
            jax.ShapeDtypeStruct((count, TILE), jnp.float32),
        ],
        compiler_params=pltpu.CompilerParams(vmem_limit_bytes=40 << 20),
        cost_estimate=cost(2 * count * rows_in * MODEL_WIDTH, 40 << 20, count * rows_in),
        name="logits",
    )(tiles, final_rows, vocab, ids)


def logit_grad_kernel(
    rows_in, tiles_ref, logit_ref, vocab_ref, id_ref, level_ref, weight_ref, grad_ref, row_ref
):
    step = pl.program_id(0)
    width = vocab_ref.shape[1]

    @pl.when(step == 0)
    def _():
        row_ref[...] = jnp.zeros_like(row_ref)

    grad_ref[...] = jnp.zeros_like(grad_ref)
    places = logit_places(step, rows_in, width)
    inside = step * width + lax.broadcasted_iota(jnp.int32, (1, width), 1) < rows_in
    table = jnp.where(inside, vocab_ref[...], jnp.zeros_like(vocab_ref[...]))

    def one(index, carry):
        rows = pl.ds(pl.multiple_of(index * TILE, TILE), TILE)
        hit = (places == id_ref[rows, :]).astype(jnp.float32)
        grads = (jnp.exp(logit_ref[rows, :] - level_ref[rows, :]) - hit) * weight_ref[rows, :]
        grads = jnp.where(places < rows_in, grads, 0.0).astype(jnp.bfloat16)
        grad_ref[rows, :] = grads
        row_ref[rows, :] = row_ref[rows, :] + dot_nt(grads, table)
        return carry

    lax.fori_loop(0, tiles_ref[0], one, 0)


def logit_grads(logits, vocab, ids, tiles, levels, weights):
    count, rows_in = logits.shape
    width = 8 * TILE
    block = pl.BlockSpec((count, width), lambda i, *_: (0, i))
    return pl.pallas_call(
        lambda *refs: logit_grad_kernel(rows_in, *refs),
        grid_spec=pltpu.PrefetchScalarGridSpec(
            num_scalar_prefetch=1,
            grid=(pl.cdiv(rows_in, width),),
            in_specs=[
                block,
                pl.BlockSpec((MODEL_WIDTH, width), lambda i, *_: (0, i)),
                whole_block((count, 1)),
                whole_block((count, 1)),
                whole_block((count, 1)),
            ],
            out_specs=[block, whole_block((count, MODEL_WIDTH))],
        ),
        out_shape=[
            jax.ShapeDtypeStruct((count, rows_in), jnp.bfloat16),
            jax.ShapeDtypeStruct((count, MODEL_WIDTH), jnp.float32),
        ],
        compiler_params=pltpu.CompilerParams(vmem_limit_bytes=40 << 20),
        cost_estimate=cost(2 * count * rows_in * MODEL_WIDTH, 40 << 20, count * rows_in),
        name="logit_grads",
    )(tiles, logits, vocab, ids, levels[:, None], weights[:, None])


def packing(lengths, room):
    ends = jnp.cumsum(lengths)
    starts = ends - lengths
    places = jnp.arange(room, dtype=jnp.int32)
    segment = jnp.sum((places[:, None] >= ends[None, :]).astype(jnp.int32), axis=1)
    inside = segment[:, None] == jnp.arange(lengths.shape[0], dtype=jnp.int32)[None, :]
    position = places - jnp.sum(jnp.where(inside, starts[None, :], 0), axis=1)
    return segment, position, jnp.minimum(starts, room), jnp.minimum(ends, room)


def key_span(query_segment, query_total, key_starts, key_ends):
    number = key_starts.shape[0]
    count = query_segment.shape[0] // TILE
    begins = jnp.arange(count, dtype=jnp.int32) * TILE
    last_real = jnp.clip(query_total - 1, 0, query_segment.shape[0] - 1)
    finals = jnp.minimum(begins + TILE - 1, last_real)

    def pick(table, places):
        chosen = jnp.sum(
            jnp.where(
                jnp.arange(query_segment.shape[0], dtype=jnp.int32)[None, :] == places[:, None],
                query_segment[None, :],
                0,
            ),
            axis=1,
        )
        return jnp.sum(
            jnp.where(
                chosen[:, None] == jnp.arange(number, dtype=jnp.int32)[None, :], table[None, :], 0
            ),
            axis=1,
        )

    some = begins < query_total
    first = jnp.where(some, pick(key_starts, begins) // TILE, 0)
    last = jnp.where(some, (pick(key_ends, finals) + TILE - 1) // TILE, 0)
    return first, jnp.maximum(first, last)


def packed_gradients(
    source_stream, target_stream, gain_rows, biases, weights, later, layout, head, column_start, column_width
):
    enc_attention, enc_feed = weights[:3], weights[3:]
    (
        source_span,
        target_span,
        cross_span,
        source_row,
        source_column,
        target_row,
        target_column,
    ) = layout
    bias_source, bias_target = biases

    def shard(grad, which=0):
        return lax.dynamic_slice_in_dim(grad, which * MODEL_WIDTH + column_start, column_width, 1)

    def attention(stream, gain_row, context, matrices, span, row, column, causal, bias):
        to_query, to_pair, outward = matrices
        normed = root_norm(stream, gain_row).astype(jnp.bfloat16)
        context = normed if context is None else context
        queries = dot(normed, to_query).astype(jnp.bfloat16)
        pair_rows = dot(context, to_pair).astype(jnp.bfloat16)
        attended, levels = packed_forward(queries, pair_rows, span, row, column, causal, bias)
        return stream + dot(attended, outward), (
            normed,
            context,
            queries,
            pair_rows,
            attended,
            levels,
        )

    def attention_back(grad, stream, gain_row, crossed, matrices, saved, span, row, column, causal, bias):
        to_query, to_pair, outward = matrices
        normed, context, queries, pair_rows, attended, levels = saved
        branch = grad.astype(jnp.bfloat16)
        arriving = dot_nt(branch, outward).astype(jnp.bfloat16)
        grads = packed_backward(
            queries, arriving, pair_rows, levels, span, row, column, causal, bias
        )
        grad_queries, grad_pair = grads[:2]
        pair_shards = [shard(grad_pair), shard(grad_pair, 1)]
        if crossed:
            shares = [
                dot_tn(shard(grad_queries), normed),
                dot_tn(jnp.concatenate(pair_shards, axis=1), context),
                dot_tn(shard(branch), attended),
            ]
        else:
            shares = [
                dot_tn(jnp.concatenate([shard(grad_queries)] + pair_shards, axis=1), normed),
                dot_tn(shard(branch), attended),
            ]
        grad_normed = dot_nt(grad_queries, to_query)
        grad_context = dot_nt(grad_pair, to_pair)
        if not crossed:
            grad_normed = grad_normed + grad_context
        grad_input, grad_gain = norm_backward(stream, gain_row, grad_normed)
        return grad + grad_input, grad_gain, shares, grads[2:], grad_context

    def feed(stream, gain_row, matrices):
        inward, outward = matrices
        normed = root_norm(stream, gain_row).astype(jnp.bfloat16)
        inner = dot(normed, inward)
        hidden = jax.nn.gelu(inner).astype(jnp.bfloat16)
        return stream + dot(hidden, outward), (normed, inner, hidden)

    def feed_back(grad, stream, gain_row, matrices, saved):
        inward, outward = matrices
        normed, inner, hidden = saved
        branch = grad.astype(jnp.bfloat16)
        grad_inner = jax.vjp(jax.nn.gelu, inner)[1](dot_nt(branch, outward))[0].astype(jnp.bfloat16)
        grad_normed = dot_nt(grad_inner, inward)
        inner_shards = jnp.concatenate([shard(grad_inner, j) for j in range(4)], axis=1)
        outward_shares = dot_tn(shard(branch), hidden)
        shares = [dot_tn(inner_shards, normed)] + [
            outward_shares[:, j * MODEL_WIDTH : (j + 1) * MODEL_WIDTH] for j in range(4)
        ]
        grad_input, grad_gain = norm_backward(stream, gain_row, grad_normed)
        return grad + grad_input, grad_gain, shares

    x1, enc_saved = attention(
        source_stream, gain_rows[0], None, enc_attention, source_span, source_row, source_column, False, bias_source
    )
    x1, dec_self, dec_cross, dec_feed = later(x1)
    x2, enc_feed_saved = feed(x1, gain_rows[1], enc_feed)
    encoded = root_norm(x2, gain_rows[2]).astype(jnp.bfloat16)
    encoded, target_stream = lax.optimization_barrier((encoded, target_stream))
    target_stream = target_stream.astype(jnp.float32)
    y1, self_saved = attention(
        target_stream, gain_rows[3], None, dec_self, target_span, target_row, target_column, True, bias_target
    )
    y2, cross_saved = attention(
        y1, gain_rows[4], encoded, dec_cross, cross_span, target_row, source_column, False, None
    )
    y3, dec_feed_saved = feed(y2, gain_rows[5], dec_feed)
    final_rows = (root_norm(y3, gain_rows[6]) * MODEL_WIDTH ** (-0.5)).astype(jnp.bfloat16)

    grad_final, grad_logits, token_loss = head(final_rows)

    grad, gain_final = norm_backward(y3, gain_rows[6], grad_final * MODEL_WIDTH ** (-0.5))
    grad, gain_feed, feed_shares = feed_back(grad, y2, gain_rows[5], dec_feed, dec_feed_saved)
    grad, gain_cross, cross_shares, _, grad_encoded = attention_back(
        grad, y1, gain_rows[4], True, dec_cross, cross_saved, cross_span, target_row, source_column, False, None
    )
    target_grad, gain_self, self_shares, table_target, _ = attention_back(
        grad, target_stream, gain_rows[3], False, dec_self, self_saved, target_span, target_row, target_column, True, bias_target
    )
    grad, gain_encoded = norm_backward(x2, gain_rows[2], grad_encoded)
    grad, gain_enc_feed, enc_feed_shares = feed_back(grad, x1, gain_rows[1], enc_feed, enc_feed_saved)
    source_grad, gain_enc, enc_shares, table_source, _ = attention_back(
        grad, source_stream, gain_rows[0], False, enc_attention, enc_saved, source_span, source_row, source_column, False, bias_source
    )
    gains = jnp.stack(
        [gain_enc, gain_enc_feed, gain_encoded, gain_self, gain_cross, gain_feed, gain_final]
    )
    tables = jnp.stack(
        [
            bias_grad(table_source[0], False),
            bias_grad(table_target[0], True),
        ]
    )
    shares = jnp.concatenate(
        enc_shares + enc_feed_shares + self_shares + cross_shares + feed_shares
    ).reshape(-1, column_width, MODEL_WIDTH)
    return shares, gains, tables, source_grad, target_grad, final_rows, grad_logits, token_loss


def orthonormal_kernel(factor_ref, out_ref):
    rank = factor_ref.shape[0]
    for r in range(rank):
        out_ref[r] = factor_ref[r]
    for r in range(rank):
        row = out_ref[r]
        row = row * lax.rsqrt(jnp.sum(row * row, axis=-1, keepdims=True))
        out_ref[r] = row
        for s in range(r + 1, rank):
            other = out_ref[s]
            out_ref[s] = other - row * jnp.sum(row * other, axis=-1, keepdims=True)


def orthonormal_rows(factor):
    return pl.pallas_call(
        orthonormal_kernel,
        out_shape=jax.ShapeDtypeStruct(factor.shape, jnp.float32),
        name="orthonormal",
    )(factor)


def local(
    source_ids,
    targets,
    source_lengths,
    target_lengths,
    task_ids,
    task_counts,
    blocks,
    blocks_momentum,
    embedding,
    embed_momentum,
    gain_rows,
    gain_momentum,
    position_bias,
    bias_momentum,
    right_blocks,
    right_embed,
    error_blocks,
    error_embed,
):
    fsdp_rank = lax.axis_index("fsdp")
    cuts_rank = lax.axis_index("cuts")
    cuts_count = lax.axis_size("cuts")
    seq_count, source_len = source_ids.shape
    target_len = targets.shape[1]
    number = seq_count * lax.axis_size("fsdp")
    room_source = min(ROOM_SOURCE, source_len * number)
    room_target = min(ROOM_TARGET, target_len * number)
    fewest = min(room_source // source_len, room_target // target_len)
    shares_of = sorted({number, -(-number // 2), fewest}, reverse=True)
    vocab_rows = embedding.shape[0]
    vocab_start = fsdp_rank * vocab_rows
    once = (fsdp_rank == 0).astype(jnp.float32)

    stored_vocab = embedding.T.astype(jnp.bfloat16)
    steps = len(spread_ways())
    bands = max(n for n in range(1, max(steps, 1) + 1) if stored_vocab.shape[0] % (16 * n) == 0 or n == 1)
    vocab_shares = spread_begin(stored_vocab.reshape(bands, -1, vocab_rows))
    stored = jnp.transpose(blocks, (1, 0, 2)).astype(jnp.bfloat16)
    group = lax.all_gather(
        jnp.concatenate(
            [source_ids, targets, source_lengths[:, None], target_lengths[:, None]], axis=1
        ),
        "fsdp",
        axis=0,
        tiled=True,
    )
    group_source = group[:, :source_len]
    group_target = group[:, source_len : source_len + target_len]
    lengths = group[:, -2:]

    def fullest(share):
        padded = jnp.pad(lengths, ((0, -number % share), (0, 0)))
        return jnp.max(jnp.sum(padded.reshape(-1, share, 2), axis=1), axis=0)

    needs = lax.all_gather(
        jnp.concatenate([jnp.sum(lengths, axis=0)] + [fullest(share) for share in shares_of]),
        "cuts",
        axis=0,
    )
    for step in range(steps):
        if step:
            vocab_shares, needs = spread_tied(vocab_shares, needs)
        vocab_shares = spread_step(vocab_shares, step)
    stored, needs = lax.optimization_barrier((stored, needs))
    first_columns = jnp.concatenate(gather_fsdp(stored[:12], fsdp_rank), axis=2)
    errors = jnp.transpose(error_blocks[0], (1, 2, 0))
    biases = (bias_tiles(False, position_bias[0]), bias_tiles(True, position_bias[1]))
    vocab_shares, first_columns, biases = spread_tied(vocab_shares, first_columns, biases)
    first_shares = spread_begin(first_columns)
    first_shares = spread_step(first_shares, 0) if steps else first_shares
    vocab_pieces = spread_end(vocab_shares)
    piece_arrays = [[array for _, array in held] for _, held in vocab_pieces]
    first_arrays = [array for _, array in first_shares]
    given = (group, needs, piece_arrays, first_arrays, stored[12:], errors, biases)

    def one_round(state):
        _, turn, _, _, left_blocks, left_embed, gains_sum, table_sum, loss_sum = state
        turn, group, needs, piece_arrays, first_arrays, stored_rest, errors, biases = (
            lax.optimization_barrier((turn, *given))
        )
        group_source = group[:, :source_len]
        group_target = group[:, source_len : source_len + target_len]
        lengths = group[:, -2:]
        total_count = jnp.sum(needs[:, 1]).astype(jnp.float32)
        most = jnp.max(needs[:, 2:], axis=0)
        share = jnp.int32(shares_of[-1])
        for index in range(len(shares_of) - 2, -1, -1):
            fits = (most[2 * index] <= room_source) & (most[2 * index + 1] <= room_target)
            share = jnp.where(fits, shares_of[index], share)
        members = jnp.arange(number, dtype=jnp.int32)
        taken = (members >= turn * share) & (members < (turn + 1) * share)
        source_taken = jnp.where(taken, lengths[:, 0], 0)
        target_taken = jnp.where(taken, lengths[:, 1], 0)
        more = (turn + 1) * share < number

        chosen = jnp.sum(
            jnp.where(
                task_ids[:, None] == jnp.arange(TASKS, dtype=jnp.int32)[None, :],
                task_counts[None, :],
                0,
            ),
            axis=1,
        ).astype(jnp.float32)
        slice_weight = jnp.sum(
            jnp.where(
                jnp.arange(cuts_count, dtype=jnp.int32) == cuts_rank,
                cuts_count * chosen / jnp.sum(chosen),
                0.0,
            )
        )

        pieces = [
            (first, [(bits, array) for (bits, _), array in zip(held, own)])
            for (first, held), own in zip(vocab_pieces, piece_arrays)
        ]
        (vocab,) = place_pieces(pieces, ((tuple(range(bands)), "mixed"),), cuts_rank)
        shares = [(bits, array) for (bits, _), array in zip(first_shares, first_arrays)]
        rest_parts = [stored_rest] + [
            shifted(stored_rest, distance) for distance in range(1, lax.axis_size("fsdp"))
        ]
        for step in range(1, steps):
            shares = spread_step(shares, step)

        def attention_groups(first):
            return (
                ((first,), "columns"),
                ((first + 1, first + 2), "columns"),
                ((first + 3,), "columns"),
            )

        def feed_groups(first):
            return (
                (tuple(range(first, first + 4)), "columns"),
                (tuple(range(first + 4, first + 8)), "rows"),
            )

        source_segment, source_place, source_starts, source_ends = packing(source_taken, room_source)
        target_segment, target_place, target_starts, target_ends = packing(target_taken, room_target)
        source_real = source_segment < number
        target_real = target_segment < number
        packed_source = jnp.take(
            group_source.reshape(-1),
            jnp.where(source_real, source_segment * source_len + source_place, 0),
        )
        group_input = jnp.concatenate(
            [jnp.zeros_like(group_target[:, :1]), group_target[:, :-1]], axis=1
        )
        target_from = jnp.where(target_real, target_segment * target_len + target_place, 0)
        packed_target = jnp.take(group_target.reshape(-1), target_from)
        packed_input = jnp.take(group_input.reshape(-1), target_from)
        packed_ids = jnp.concatenate([packed_source, packed_input])
        packed_real = jnp.concatenate([source_real, target_real])
        local_ids = jnp.where(packed_real, packed_ids - vocab_start, -1)
        source_total, target_total = jnp.sum(source_taken), jnp.sum(target_taken)
        chunk = 2 * TILE
        local_ids = jnp.pad(local_ids, (0, -local_ids.shape[0] % chunk), constant_values=-1)
        spans = jnp.stack(
            [
                jnp.minimum((source_total + chunk - 1) // chunk, room_source // chunk),
                jnp.int32(room_source // chunk),
                jnp.minimum(
                    (room_source + target_total + chunk - 1) // chunk,
                    local_ids.shape[0] // chunk,
                ),
            ]
        )
        rows = lookup_rows(local_ids, spans, vocab)
        shares, rows, rest_parts = spread_tied(shares, rows, rest_parts)
        rest_columns = jnp.concatenate(in_order(rest_parts, fsdp_rank), axis=2)
        rest_shares, rows = spread_tied(spread_begin(rest_columns), rows)
        if steps:
            rest_shares = spread_step(rest_shares, 0)
        first_placed = place_pieces(
            spread_end(shares), attention_groups(0) + feed_groups(4), cuts_rank
        )
        sizes = [room_source * part // 10 for part in (4, 5, 6, 7, 8, 10)]
        fullest_source = jnp.int32(room_source)
        for index in range(len(shares_of) - 1, -1, -1):
            fullest_source = jnp.where(share == shares_of[index], most[2 * index], fullest_source)
        source_rows = lax.switch(
            sum((fullest_source > size).astype(jnp.int32) for size in sizes[:-1]),
            [
                lambda table, size=size: jnp.pad(
                    lax.psum(table[:size], "fsdp"), ((0, room_source - size), (0, 0))
                )
                for size in sizes
            ],
            rows[:room_source],
        )
        rest_shares, source_rows, target_rows = spread_tied(
            rest_shares, source_rows, rows[room_source : room_source + room_target]
        )
        for step in range(1, steps - 1):
            rest_shares = spread_step(rest_shares, step)
        rest_arriving = spread_send(rest_shares, steps - 1) if steps > 1 else []

        def decoder_weights(stream):
            shares, arriving, stream = spread_tied(rest_shares, rest_arriving, stream)
            if steps > 1:
                shares = spread_receive(shares, arriving, steps - 1)
            pieces = spread_end(shares)
            attentions = place_pieces(pieces, attention_groups(0) + attention_groups(4), cuts_rank)
            feeds = place_pieces(pieces, feed_groups(8), cuts_rank)
            return stream, attentions[:3], attentions[3:], feeds

        target_rows = lax.psum(target_rows, "fsdp")
        source_stream = source_rows.astype(jnp.float32)
        target_stream = target_rows
        layout = (
            key_span(source_segment, source_total, source_starts, source_ends),
            key_span(target_segment, target_total, target_starts, target_ends),
            key_span(target_segment, target_total, source_starts, source_ends),
            source_segment[None, :],
            source_segment[:, None],
            target_segment[None, :],
            target_segment[:, None],
        )

        token_mask = target_real.astype(jnp.float32)
        token_weight = token_mask * (slice_weight / total_count)
        target_ids = (packed_target - vocab_start)[:, None]
        target_tiles = ((target_total + TILE - 1) // TILE)[None]

        def head(final_rows):
            logits, own_stats = logit_stats(final_rows, vocab, target_ids, target_tiles)
            stats = lax.all_gather(own_stats[:, :3].T, "fsdp", axis=0)
            top = jnp.max(stats[:, 0], axis=0)
            log_total = top + jnp.log(
                jnp.sum(stats[:, 1] * jnp.exp(stats[:, 0] - top[None, :]), axis=0)
            )
            token_loss = (log_total - jnp.sum(stats[:, 2], axis=0)) * token_mask
            grad_logits, grad_rows = logit_grads(
                logits, vocab, target_ids, target_tiles, log_total, token_weight
            )
            grad_rows = sum_fsdp(grad_rows, fsdp_rank)
            return grad_rows, grad_logits, token_loss

        shares, gains, table_found, source_grad, target_grad, final_rows, grad_logits, token_loss = (
            packed_gradients(
                source_stream,
                target_stream,
                gain_rows,
                biases,
                first_placed,
                decoder_weights,
                layout,
                head,
                fsdp_rank * blocks.shape[2],
                blocks.shape[2],
            )
        )
        lookups = jnp.concatenate([source_grad, target_grad]).astype(jnp.bfloat16)
        lookups = jnp.pad(lookups, ((0, local_ids.shape[0] - lookups.shape[0]), (0, 0)))
        left_embed = vocab_grad(
            error_embed[0], left_embed, turn, local_ids, spans, lookups, grad_logits, final_rows
        )
        before = jnp.where(turn == 0, errors, left_blocks)
        return (
            more,
            turn + 1,
            total_count,
            slice_weight,
            before + shares,
            left_embed,
            gains_sum + gains,
            table_sum + table_found,
            loss_sum + jnp.sum(token_loss),
        )

    zero = jnp.zeros((), jnp.float32)
    _, _, total_count, slice_weight, left_blocks, left_embed, gains_grad, table_grad, loss_local = (
        lax.while_loop(
            lambda state: state[0],
            one_round,
            (
                jnp.ones((), jnp.bool_),
                jnp.zeros((), jnp.int32),
                zero,
                zero,
                unset((blocks.shape[1], blocks.shape[2], MODEL_WIDTH)),
                unset((vocab_rows, MODEL_WIDTH)),
                jnp.zeros_like(gain_rows),
                jnp.zeros_like(position_bias),
                zero,
            ),
        )
    )

    left_factor = jnp.einsum("kji,kjr->rki", left_blocks, right_blocks, precision=lax.Precision.HIGH)
    embed_factor = jnp.einsum("vd,vr->rd", left_embed, right_embed, precision=lax.Precision.HIGH)
    rank, count = left_factor.shape[:2]
    small = jnp.concatenate(
        [
            gains_grad * once,
            (table_grad * once).reshape(-1, MODEL_WIDTH),
            jnp.full((1, MODEL_WIDTH), loss_local * slice_weight * once),
        ]
    )
    factor = jnp.concatenate([left_factor, embed_factor[:, None]], axis=1)
    packed = jnp.concatenate([factor.reshape(-1, MODEL_WIDTH), small])
    packed = jnp.pad(packed, ((0, -packed.shape[0] % (8 * cuts_count)), (0, 0)))
    packed = sum_everywhere(packed, cuts_rank)
    factor = packed[: rank * (count + 1)].reshape(factor.shape)
    small = packed[rank * (count + 1) :]
    gains_grad = small[: gain_rows.shape[0]]
    table_rows = position_bias.size // MODEL_WIDTH
    table_grad = small[gain_rows.shape[0] :][:table_rows].reshape(position_bias.shape)
    loss_total = small[gain_rows.shape[0] + table_rows, 0]
    factor = orthonormal_rows(factor)
    left_factor, embed_factor = factor[:, :-1], factor[:, -1]
    factors_blocks = jnp.einsum("kji,rki->rkj", left_blocks, left_factor, precision=lax.Precision.DEFAULT)
    factors_embed = jnp.einsum("vd,rd->rv", left_embed, embed_factor, precision=lax.Precision.DEFAULT)
    both = sum_cuts(jnp.concatenate([factors_blocks.reshape(rank, -1), factors_embed], axis=1))
    factors_embed = both[:, -vocab_rows:]
    factors_blocks = both[:, :-vocab_rows].reshape(factors_blocks.shape)
    gram_blocks = jnp.einsum("rki,ski->krs", left_factor, left_factor, precision=TOP_PRECISION)
    gram_embed = jnp.einsum("rd,sd->rs", embed_factor, embed_factor, precision=TOP_PRECISION)
    squares = jnp.sum(
        factors_blocks
        * jnp.einsum("krs,skj->rkj", gram_blocks, factors_blocks, precision=lax.Precision.HIGH)
    ) + jnp.sum(factors_embed * jnp.dot(gram_embed, factors_embed, precision=lax.Precision.HIGH))
    squares = lax.psum(squares, "fsdp")
    full_blocks = jnp.einsum("rki,rkj->kji", left_factor, factors_blocks, precision=lax.Precision.DEFAULT)
    full_embed = jnp.einsum("rv,rd->vd", factors_embed, embed_factor, precision=lax.Precision.DEFAULT)
    owned_rows = blocks.shape[0]
    owned_columns = embedding.shape[1]
    own_left = lax.dynamic_slice_in_dim(left_factor, cuts_rank * owned_rows, owned_rows, 2)
    own_right = lax.dynamic_slice_in_dim(embed_factor, cuts_rank * owned_columns, owned_columns, 1)
    own_blocks = jnp.einsum("rki,rkj->ikj", own_left, factors_blocks, precision=lax.Precision.DEFAULT)
    own_embed = jnp.einsum("rv,rd->vd", factors_embed, own_right, precision=lax.Precision.DEFAULT)
    small_squares = jnp.sum(gains_grad * gains_grad) + jnp.sum(table_grad * table_grad)
    grad_norm = jnp.sqrt(squares + small_squares)
    clip_factor = jnp.minimum(1.0, CLIP_NORM / grad_norm)
    step_size = STEP_RATE * math.sqrt(PARAMS / MODEL_WIDTH) / CLIP_NORM
    embed_step = step_size * EMBED_SHARE * math.sqrt(MODEL_WIDTH)
    small_step = step_size * SMALL_SHARE * math.sqrt(MODEL_WIDTH)
    momentum_blocks = MOMENTUM_DECAY * blocks_momentum + (1.0 - MOMENTUM_DECAY) * (
        clip_factor * own_blocks
    )
    momentum_embed = MOMENTUM_DECAY * embed_momentum + (1.0 - MOMENTUM_DECAY) * (
        clip_factor * own_embed
    )
    momentum_gains = MOMENTUM_DECAY * gain_momentum + (1.0 - MOMENTUM_DECAY) * (
        clip_factor * gains_grad
    )
    momentum_bias = MOMENTUM_DECAY * bias_momentum + (1.0 - MOMENTUM_DECAY) * (
        clip_factor * table_grad
    )
    return (
        loss_total,
        total_count,
        grad_norm,
        blocks - step_size * momentum_blocks,
        momentum_blocks,
        embedding - embed_step * momentum_embed,
        momentum_embed,
        gain_rows - small_step * momentum_gains,
        momentum_gains,
        position_bias - small_step * momentum_bias,
        momentum_bias,
        jnp.transpose(factors_blocks, (1, 2, 0)),
        factors_embed.T,
        jnp.transpose(left_blocks - full_blocks, (2, 0, 1))[None],
        (left_embed - full_embed)[None],
    )


def solution(mesh):
    return jax.shard_map(
        local,
        mesh=mesh,
        in_specs=(
            P(("cuts", "fsdp"), None),
            P(("cuts", "fsdp"), None),
            P(("cuts", "fsdp")),
            P(("cuts", "fsdp")),
            P(),
            P(),
            P("cuts", None, "fsdp"),
            P("cuts", None, "fsdp"),
            P("fsdp", "cuts"),
            P("fsdp", "cuts"),
            P(),
            P(),
            P(),
            P(),
            P(None, "fsdp", None),
            P("fsdp", None),
            P("cuts", None, None, "fsdp"),
            P("cuts", "fsdp", None),
        ),
        out_specs=(
            P(),
            P(),
            P(),
            P("cuts", None, "fsdp"),
            P("cuts", None, "fsdp"),
            P("fsdp", "cuts"),
            P("fsdp", "cuts"),
            P(),
            P(),
            P(),
            P(),
            P(None, "fsdp", None),
            P("fsdp", None),
            P("cuts", None, None, "fsdp"),
            P("cuts", "fsdp", None),
        ),
        check_vma=False,
    )
```
